128 devices in a mesh: experts: 16 (over x, z), context: 4 (over y), dp: 2 (over core).
Axes of the slice: x: 4, y: 4, z: 4, core: 2. Of those that a mesh axis runs over, the one named last changes fastest.
Arguments:
- tokens: bfloat16 [2, 32, 256, 2048], P(None, ('experts', 'dp'), 'context'), may hold values from -6 to 6
- lengths: int32 [2, 32], P(None, ('experts', 'dp')), may hold values from 64 to 256, as said below
- routes: int32 [2, 32, 256, 8], P(None, ('experts', 'dp'), 'context'), may hold values from 0 to 15, all different within a row; in each aligned block of 64 rows (0 to 63, 64 to 127, ..., all dimensions but the last counted through in order) at most 33 rows name the same one
- mix_weights: float32 [2, 32, 256, 8], P(None, ('experts', 'dp'), 'context'), may hold values from 0.06 to 0.25
- cotangent: bfloat16 [2, 32, 256, 2048], P(None, ('experts', 'dp'), 'context'), may hold values from -6 to 6
- w_query: bfloat16 [2048, 4096], P('experts'), may hold values from -0.125 to 0.125
- key_weight: bfloat16 [2048, 512], P('experts'), may hold values from -0.125 to 0.125
- value_weight: bfloat16 [2048, 512], P('experts'), may hold values from -0.125 to 0.125
- w_out: bfloat16 [4096, 2048], P('experts'), may hold values from -0.375 to 0.375
- norm_attn: bfloat16 [2048], P('experts'), may hold values from 0.5 to 1.5
- norm_moe: bfloat16 [2048], P('experts'), may hold values from 0.5 to 1.5
- norm_query: bfloat16 [128], P('experts'), may hold values from 0.5 to 1.5
- norm_key: bfloat16 [128], P('experts'), may hold values from 0.5 to 1.5
- w_gate: bfloat16 [16, 2048, 768], P('experts'), may hold values from -0.125 to 0.125
- w_up: bfloat16 [16, 2048, 768], P('experts'), may hold values from -0.125 to 0.125
- w_down: bfloat16 [16, 768, 2048], P('experts'), may hold values from -0.4375 to 0.4375
Outputs:
- output: bfloat16 [2, 32, 256, 2048], P(None, ('experts', 'dp'), 'context')
- input_grad: float32 [2, 32, 256, 2048], P(None, ('experts', 'dp'), 'context')
- grad_w_query: float32 [2048, 4096], P('experts')
- grad_w_key: float32 [2048, 512], P('experts')
- grad_w_value: float32 [2048, 512], P('experts')
- grad_w_out: float32 [4096, 2048], P('experts')
- grad_norm_attn: float32 [2048], P('experts')
- grad_norm_moe: float32 [2048], P('experts')
- grad_norm_query: float32 [128], P('experts')
- grad_norm_key: float32 [128], P('experts')
- grad_w_gate: float32 [16, 2048, 768], P('experts')
- grad_w_up: float32 [16, 2048, 768], P('experts')
- grad_w_down: float32 [16, 768, 2048], P('experts')
The draws below stay inside these ranges and needn't reach their ends.
Inputs may be any that keep to these rules, and one draw needn't show every extreme that they name: `routes`: each row names 8 distinct experts; in each aligned block of 64 rows (leading dimensions taken together in order) no expert is named by more than 33 rows. `lengths`: for every slot index, one of its 2 micro-batches, drawn from the seed, is full.
All inputs are finite; a program needn't handle non-finite values.
Results may differ from the reference program's by a relative error of at most 0.035.
Values may be sent and summed in bfloat16 or wider, within the bound.
No kernel may reach another device: no remote copies, remote signals or barrier semaphores. Data moves between devices by JAX's collectives and lax.ppermute only.
A program may use at most 320 MiB of HBM per device.

```python
import math
import jax
import jax.numpy as jnp
import numpy as np
from jax import lax

MODEL_DIM = 2048
FF = 768
HQ = 32
KEY_HEADS = 4
HEAD_DIM = 128
TOPK = 8
EXPERTS = 16
MB = 2
SLOT_DEV = 64
SLOT_LENGTH = 256
SEQS = 32
QUERY_PER_KEY = 8
MOST = 33


def draw_lengths(key, part):
    key = jax.random.fold_in(key, 7)
    base = jax.random.randint(key, (MB, SEQS), SLOT_LENGTH // 4, SLOT_LENGTH + 1)
    picked = jax.random.randint(jax.random.fold_in(key, 1), (1, SEQS), 0, MB)
    full = jnp.arange(MB, dtype=jnp.int32)[:, None] == picked
    return jnp.where(full, SLOT_LENGTH, base).astype(jnp.int32)


def levels(key, shape, cuts, least, largest):
    loudness = 1.0
    for axis_at, shards_of in cuts:
        heights = jax.random.uniform(jax.random.fold_in(jax.random.fold_in(key, 6), axis_at), (shards_of,), jnp.float32, least / len(cuts), largest / len(cuts))
        loudness = loudness * jnp.repeat(jnp.exp(heights), shape[axis_at] // shards_of).reshape((-1,) + (1,) * (len(shape) - 1 - axis_at))
    return loudness


def assign_block(own_key, own, number, rows, amount, top, reach, lean):
    order = jax.random.permutation(own_key, amount)
    heavy_load, common = shares(amount, rows * top, reach, lean, True), shares(amount, rows * top, reach, lean, False)
    places = jnp.arange(amount)

    def named(sizes, offset_by):
        used = int((sizes > 0).sum())
        fixed = max(1, used // 4)
        moved = fixed + (places - fixed + offset_by * (used - fixed)) % max(1, amount - fixed)
        return jnp.zeros((amount,), jnp.int32).at[order[jnp.where(places < fixed, places, moved)]].set(jnp.asarray(sizes, jnp.int32))

    sizes = jnp.where(number % 4 == 0, named(heavy_load, number // 4), named(common, number - number // 4 - 1))
    mixed = jax.random.permutation(jax.random.fold_in(own, 3), amount)
    source_of, taker = mixed[0:amount // 2 * 2:2], mixed[1:amount // 2 * 2:2]
    room = jnp.minimum(sizes[source_of] - 1, reach - sizes[taker]) // 2
    room = jnp.where((source_of == order[0]) | (taker == order[0]) | (sizes[taker] == 0), 0, jnp.maximum(room, 0))
    moved = jax.random.randint(jax.random.fold_in(own, 4), (amount // 2,), 0, 1 << 20) % (room + 1)
    sizes = sizes.at[source_of].add(-moved).at[taker].add(moved)
    items = jnp.searchsorted(jnp.cumsum(sizes), jnp.arange(rows * top), side="right").astype(jnp.int32)
    grid = items.reshape(top, rows).T
    grid = grid[jax.random.permutation(jax.random.fold_in(own, 1), rows)]
    offset_by = jax.random.randint(jax.random.fold_in(own, 2), (rows, 1), 0, top)
    return jnp.take_along_axis(grid, (jnp.arange(top)[None, :] + offset_by) % top, axis=1)


def shares(amount, total, reach, lean, full):
    loads = [(1 << 20) // math.isqrt(rank ** lean) + 1 for rank in range(1, amount + 1)]
    largest = reach if full else min(reach, max(-(-total // amount), total * loads[0] // sum(loads)))
    least = 1 if total - largest >= amount - 1 else 0
    given, rest = [largest] + [least] * (amount - 1), total - largest - least * (amount - 1)
    while rest > 0:
        movable = [i for i in range(1, amount) if given[i] < largest] or [i for i in range(1, amount) if given[i] < reach]
        pool, left = sum([loads[i] for i in movable]), rest
        for i in movable:
            more = min(reach - given[i], max(1, left * loads[i] // pool), rest)
            given[i] = given[i] + more
            rest = rest - more
    return np.array(given)


def gaussian(rng, dims, width, most, shards=(), kind=jnp.bfloat16):
    values = width * jax.random.normal(rng, dims, jnp.float32)
    if shards:
        values = values * levels(rng, dims, shards, -0.22, 0.18)
    return jnp.clip(values, -most, most).astype(kind)


def setup_inputs(seed: int = 0) -> dict:
    key_list = jax.random.split(jax.random.key(seed), 17)
    tokens = gaussian(key_list[0], (MB, SEQS, SLOT_LENGTH, MODEL_DIM), 1.0, 6.0, ((1, 32), (2, 4)))
    lengths = draw_lengths(jax.random.fold_in(key_list[16], 71), 0)
    routes_keys = jax.random.split(jax.random.fold_in(key_list[2], 1), MB * SEQS * SLOT_LENGTH // SLOT_DEV)
    routes_turns = jax.random.permutation(jax.random.fold_in(key_list[2], 3), MB * SEQS * SLOT_LENGTH // SLOT_DEV)
    routes = jax.vmap(lambda own, number: assign_block(jax.random.fold_in(key_list[2], 2), own, number, SLOT_DEV, EXPERTS, TOPK, MOST, 0))(routes_keys, routes_turns).reshape((MB, SEQS, SLOT_LENGTH, TOPK))
    mix_weights = jnp.clip(jnp.exp(math.log(0.25) - 1.4271164 * jax.random.uniform(key_list[3], (MB, SEQS, SLOT_LENGTH, TOPK), jnp.float32) ** levels(key_list[3], (MB, SEQS, SLOT_LENGTH, TOPK), ((1, 32), (2, 4)), -0.2, 0.2)), 0.06, 0.25)
    cotangent = gaussian(key_list[4], (MB, SEQS, SLOT_LENGTH, MODEL_DIM), 1.0, 6.0, ((1, 32), (2, 4)))
    w_query = gaussian(key_list[5], (MODEL_DIM, HQ * HEAD_DIM), MODEL_DIM ** -0.5, 0.125, ((0, 16),))
    key_weight = gaussian(key_list[6], (MODEL_DIM, KEY_HEADS * HEAD_DIM), MODEL_DIM ** -0.5, 0.125, ((0, 16),))
    value_weight = gaussian(key_list[7], (MODEL_DIM, KEY_HEADS * HEAD_DIM), MODEL_DIM ** -0.5, 0.125, ((0, 16),))
    w_out = gaussian(key_list[8], (HQ * HEAD_DIM, MODEL_DIM), (HQ * HEAD_DIM // 16) ** -0.5, 0.375, ((0, 16),))
    norm_attn = jnp.clip(1.0 + 0.1 * jax.random.normal(key_list[9], (MODEL_DIM,), jnp.float32), 0.5, 1.5).astype(jnp.bfloat16)
    norm_moe = jnp.clip(1.0 + 0.1 * jax.random.normal(key_list[10], (MODEL_DIM,), jnp.float32), 0.5, 1.5).astype(jnp.bfloat16)
    norm_query = jnp.clip(1.0 + 0.1 * jax.random.normal(key_list[11], (HEAD_DIM,), jnp.float32), 0.5, 1.5).astype(jnp.bfloat16)
    norm_key = jnp.clip(1.0 + 0.1 * jax.random.normal(key_list[12], (HEAD_DIM,), jnp.float32), 0.5, 1.5).astype(jnp.bfloat16)
    w_gate = gaussian(key_list[13], (EXPERTS, MODEL_DIM, FF), MODEL_DIM ** -0.5, 0.125, ((0, 16),))
    w_up = gaussian(key_list[14], (EXPERTS, MODEL_DIM, FF), MODEL_DIM ** -0.5, 0.125, ((0, 16),))
    w_down = gaussian(key_list[15], (EXPERTS, FF, MODEL_DIM), (FF // 4) ** -0.5, 0.4375, ((0, 16),))
    return dict(tokens=tokens, lengths=lengths, routes=routes, mix_weights=mix_weights, cotangent=cotangent, w_query=w_query, key_weight=key_weight, value_weight=value_weight, w_out=w_out, norm_attn=norm_attn, norm_moe=norm_moe, norm_query=norm_query, norm_key=norm_key, w_gate=w_gate, w_up=w_up, w_down=w_down)


EPS = 1e-06
ROPE_BASE = 1000000.0
HIGHEST = lax.Precision.HIGHEST

@jax.custom_vjp
def reduced_precision(v):
    return lax.optimization_barrier(v.astype(jnp.bfloat16)).astype(jnp.float32)

@jax.custom_vjp
def low_back(v):
    return v

def low_keep(v):
    return (reduced_precision(v), None)

def low_pass(kept, grad):
    return (grad,)

def back_keep(v):
    return (v, None)

def back_low(kept, grad):
    return (reduced_precision(grad),)
reduced_precision.defvjp(low_keep, low_pass)
low_back.defvjp(back_keep, back_low)

def normalized_input(value_matrix, gain):
    return value_matrix * lax.rsqrt(lax.optimization_barrier(jnp.mean(value_matrix * value_matrix, axis=-1, keepdims=True)) + EPS) * gain

def angles(positions, head_size):
    half_size = head_size // 2
    frequency = ROPE_BASE ** (-jnp.arange(half_size, dtype=jnp.float32) * 2.0 / head_size)
    phase_angle = positions.astype(jnp.float32)[:, None] * frequency[None, :]
    return (jnp.cos(phase_angle), jnp.sin(phase_angle))

def apply_rotation(value_matrix, cosine_table, sine_values):
    half_size = value_matrix.shape[-1] // 2
    first_half = value_matrix[..., :half_size]
    second = value_matrix[..., half_size:]
    cos_rows = cosine_table[:, None, :]
    sin_rows = sine_values[:, None, :]
    return jnp.concatenate([first_half * cos_rows - second * sin_rows, second * cos_rows + first_half * sin_rows], axis=-1)

def attend(packed):
    query_rows, key_matrix, value_matrix, length = packed
    grouped_queries = query_rows.reshape(SLOT_LENGTH, KEY_HEADS, QUERY_PER_KEY, HEAD_DIM)
    logits = jnp.einsum('qhgd,khd->hgqk', grouped_queries, key_matrix, precision=HIGHEST) * HEAD_DIM ** (-0.5)
    logits = low_back(logits)
    positions = jnp.arange(SLOT_LENGTH, dtype=jnp.int32)
    allowed = (positions[None, :] <= positions[:, None]) & (positions[None, :] < length)
    probabilities = reduced_precision(jax.nn.softmax(jnp.where(allowed[None, None], logits, -1e+30), axis=-1))
    mixed = jnp.einsum('hgqk,khd->qhgd', probabilities, value_matrix, precision=HIGHEST)
    return mixed.reshape(SLOT_LENGTH, HQ * HEAD_DIM)

def reference(tokens, lengths, routes, mix_weights, cotangent, w_query, key_weight, value_weight, w_out, norm_attn, norm_moe, norm_query, norm_key, w_gate, w_up, w_down):
    token_batch = MB * SEQS
    total_rows = token_batch * SLOT_LENGTH
    flat = tokens.astype(jnp.float32).reshape(total_rows, MODEL_DIM)
    positions = jnp.arange(SLOT_LENGTH, dtype=jnp.int32)
    valid = (positions[None, None, :] < lengths[:, :, None]).astype(jnp.float32).reshape(total_rows, 1)
    picks = routes.reshape(total_rows, TOPK)
    chosen = (picks[:, :, None] == jnp.arange(EXPERTS, dtype=jnp.int32)[None, None, :]).astype(jnp.float32)
    mixing = lax.optimization_barrier(jnp.sum(chosen * mix_weights.astype(jnp.float32).reshape(total_rows, TOPK, 1), axis=1))
    seq_lengths = lengths.reshape(token_batch)
    cosine_table, sine_values = angles(positions, HEAD_DIM)

    def forward(flat_in, query_w, key_w, value_w, out_w, gain_attn, gain_moe, gain_query, key_gain, gate_w, up_w, down_w):
        normed_in = reduced_precision(normalized_input(flat_in, gain_attn))
        query_pre = low_back(jnp.dot(normed_in, query_w, precision=HIGHEST))
        key_unrotated = low_back(jnp.dot(normed_in, key_w, precision=HIGHEST))
        value_projected = reduced_precision(low_back(jnp.dot(normed_in, value_w, precision=HIGHEST)))
        query_rows = reduced_precision(apply_rotation(normalized_input(query_pre.reshape(token_batch, SLOT_LENGTH, HQ, HEAD_DIM), gain_query), cosine_table, sine_values))
        key_matrix = reduced_precision(apply_rotation(normalized_input(key_unrotated.reshape(token_batch, SLOT_LENGTH, KEY_HEADS, HEAD_DIM), key_gain), cosine_table, sine_values))
        value_matrix = value_projected.reshape(token_batch, SLOT_LENGTH, KEY_HEADS, HEAD_DIM)
        mixed = lax.map(jax.checkpoint(attend), (query_rows, key_matrix, value_matrix, seq_lengths))
        mixed = low_back(reduced_precision(mixed.reshape(total_rows, HQ * HEAD_DIM)))
        resid_mid = flat_in + low_back(jnp.dot(mixed, out_w, precision=HIGHEST))
        normed_mid = reduced_precision(normalized_input(resid_mid, gain_moe))

        def one_expert(carry, packed):
            expert_gate, expert_up, expert_down, weight_col = packed
            inputs = low_back(normed_mid)
            gate_act = low_back(jnp.dot(inputs, expert_gate, precision=HIGHEST))
            up_act = low_back(jnp.dot(inputs, expert_up, precision=HIGHEST))
            hidden = reduced_precision(jax.nn.silu(gate_act) * up_act)
            result = low_back(reduced_precision(jnp.dot(hidden, expert_down, precision=HIGHEST)))
            return (carry + weight_col[:, None] * result, None)
        moe_sum, unused = lax.scan(jax.checkpoint(one_expert), jnp.zeros((total_rows, MODEL_DIM), jnp.float32), (gate_w, up_w, down_w, mixing.T))
        return resid_mid + moe_sum
    params = tuple((weight.astype(jnp.float32) for weight in (w_query, key_weight, value_weight, w_out, norm_attn, norm_moe, norm_query, norm_key, w_gate, w_up, w_down)))
    output, pull = jax.vjp(forward, flat, *params)
    grads = pull(cotangent.astype(jnp.float32).reshape(total_rows, MODEL_DIM) * valid)
    return (output.reshape(MB, SEQS, SLOT_LENGTH, MODEL_DIM).astype(jnp.bfloat16), grads[0].reshape(MB, SEQS, SLOT_LENGTH, MODEL_DIM), grads[1], grads[2], grads[3], grads[4], grads[5], grads[6], grads[7], grads[8], grads[9], grads[10], grads[11])
```

```python
import functools

import jax
import jax.numpy as jnp
from jax import lax
from jax.experimental import pallas as pl
from jax.experimental.pallas import tpu as pltpu
from jax.sharding import PartitionSpec as P

EPS = 1e-06
ROPE_BASE = 1000000.0
F32 = jnp.float32
BF16 = jnp.bfloat16
GROUP = ("context", "dp")
EVERY = ("experts", "context", "dp")
VMEM = 60 * 1024 * 1024
SIDE = 4
TINY = pl.CostEstimate(flops=0, bytes_accessed=1000, transcendentals=0)


def inverse_rms(v):
    return lax.rsqrt(jnp.mean(v * v, axis=-1, keepdims=True) + EPS)


def norm_back(grad_in, v, inverse, gain):
    scaled = grad_in * gain
    return inverse * scaled - v * inverse**3 * jnp.mean(scaled * v, axis=-1, keepdims=True)


def matmul(left, right):
    return jnp.dot(left, right, preferred_element_type=F32)


def against(left, right):
    return lax.dot_general(left, right, (((1,), (1,)), ((), ())), preferred_element_type=F32)


def outer(left, right):
    return lax.dot_general(left, right, (((0,), (0,)), ((), ())), preferred_element_type=F32)


def swap(v):
    return lax.ppermute(v, "dp", [(0, 1), (1, 0)])


def gather_rows(own, ring):
    pieces = [own]
    for k in range(1, ring):
        pieces.append(lax.ppermute(own, "context", [((i + k) % ring, i) for i in range(ring)]))
    mine = jnp.stack(pieces)
    return jnp.stack([mine, swap(mine)])


def ring_sum(pieces):
    ring = len(pieces)
    total = pieces[0].astype(F32)
    for k in range(1, ring):
        got = lax.ppermute(pieces[k], "context", [(i, (i + k) % ring) for i in range(ring)])
        total = total + got.astype(F32)
    return total


def add_cores(theirs, mine):
    other = swap(theirs)
    return [
        (mine[k].astype(F32) + other[k].astype(F32)).astype(BF16) for k in range(mine.shape[0])
    ]


def scatter_rows(theirs, mine):
    return ring_sum(add_cores(theirs, mine))


def gather_members(v):
    ring = lax.axis_size("context")
    pieces = [v]
    for k in range(1, ring):
        pieces.append(lax.ppermute(v, "context", [((i + k) % ring, i) for i in range(ring)]))
    mine = jnp.stack(pieces)
    return mine, swap(mine)


def plane(v, dx, dz):
    moves = [
        (((i // SIDE + dx) % SIDE) * SIDE + (i % SIDE + dz) % SIDE, i) for i in range(SIDE * SIDE)
    ]
    return lax.ppermute(v, "experts", moves)


def after_kernel(v_ref, token_ref, out_ref):
    pass


def after_call(v, token):
    anywhere = pl.BlockSpec(memory_space=pl.ANY)
    return pl.pallas_call(
        after_kernel,
        in_specs=[anywhere, anywhere],
        out_specs=anywhere,
        out_shape=jax.ShapeDtypeStruct(v.shape, v.dtype),
        input_output_aliases={0: 0},
        cost_estimate=TINY,
        name="after",
    )(v, token)


def rope(v, cosines, sines):
    return v * cosines + pltpu.roll(v, v.shape[-1] // 2, 1) * sines


def rope_back(v, cosines, sines):
    return v * cosines + pltpu.roll(v * sines, v.shape[-1] // 2, 1)


def flat(ref):
    v = ref[...]
    return v.reshape(v.shape[1] * v.shape[3], v.shape[4])


def chunks(ref, columns):
    v = ref[:, :-16, :columns]
    return v.reshape(v.shape[0] * v.shape[1], columns)


def out_blocks(ref, first):
    last = ref.shape[2] - first
    rows = last // ref.shape[0]
    for k in range((ref.shape[1] - 16) // rows):
        yield k * last, (k + 1) * last, ref[:, k * rows : (k + 1) * rows, first:].reshape(last, last)


def put(ref, v):
    ref[...] = v.reshape(ref.shape).astype(ref.dtype)


def attend_kernel(
    heads,
    scale,
    x_ref,
    gain_ref,
    w_ref,
    cos_ref,
    sin_ref,
    bias_ref,
    gain_q_ref,
    gain_k_ref,
    token_ref,
    h1_ref,
    qkv_ref,
    heads_ref,
    theirs_ref,
    mine_ref,
    heads_out,
    total,
):
    size = cos_ref.shape[1]
    x = flat(x_ref).astype(F32)
    h1 = (x * inverse_rms(x) * gain_ref[...]).astype(BF16)
    put(h1_ref, h1)
    width = (heads + 2) * size
    qkv = matmul(h1, chunks(w_ref, width))
    put(qkv_ref, qkv)
    cosines, sines, bias = cos_ref[...], sin_ref[...], bias_ref[0]
    k_pre = qkv[:, heads * size : (heads + 1) * size]
    key = rope(k_pre * inverse_rms(k_pre) * gain_k_ref[...], cosines, sines).astype(BF16)
    value = qkv[:, (heads + 1) * size :].astype(BF16)
    for g in range(heads):
        q_pre = qkv[:, g * size : (g + 1) * size]
        query = rope(q_pre * inverse_rms(q_pre) * gain_q_ref[...], cosines, sines).astype(BF16)
        logits = against(query, key) * scale + bias
        scaled = jnp.exp(logits - jnp.max(logits, axis=-1, keepdims=True))
        soft = (scaled / jnp.sum(scaled, axis=-1, keepdims=True)).astype(BF16)
        heads_out[:, g * size : (g + 1) * size] = matmul(soft, value).astype(BF16)
    out = heads_out[...]
    put(heads_ref, out)
    for first, last, block in out_blocks(w_ref, width):
        total[:, first:last] = matmul(out, block).astype(BF16)

    @pl.when(pl.program_id(0) < 2)
    def _():
        put(theirs_ref, total[...])

    @pl.when(pl.program_id(0) >= 2)
    def _():
        put(mine_ref, total[...])


def attend_back_kernel(
    heads,
    scale,
    da_ref,
    x_ref,
    gain_ref,
    w_ref,
    cos_ref,
    sin_ref,
    bias_ref,
    gain_q_ref,
    gain_k_ref,
    qkv_ref,
    token_ref,
    other_token_ref,
    d_qkv_ref,
    theirs_ref,
    mine_ref,
    sum_q_ref,
    sum_k_ref,
    sum_x_ref,
    d_qkv,
):
    size = cos_ref.shape[1]
    step = pl.program_id(0)

    @pl.when(step == 0)
    def _():
        sum_q_ref[...] = jnp.zeros_like(sum_q_ref)
        sum_k_ref[...] = jnp.zeros_like(sum_k_ref)
        sum_x_ref[...] = jnp.zeros_like(sum_x_ref)

    width = (heads + 2) * size
    da = flat(da_ref)
    d_heads = None
    for first, last, block in out_blocks(w_ref, width):
        piece = against(da[:, first:last], block)
        d_heads = piece if d_heads is None else d_heads + piece
    d_heads = d_heads.astype(BF16)
    qkv = flat(qkv_ref)
    cosines, sines, bias = cos_ref[...], sin_ref[...], bias_ref[0]
    gain_q, gain_k = gain_q_ref[...], gain_k_ref[...]
    k_pre = qkv[:, heads * size : (heads + 1) * size]
    inverse_k = inverse_rms(k_pre)
    key = rope(k_pre * inverse_k * gain_k, cosines, sines).astype(BF16)
    value = qkv[:, (heads + 1) * size :].astype(BF16)
    d_key = jnp.zeros(k_pre.shape, F32)
    d_value = jnp.zeros(k_pre.shape, F32)
    sum_q = jnp.zeros((1, size), F32)
    for g in range(heads):
        q_pre = qkv[:, g * size : (g + 1) * size]
        inverse_q = inverse_rms(q_pre)
        query = rope(q_pre * inverse_q * gain_q, cosines, sines).astype(BF16)
        logits = against(query, key) * scale + bias
        scaled = jnp.exp(logits - jnp.max(logits, axis=-1, keepdims=True))
        probs = scaled / jnp.sum(scaled, axis=-1, keepdims=True)
        d_head = d_heads[:, g * size : (g + 1) * size]
        d_probs = against(d_head, value)
        d_scores = probs * (d_probs - jnp.sum(probs * d_probs, axis=-1, keepdims=True))
        d_scores = d_scores.astype(BF16)
        d_query = rope_back(matmul(d_scores, key) * scale, cosines, sines)
        d_key = d_key + outer(d_scores, query)
        d_value = d_value + outer(probs.astype(BF16), d_head)
        sum_q = sum_q + jnp.sum(d_query * q_pre * inverse_q, axis=0, keepdims=True)
        d_qkv[:, g * size : (g + 1) * size] = norm_back(d_query, q_pre, inverse_q, gain_q).astype(
            BF16
        )
    d_key = rope_back(d_key * scale, cosines, sines)
    sum_k = jnp.sum(d_key * k_pre * inverse_k, axis=0, keepdims=True)
    d_qkv[:, heads * size : (heads + 1) * size] = norm_back(d_key, k_pre, inverse_k, gain_k).astype(
        BF16
    )
    d_qkv[:, (heads + 1) * size :] = d_value.astype(BF16)
    grads = d_qkv[...]
    put(d_qkv_ref, grads)
    part = against(grads, chunks(w_ref, width))
    x = flat(x_ref).astype(F32)
    sum_x_ref[0:1, :] += jnp.sum(part * (x * inverse_rms(x)), axis=0, keepdims=True)
    sum_q_ref[0:1, :] += sum_q
    sum_k_ref[0:1, :] += sum_k

    @pl.when(step < 2)
    def _():
        put(theirs_ref, part)

    @pl.when(step >= 2)
    def _():
        put(mine_ref, part)


def attend_call(kernel, operands, extra, outputs, scratch, shape, name, flops):
    ring, micro, row_count, width = shape

    def rows_spec(last):
        return pl.BlockSpec(
            (1, ring, 1, row_count, last), lambda b: (1 - b // 2, 0, b % 2, 0, 0)
        )

    def whole(v):
        return pl.BlockSpec(v.shape, lambda b: (0,) * v.ndim)

    in_specs = [
        rows_spec(v.shape[-1])
        if kind == "rows"
        else pl.BlockSpec((1,) + v.shape[1:], lambda b: ((1 - b // 2) * micro + b % 2, 0, 0))
        if kind == "bias"
        else pl.BlockSpec(memory_space=pl.ANY)
        if kind == "token"
        else whole(v)
        for v, kind in zip(operands, extra)
    ]
    out_shape, out_specs = [], []
    for kind, last, dtype in outputs:
        if kind == "rows":
            out_shape.append(jax.ShapeDtypeStruct((2, ring, micro, row_count, last), dtype))
            out_specs.append(rows_spec(last))
        elif kind == "parts":
            one = jax.ShapeDtypeStruct((1, ring, micro, row_count, last), dtype)
            out_shape += [one, one]
            block = (1, ring, 1, row_count, last)
            out_specs.append(pl.BlockSpec(block, lambda b: (0, 0, jnp.minimum(b, 1), 0, 0)))
            out_specs.append(pl.BlockSpec(block, lambda b: (0, 0, jnp.maximum(b - 2, 0), 0, 0)))
        else:
            out_shape.append(jax.ShapeDtypeStruct((8, last), dtype))
            out_specs.append(pl.BlockSpec((8, last), lambda b: (0, 0)))
    return pl.pallas_call(
        kernel,
        grid=(2 * micro,),
        in_specs=in_specs,
        out_specs=out_specs,
        out_shape=out_shape,
        scratch_shapes=scratch,
        compiler_params=pltpu.CompilerParams(vmem_limit_bytes=VMEM),
        cost_estimate=TINY,
        name=name,
    )(*operands)


def experts_kernel(
    part, h2_ref, dy_ref, w_ref, spread_ref, dg_ref, du_ref, hid_ref, theirs_ref, mine_ref, acc
):
    chunk, block = pl.program_id(0), pl.program_id(1)
    width = h2_ref.shape[1]
    count = w_ref.shape[0] * part
    gate_w = w_ref[:, :part].reshape(count, width)
    up_w = w_ref[:, part : 2 * part].reshape(count, width)
    down_w = w_ref[:, 2 * part :].reshape(count, width)
    h2 = h2_ref[...]
    mix = matmul(dy_ref[:, width:], spread_ref[...])
    gate = against(h2, gate_w)
    up = against(h2, up_w)
    d_hidden = against(dy_ref[:, :width], down_w) * mix
    sigma = jax.nn.sigmoid(gate)
    silu = gate * sigma
    hid_ref[...] = (silu * up * mix).astype(BF16)
    d_gate = (d_hidden * up * sigma * (1.0 + gate * (1.0 - sigma))).astype(BF16)
    d_up = (d_hidden * silu).astype(BF16)
    dg_ref[...] = d_gate
    du_ref[...] = d_up
    total = matmul(d_gate, gate_w) + matmul(d_up, up_w)

    @pl.when(chunk == 0)
    def _():
        acc[block] = total

    @pl.when((chunk == 1) & (block < 2))
    def _():
        theirs_ref[...] = (acc[block] + total).astype(BF16)

    @pl.when((chunk == 1) & (block >= 2))
    def _():
        mine_ref[...] = (acc[block] + total).astype(BF16)


def experts_call(h2, dy, weights, spread, part):
    rows, width = h2.shape
    owners, depth, _ = weights.shape
    hidden = owners * part
    n, blocks = 2, 4
    step, wide = rows // blocks, hidden // n
    half = jax.ShapeDtypeStruct((rows // 2, width), BF16)
    wide_shape = jax.ShapeDtypeStruct((rows, hidden), BF16)

    def row(c, b):
        return (b + blocks // 2) % blocks

    wide_spec = pl.BlockSpec((step, wide), lambda c, b: (row(c, b), c))
    return pl.pallas_call(
        functools.partial(experts_kernel, part),
        grid=(n, blocks),
        in_specs=[
            pl.BlockSpec((step, width), lambda c, b: (row(c, b), 0)),
            pl.BlockSpec((step, dy.shape[1]), lambda c, b: (row(c, b), 0)),
            pl.BlockSpec((owners // n, depth, width), lambda c, b: (c, 0, 0)),
            pl.BlockSpec((spread.shape[0], wide), lambda c, b: (0, c)),
        ],
        out_specs=[
            wide_spec,
            wide_spec,
            wide_spec,
            pl.BlockSpec((step, width), lambda c, b: (c * jnp.minimum(b, 1), 0)),
            pl.BlockSpec((step, width), lambda c, b: (c * jnp.maximum(b - 2, 0), 0)),
        ],
        out_shape=[wide_shape, wide_shape, wide_shape, half, half],
        scratch_shapes=[pltpu.VMEM((blocks, step, width), F32)],
        compiler_params=pltpu.CompilerParams(vmem_limit_bytes=VMEM),
        cost_estimate=TINY,
        name="experts_rows",
    )(h2, dy, weights, spread)


def expert_grads_kernel(
    part, dg_ref, du_ref, hid_ref, h2_ref, dy_ref, after_ref, out_ref, token_ref
):
    width = h2_ref.shape[1]
    group = out_ref.shape[0]
    h2 = h2_ref[...]
    out_ref[:, :part] = outer(dg_ref[...], h2).astype(BF16).reshape(group, part, width)
    out_ref[:, part : 2 * part] = outer(du_ref[...], h2).astype(BF16).reshape(group, part, width)
    out_ref[:, 2 * part :] = (
        outer(hid_ref[...], dy_ref[:, :width]).astype(BF16).reshape(group, part, width)
    )
    token_ref[...] = jnp.zeros_like(token_ref)


def expert_grads_call(d_gate, d_up, hidden, h2, dy, after, owners, part):
    rows, width = h2.shape
    n = 4
    wide = d_gate.shape[1] // n
    wide_spec = pl.BlockSpec((rows, wide), lambda c: (0, c))
    return pl.pallas_call(
        functools.partial(expert_grads_kernel, part),
        grid=(n,),
        in_specs=[
            wide_spec,
            wide_spec,
            wide_spec,
            pl.BlockSpec((rows, width), lambda c: (0, 0)),
            pl.BlockSpec((rows, dy.shape[1]), lambda c: (0, 0)),
            pl.BlockSpec(memory_space=pl.ANY),
        ],
        out_specs=[
            pl.BlockSpec((owners // n, 3 * part, width), lambda c: (c, 0, 0)),
            pl.BlockSpec((8, 128), lambda c: (0, 0)),
        ],
        out_shape=[
            jax.ShapeDtypeStruct((owners, 3 * part, width), BF16),
            jax.ShapeDtypeStruct((8, 128), F32),
        ],
        compiler_params=pltpu.CompilerParams(vmem_limit_bytes=VMEM),
        cost_estimate=TINY,
        name="experts_weights",
    )(d_gate, d_up, hidden, h2, dy, after)


def add_kernel(theirs_ref, mine_ref, token_ref, *out_refs):
    for k, out_ref in enumerate(out_refs):
        out_ref[...] = (theirs_ref[k].astype(F32) + mine_ref[k].astype(F32)).astype(BF16)


def add_call(theirs, mine, token):
    shape = theirs.shape
    one = jax.ShapeDtypeStruct(shape[1:], BF16)
    vmem = pl.BlockSpec(memory_space=pltpu.VMEM)
    return pl.pallas_call(
        add_kernel,
        in_specs=[vmem, vmem, pl.BlockSpec(memory_space=pl.ANY)],
        out_specs=[vmem] * shape[0],
        out_shape=[one] * shape[0],
        compiler_params=pltpu.CompilerParams(vmem_limit_bytes=VMEM),
        cost_estimate=TINY,
        name="add_cores",
    )(theirs, mine, token)


def gate_up_down_kernel(part, in_ref, gate_ref, up_ref, down_ref):
    last = in_ref.shape[2]
    count = in_ref.shape[0] * part
    gate_ref[...] = in_ref[:, :part].reshape(count, last).astype(F32).T
    up_ref[...] = in_ref[:, part : 2 * part].reshape(count, last).astype(F32).T
    down_ref[...] = in_ref[:, 2 * part :].reshape(count, last).astype(F32)


def gate_up_down_call(gathered, part):
    members, depth, width = gathered.shape
    ff = members * part
    n = 8
    step = width // n
    return pl.pallas_call(
        functools.partial(gate_up_down_kernel, part),
        grid=(n,),
        in_specs=[pl.BlockSpec((members, depth, step), lambda c: (0, 0, c))],
        out_specs=[
            pl.BlockSpec((step, ff), lambda c: (c, 0)),
            pl.BlockSpec((step, ff), lambda c: (c, 0)),
            pl.BlockSpec((ff, step), lambda c: (0, c)),
        ],
        out_shape=[
            jax.ShapeDtypeStruct((width, ff), F32),
            jax.ShapeDtypeStruct((width, ff), F32),
            jax.ShapeDtypeStruct((ff, width), F32),
        ],
        compiler_params=pltpu.CompilerParams(vmem_limit_bytes=VMEM),
        cost_estimate=TINY,
        name="experts_results",
    )(gathered)


def attend_grads_kernel(
    cut, place_ref, h1_ref, d_qkv_ref, out_ref, gains_ref, token_ref, *refs
):
    firsts, seconds, share = refs[:SIDE], refs[SIDE : 2 * SIDE], refs[-1]
    step = pl.program_id(0)
    last = d_qkv_ref.shape[1]
    depth = share.shape[1] - 16
    grad = outer(h1_ref[...], d_qkv_ref[...]).astype(BF16)
    share[:, :depth, :last] = grad.reshape(SIDE, depth, last)
    rows, columns = out_ref.shape[1], share.shape[2] - last
    for k in range(depth // rows):
        share[:, k * rows : (k + 1) * rows, last:] = out_ref[:, :, k * columns : (k + 1) * columns]
    share[:, depth:] = gains_ref[...]
    for k in range(SIDE):

        @pl.when(step == k)
        def _():
            firsts[k][...] = share[:, :cut]

        seconds[k][0] = share[lax.rem(place_ref[1] + k, SIDE), cut:]


def attend_grads_call(place, h1, d_qkv, grad_out, gains, token, cut):
    rows, width = h1.shape
    owners, extra, columns = gains.shape
    depth = width // owners
    last = d_qkv.shape[1]

    def at(i, place):
        return lax.rem(place[0] + i, SIDE)

    first = jax.ShapeDtypeStruct((SIDE, cut, columns), BF16)
    second = jax.ShapeDtypeStruct((SIDE, depth + extra - cut, columns), BF16)
    outs = pl.pallas_call(
        functools.partial(attend_grads_kernel, cut),
        grid_spec=pltpu.PrefetchScalarGridSpec(
            num_scalar_prefetch=1,
            grid=(SIDE,),
            in_specs=[
                pl.BlockSpec((rows, width // SIDE), lambda i, place: (0, at(i, place))),
                pl.BlockSpec((rows, last), lambda i, place: (0, 0)),
                pl.BlockSpec((SIDE,) + grad_out.shape[1:], lambda i, place: (at(i, place), 0, 0)),
                pl.BlockSpec((SIDE, extra, columns), lambda i, place: (at(i, place), 0, 0)),
                pl.BlockSpec(memory_space=pl.ANY),
            ],
            out_specs=[pl.BlockSpec(first.shape, lambda i, place: (0, 0, 0))] * SIDE
            + [pl.BlockSpec((1,) + second.shape[1:], lambda i, place: (i, 0, 0))] * SIDE,
            scratch_shapes=[pltpu.VMEM((SIDE, depth + extra, columns), BF16)],
        ),
        out_shape=[first] * SIDE + [second] * SIDE,
        compiler_params=pltpu.CompilerParams(vmem_limit_bytes=VMEM),
        cost_estimate=TINY,
        name="attention_weights",
    )(place, h1, d_qkv, grad_out, gains, token)
    return outs[:SIDE], outs[SIDE:]


def total_of(refs):
    total = refs[0][...].astype(F32)
    for ref in refs[1:]:
        total = total + ref[...].astype(F32)
    return total.astype(BF16)


def half_sum_kernel(place_ref, *refs):
    firsts, seconds, total = refs[2 * SIDE : 3 * SIDE], refs[3 * SIDE : 4 * SIDE], refs[-1]
    total[...] = total_of(refs[:SIDE])
    other = total_of(refs[SIDE : 2 * SIDE])
    for k in range(SIDE):
        firsts[k][...] = total[lax.rem(place_ref[1] + k, SIDE)]
        seconds[k][...] = other[k]


def half_sum_call(place, firsts, seconds):
    vmem = pl.BlockSpec(memory_space=pltpu.VMEM)
    outs = pl.pallas_call(
        half_sum_kernel,
        grid_spec=pltpu.PrefetchScalarGridSpec(
            num_scalar_prefetch=1,
            grid=(),
            in_specs=[vmem] * (2 * SIDE),
            out_specs=[vmem] * (2 * SIDE),
            scratch_shapes=[pltpu.VMEM(firsts[0].shape, BF16)],
        ),
        out_shape=[jax.ShapeDtypeStruct(v.shape[1:], BF16) for v in (*firsts, *seconds)],
        compiler_params=pltpu.CompilerParams(vmem_limit_bytes=VMEM),
        cost_estimate=TINY,
        name="half_sum",
    )(place, *firsts, *seconds)
    return outs[:SIDE], outs[SIDE:]


def last_sum_kernel(*refs):
    out = refs[-1]
    cut = refs[0].shape[0]
    out[:cut] = total_of(refs[:SIDE])
    out[cut:] = total_of(refs[SIDE : 2 * SIDE])


def last_sum_call(firsts, seconds):
    rows, columns = firsts[0].shape[0] + seconds[0].shape[0], firsts[0].shape[1]
    vmem = pl.BlockSpec(memory_space=pltpu.VMEM)
    return pl.pallas_call(
        last_sum_kernel,
        in_specs=[vmem] * (2 * SIDE),
        out_specs=vmem,
        out_shape=jax.ShapeDtypeStruct((rows, columns), BF16),
        compiler_params=pltpu.CompilerParams(vmem_limit_bytes=VMEM),
        cost_estimate=TINY,
        name="last_sum",
    )(*firsts, *seconds)


def plane_send(pieces, dx, dz):
    return [pieces[0]] + [plane(pieces[k], -k * dx, -k * dz) for k in range(1, SIDE)]


def columns_kernel(
    heads_width, size, where_ref, mine_ref, theirs_ref, q_ref, k_ref, v_ref, out_ref, sum_ref
):
    depth = q_ref.shape[0]
    last = heads_width + 2 * size
    mine, theirs = mine_ref[0].astype(F32), theirs_ref[0].astype(F32)
    first = where_ref[1] == 0
    low, high = jnp.where(first, mine, theirs), jnp.where(first, theirs, mine)
    q_ref[:, :heads_width] = low[:depth, :heads_width]
    q_ref[:, heads_width:] = high[:depth, :heads_width]
    both = mine + theirs
    k_ref[...] = both[:depth, heads_width : heads_width + size]
    v_ref[...] = both[:depth, heads_width + size : last]
    columns = mine.shape[1] - last
    rows = out_ref.shape[0] // 2
    for k in range(depth // rows):
        out_ref[:rows, k * columns : (k + 1) * columns] = low[k * rows : (k + 1) * rows, last:]
        out_ref[rows:, k * columns : (k + 1) * columns] = high[k * rows : (k + 1) * rows, last:]

    @pl.when(pl.program_id(0) == 0)
    def _():
        sum_ref[...] = jnp.zeros_like(sum_ref)

    sum_ref[...] += both[depth:]


def columns_call(where, mine, theirs, depth, heads_width, size, out_rows, width):
    ring, rows, last = mine.shape
    cores = 2

    def at(k, where):
        return (0, lax.rem(where[0] + k, ring))

    def row_at(k, where):
        return (lax.rem(where[0] + k, ring), 0)

    return pl.pallas_call(
        functools.partial(columns_kernel, heads_width, size),
        grid_spec=pltpu.PrefetchScalarGridSpec(
            num_scalar_prefetch=1,
            grid=(ring,),
            in_specs=[pl.BlockSpec((1, rows, last), lambda k, where: (k, 0, 0))] * 2,
            out_specs=[
                pl.BlockSpec((depth, cores * heads_width), at),
                pl.BlockSpec((depth, size), at),
                pl.BlockSpec((depth, size), at),
                pl.BlockSpec((out_rows // ring, width), row_at),
                pl.BlockSpec((rows - depth, last), lambda k, where: (0, 0)),
            ],
        ),
        out_shape=[
            jax.ShapeDtypeStruct((depth, ring * cores * heads_width), F32),
            jax.ShapeDtypeStruct((depth, ring * size), F32),
            jax.ShapeDtypeStruct((depth, ring * size), F32),
            jax.ShapeDtypeStruct((out_rows, width), F32),
            jax.ShapeDtypeStruct((rows - depth, last), F32),
        ],
        compiler_params=pltpu.CompilerParams(vmem_limit_bytes=VMEM),
        cost_estimate=TINY,
        name="attention_results",
    )(where, mine, theirs)


def expert_out_kernel(part, hid_ref, w_ref, token_ref, theirs_ref, mine_ref):
    width = w_ref.shape[2]
    block = pl.program_id(0)
    total = matmul(hid_ref[...], w_ref[...].reshape(w_ref.shape[0] * part, width)).astype(BF16)

    @pl.when(block < 2)
    def _():
        theirs_ref[...] = total

    @pl.when(block >= 2)
    def _():
        mine_ref[...] = total


def expert_out_call(hidden, weights, token, part):
    rows, wide = hidden.shape
    owners, _, width = weights.shape
    blocks = 4
    step = rows // blocks
    half = jax.ShapeDtypeStruct((rows // 2, width), BF16)
    return pl.pallas_call(
        functools.partial(expert_out_kernel, part),
        grid=(blocks,),
        in_specs=[
            pl.BlockSpec((step, wide), lambda b: ((b + blocks // 2) % blocks, 0)),
            pl.BlockSpec((owners, part, width), lambda b: (0, 2, 0)),
            pl.BlockSpec(memory_space=pl.ANY),
        ],
        out_specs=[
            pl.BlockSpec((step, width), lambda b: (jnp.minimum(b, 1), 0)),
            pl.BlockSpec((step, width), lambda b: (jnp.maximum(b - 2, 0), 0)),
        ],
        out_shape=[half, half],
        compiler_params=pltpu.CompilerParams(vmem_limit_bytes=VMEM),
        cost_estimate=TINY,
        name="experts_out",
    )(hidden, weights, token)


def local(
    tokens,
    lengths,
    routes,
    mix_weights,
    cotangent,
    w_query,
    key_weight,
    value_weight,
    w_out,
    norm_attn,
    norm_moe,
    norm_query,
    norm_key,
    w_gate,
    w_up,
    w_down,
):
    owners = lax.axis_size("experts")
    ring = lax.axis_size("context")
    cores = lax.axis_size("dp")
    members = ring * cores
    y = lax.axis_index("context")
    d = lax.axis_index("dp")
    j = y * cores + d
    micro, _, row_count, width = tokens.shape
    head = norm_query.shape[0] * owners
    q_width = w_query.shape[1] // members
    q_heads = q_width // head
    depth = w_query.shape[0]
    ff = w_gate.shape[2]
    ff_part = ff // members
    out_rows = w_out.shape[0]
    out_part = out_rows // members
    seqs = cores * micro
    span = ring * row_count
    rows = seqs * span
    scale = head ** (-0.5)

    forth = [
        (es * members + k, ((es % cores) * members + k) * members + es // cores)
        for es in range(owners)
        for k in range(members)
    ]
    back = [(b, a) for a, b in forth]
    out_chunk = lax.ppermute(
        lax.dynamic_slice_in_dim(w_out, j * out_part, out_part, axis=0), EVERY, forth
    )
    expert_pack = jnp.concatenate(
        [
            lax.dynamic_slice_in_dim(w_gate[0], j * ff_part, ff_part, axis=1).T,
            lax.dynamic_slice_in_dim(w_up[0], j * ff_part, ff_part, axis=1).T,
            lax.dynamic_slice_in_dim(w_down[0], j * ff_part, ff_part, axis=0),
        ],
        axis=0,
    )
    gains = jnp.concatenate([norm_attn, norm_moe, norm_query, norm_key])
    packed = jnp.concatenate(
        [
            lax.dynamic_slice_in_dim(w_query, j * q_width, q_width, axis=1),
            lax.dynamic_slice_in_dim(key_weight, y * head, head, axis=1),
            lax.dynamic_slice_in_dim(value_weight, y * head, head, axis=1),
            jnp.concatenate(jnp.split(out_chunk, depth // out_part, axis=1), axis=0),
        ],
        axis=1,
    )
    qkv_width = q_width + 2 * head
    gain_rows = jnp.pad(gains[None], ((0, 15), (0, packed.shape[1] - gains.shape[0])))
    shared = lax.all_gather(
        jnp.concatenate([packed, gain_rows]), "experts", axis=0, tiled=False
    )
    expert_all = lax.all_gather(expert_pack, "experts", axis=0, tiled=False)
    gain_row = shared[:, depth]
    gain_row = gain_row.astype(F32)
    gain_attn = gain_row[:, :depth].reshape(-1)
    gain_moe = gain_row[:, depth : 2 * depth].reshape(-1)
    eighth = norm_query.shape[0]
    gain_query = gain_row[:, 2 * depth : 2 * depth + eighth].reshape(-1)
    gain_key = gain_row[:, 2 * depth + eighth : 2 * depth + 2 * eighth].reshape(-1)
    hidden_width = owners * ff_part

    x_own = tokens[:, 0]
    x_rows = gather_rows(x_own, ring)
    len_all = jnp.stack([lengths[:, 0], swap(lengths[:, 0])]).reshape(seqs)
    own_pos = y * row_count + jnp.arange(row_count, dtype=jnp.int32)
    valid = (own_pos[None, :] < lengths[:, 0][:, None]).astype(F32)
    dy_own = (cotangent[:, 0].astype(F32) * valid[:, :, None]).astype(BF16)
    ids = jnp.arange(owners, dtype=jnp.int32)
    mix_own = jnp.sum(
        jnp.where(routes[:, 0][..., None] == ids, mix_weights[:, 0][..., None], 0.0), axis=2
    )
    mix_high = mix_own.astype(BF16)
    mix_low = (mix_own - mix_high.astype(F32)).astype(BF16)
    lanes = 128
    mix_pad = jnp.zeros((micro, row_count, lanes - 2 * owners), BF16)
    dy_mix = gather_rows(jnp.concatenate([dy_own, mix_high, mix_low, mix_pad], axis=-1), ring)
    dy_mix = dy_mix.reshape(rows, width + lanes)
    lane = jnp.arange(lanes, dtype=jnp.int32)
    spread = (
        (jnp.arange(hidden_width, dtype=jnp.int32)[None, :] // ff_part == (lane % owners)[:, None])
        & (lane < 2 * owners)[:, None]
    ).astype(BF16)

    k_index = jnp.arange(span, dtype=jnp.int32)
    pos = ((y + k_index // row_count) % ring) * row_count + k_index % row_count
    frequency = ROPE_BASE ** (-jnp.arange(head // 2, dtype=F32) * 2.0 / head)
    phase = pos.astype(F32)[:, None] * frequency[None, :]
    cosines, sines = jnp.cos(phase), jnp.sin(phase)
    cosines = jnp.concatenate([cosines, cosines], axis=1)
    sines = jnp.concatenate([-sines, sines], axis=1)
    allowed = (pos[None, None, :] <= pos[None, :, None]) & (
        pos[None, None, :] < len_all[:, None, None]
    )
    bias = jnp.where(allowed, 0.0, -1e30).astype(F32)

    shape = (ring, micro, row_count, width)
    head_gains = (gain_query[None], gain_key[None])
    h1, qkv, heads_out, theirs, mine = attend_call(
        functools.partial(attend_kernel, q_heads, scale),
        (x_rows, gain_attn[None], shared, cosines, sines, bias, *head_gains, dy_mix),
        ("rows", "", "", "", "", "bias", "", "", "token"),
        (
            ("rows", width, BF16),
            ("rows", qkv_width, F32),
            ("rows", q_width, BF16),
            ("parts", width, BF16),
        ),
        [pltpu.VMEM((span, q_width), BF16), pltpu.VMEM((span, width), BF16)],
        shape,
        "attention",
        6_000_000_000,
    )
    attn_own = scatter_rows(theirs[0], mine[0])
    x1 = x_own.astype(F32) + attn_own
    inverse_mid = inverse_rms(x1)
    h2 = gather_rows((x1 * inverse_mid * gain_moe).astype(BF16), ring).reshape(rows, width)

    d_gate, d_up, hidden, theirs, mine = experts_call(h2, dy_mix, expert_all, spread, ff_part)
    pieces = add_call(swap(theirs.reshape(shape)), mine.reshape(shape), d_gate)
    d_h2 = ring_sum(pieces)
    grad_experts, token = expert_grads_call(
        d_gate, d_up, hidden, h2, dy_mix, pieces[1], owners, ff_part
    )
    moe_theirs, moe_mine = expert_out_call(hidden, expert_all, token, ff_part)

    grad_gain_moe = jnp.sum(d_h2 * x1 * inverse_mid, axis=(0, 1))
    d_x1 = dy_own.astype(F32) + norm_back(d_h2, x1, inverse_mid, gain_moe)
    grad_experts = lax.psum_scatter(
        after_call(grad_experts, d_x1), "experts", scatter_dimension=0, tiled=False
    )
    d_attn = gather_rows(d_x1.astype(BF16), ring)
    moe_pieces = add_call(swap(moe_theirs.reshape(shape)), moe_mine.reshape(shape), d_attn)
    output = (x1 + ring_sum(moe_pieces)).astype(BF16)[:, None]
    grad_out = outer(heads_out.reshape(rows, q_width), d_attn.reshape(rows, width)).astype(BF16)
    grad_out = grad_out.reshape(owners, out_part, width)
    d_qkv, theirs, mine, sum_q, sum_k, sum_x = attend_call(
        functools.partial(attend_back_kernel, q_heads, scale),
        (
            d_attn,
            x_rows,
            gain_attn[None],
            shared,
            cosines,
            sines,
            bias,
            *head_gains,
            qkv,
            moe_pieces[0],
            grad_out,
        ),
        ("rows", "rows", "", "", "", "", "bias", "", "", "rows", "token", "token"),
        (
            ("rows", qkv_width, BF16),
            ("parts", width, BF16),
            ("sum", head, F32),
            ("sum", head, F32),
            ("sum", width, F32),
        ),
        [pltpu.VMEM((span, qkv_width), BF16)],
        shape,
        "attention_back",
        9_000_000_000,
    )
    grad_gain_query, grad_gain_key, grad_gain_attn = sum_q[0], sum_k[0], sum_x[0]
    d_h1 = scatter_rows(theirs[0], mine[0])
    x_f32 = x_own.astype(F32)
    input_grad = (d_x1 + norm_back(d_h1, x_f32, inverse_rms(x_f32), gain_attn))[:, None]
    h1, d_qkv = h1.reshape(rows, width), d_qkv.reshape(rows, qkv_width)

    where = jnp.stack([y, d]).astype(jnp.int32)
    grad_gains = jnp.concatenate(
        [
            grad_gain_attn.reshape(owners, depth),
            grad_gain_moe.reshape(owners, depth),
            grad_gain_query.reshape(owners, eighth),
            grad_gain_key.reshape(owners, eighth),
        ],
        axis=1,
    ).astype(BF16)
    grad_gains = jnp.pad(
        grad_gains[:, None], ((0, 0), (0, 15), (0, shared.shape[2] - grad_gains.shape[1]))
    )
    index = lax.axis_index("experts")
    place = jnp.stack([index // SIDE, index % SIDE]).astype(jnp.int32)
    firsts, seconds = attend_grads_call(
        place, h1, d_qkv, grad_out, grad_gains, output, depth // 2 + 16
    )
    firsts, seconds = half_sum_call(
        place, plane_send(firsts, 1, 0), plane_send(seconds, 0, 1)
    )
    grads = last_sum_call(plane_send(firsts, 0, 1), plane_send(seconds, 1, 0))
    out_back = lax.ppermute(grads[:depth, qkv_width:], EVERY, back)
    grads = jnp.concatenate(
        [grads[:, :qkv_width], jnp.pad(out_back, ((0, 16), (0, 0)))], axis=1
    )
    result_q, result_k, result_v, result_out, gain_sum = columns_call(
        where, *gather_members(grads), depth, q_width, head, w_out.shape[0], width
    )
    gain_sum = gain_sum[0]
    grad_experts = after_call(grad_experts, seconds[1])
    all_experts = lax.all_gather(grad_experts, GROUP, axis=0, tiled=False)
    result_gate, result_up, result_down = gate_up_down_call(all_experts, ff_part)
    return (
        output,
        input_grad,
        result_q,
        result_k,
        result_v,
        result_out,
        gain_sum[:depth],
        gain_sum[depth : 2 * depth],
        gain_sum[2 * depth : 2 * depth + eighth],
        gain_sum[2 * depth + eighth : 2 * depth + 2 * eighth],
        result_gate[None],
        result_up[None],
        result_down[None],
    )


def solution(mesh):
    rows = P(None, ("experts", "dp"), "context", None)
    in_specs = (
        rows,
        P(None, ("experts", "dp")),
        rows,
        rows,
        rows,
        P("experts", None),
        P("experts", None),
        P("experts", None),
        P("experts", None),
        P("experts"),
        P("experts"),
        P("experts"),
        P("experts"),
        P("experts", None, None),
        P("experts", None, None),
        P("experts", None, None),
    )
    out_specs = (
        rows,
        rows,
        P("experts", None),
        P("experts", None),
        P("experts", None),
        P("experts", None),
        P("experts"),
        P("experts"),
        P("experts"),
        P("experts"),
        P("experts", None, None),
        P("experts", None, None),
        P("experts", None, None),
    )
    return jax.shard_map(local, mesh=mesh, in_specs=in_specs, out_specs=out_specs, check_vma=False)
```

```python
import functools

import jax
import jax.numpy as jnp
from jax import lax
from jax.experimental import pallas as pl
from jax.experimental.pallas import tpu as pltpu
from jax.sharding import PartitionSpec as P

EPS = 1e-06
ROPE_BASE = 1000000.0
F32 = jnp.float32
BF16 = jnp.bfloat16
GROUP = ("context", "dp")
EVERY = ("experts", "context", "dp")
VMEM = 60 * 1024 * 1024
SIDE = 4
TINY = pl.CostEstimate(flops=0, bytes_accessed=1000, transcendentals=0)


def inverse_rms(v):
    return lax.rsqrt(jnp.mean(v * v, axis=-1, keepdims=True) + EPS)


def norm_back(grad_in, v, inverse, gain):
    scaled = grad_in * gain
    return inverse * scaled - v * inverse**3 * jnp.mean(scaled * v, axis=-1, keepdims=True)


def matmul(left, right):
    return jnp.dot(left, right, preferred_element_type=F32)


def against(left, right):
    return lax.dot_general(left, right, (((1,), (1,)), ((), ())), preferred_element_type=F32)


def outer(left, right):
    return lax.dot_general(left, right, (((0,), (0,)), ((), ())), preferred_element_type=F32)


def swap(v):
    return lax.ppermute(v, "dp", [(0, 1), (1, 0)])


def ring_stack(own, ring):
    pieces = [own]
    for k in range(1, ring):
        pieces.append(lax.ppermute(own, "context", [((i + k) % ring, i) for i in range(ring)]))
    return jnp.stack(pieces)


def gather_rows(own, ring):
    mine = ring_stack(own, ring)
    return jnp.stack([mine, swap(mine)])


def ring_sum(pieces):
    ring = len(pieces)
    total = pieces[0].astype(F32)
    for k in range(1, ring):
        got = lax.ppermute(pieces[k], "context", [(i, (i + k) % ring) for i in range(ring)])
        total = total + got.astype(F32)
    return total


def add_cores(theirs, mine):
    other = swap(theirs)
    return [
        (mine[k].astype(F32) + other[k].astype(F32)).astype(BF16) for k in range(mine.shape[0])
    ]


def scatter_rows(theirs, mine):
    return ring_sum(add_cores(theirs, mine))


def gather_members(v):
    ring = lax.axis_size("context")
    pieces = [v]
    for k in range(1, ring):
        pieces.append(lax.ppermute(v, "context", [((i + k) % ring, i) for i in range(ring)]))
    mine = jnp.stack(pieces)
    return mine, swap(mine)


def plane(v, dx, dz):
    moves = [
        (((i // SIDE + dx) % SIDE) * SIDE + (i % SIDE + dz) % SIDE, i) for i in range(SIDE * SIDE)
    ]
    return lax.ppermute(v, "experts", moves)


def after_kernel(v_ref, *refs):
    pass


def after_call(v, *tokens):
    anywhere = pl.BlockSpec(memory_space=pl.ANY)
    return pl.pallas_call(
        after_kernel,
        in_specs=[anywhere] * (1 + len(tokens)),
        out_specs=anywhere,
        out_shape=jax.ShapeDtypeStruct(v.shape, v.dtype),
        input_output_aliases={0: 0},
        cost_estimate=TINY,
        name="after",
    )(v, *tokens)


def rope(v, cosines, sines):
    return v * cosines + pltpu.roll(v, v.shape[-1] // 2, 1) * sines


def rope_back(v, cosines, sines):
    return v * cosines + pltpu.roll(v * sines, v.shape[-1] // 2, 1)


def flat(ref):
    v = ref[...]
    return v.reshape(v.shape[1] * v.shape[3], v.shape[4])


def chunks(ref, columns):
    v = ref[:, :-16, :columns]
    return v.reshape(v.shape[0] * v.shape[1], columns)


def out_blocks(ref, first):
    last = ref.shape[2] - first
    rows = last // ref.shape[0]
    for k in range((ref.shape[1] - 16) // rows):
        yield k * last, (k + 1) * last, ref[:, k * rows : (k + 1) * rows, first:].reshape(last, last)


def put(ref, v):
    ref[...] = v.reshape(ref.shape).astype(ref.dtype)


def attend_kernel(
    heads,
    scale,
    x_ref,
    gain_ref,
    w_ref,
    cos_ref,
    sin_ref,
    bias_ref,
    gain_q_ref,
    gain_k_ref,
    token_ref,
    h1_ref,
    qkv_ref,
    heads_ref,
    theirs_ref,
    mine_ref,
    heads_out,
    total,
):
    size = cos_ref.shape[1]
    x = flat(x_ref).astype(F32)
    h1 = (x * inverse_rms(x) * gain_ref[...]).astype(BF16)
    put(h1_ref, h1)
    width = (heads + 2) * size
    qkv = matmul(h1, chunks(w_ref, width))
    put(qkv_ref, qkv)
    cosines, sines, bias = cos_ref[...], sin_ref[...], bias_ref[0]
    k_pre = qkv[:, heads * size : (heads + 1) * size]
    key = rope(k_pre * inverse_rms(k_pre) * gain_k_ref[...], cosines, sines).astype(BF16)
    value = qkv[:, (heads + 1) * size :].astype(BF16)
    for g in range(heads):
        q_pre = qkv[:, g * size : (g + 1) * size]
        query = rope(q_pre * inverse_rms(q_pre) * gain_q_ref[...], cosines, sines).astype(BF16)
        logits = against(query, key) * scale + bias
        scaled = jnp.exp(logits - jnp.max(logits, axis=-1, keepdims=True))
        soft = (scaled / jnp.sum(scaled, axis=-1, keepdims=True)).astype(BF16)
        heads_out[:, g * size : (g + 1) * size] = matmul(soft, value).astype(BF16)
    out = heads_out[...]
    put(heads_ref, out)
    for first, last, block in out_blocks(w_ref, width):
        total[:, first:last] = matmul(out, block).astype(BF16)

    @pl.when(pl.program_id(0) < 2)
    def _():
        put(theirs_ref, total[...])

    @pl.when(pl.program_id(0) >= 2)
    def _():
        put(mine_ref, total[...])


def attend_back_kernel(
    heads,
    scale,
    theirs_da_ref,
    mine_da_ref,
    x_ref,
    gain_ref,
    w_ref,
    cos_ref,
    sin_ref,
    bias_ref,
    gain_q_ref,
    gain_k_ref,
    qkv_ref,
    token_ref,
    other_token_ref,
    d_qkv_ref,
    theirs_ref,
    mine_ref,
    sum_q_ref,
    sum_k_ref,
    sum_x_ref,
    d_qkv,
):
    size = cos_ref.shape[1]
    step = pl.program_id(0)

    @pl.when(step == 0)
    def _():
        sum_q_ref[...] = jnp.zeros_like(sum_q_ref)
        sum_k_ref[...] = jnp.zeros_like(sum_k_ref)
        sum_x_ref[...] = jnp.zeros_like(sum_x_ref)

    width = (heads + 2) * size
    da = jnp.where(step < 2, flat(theirs_da_ref), flat(mine_da_ref))
    d_heads = None
    for first, last, block in out_blocks(w_ref, width):
        piece = against(da[:, first:last], block)
        d_heads = piece if d_heads is None else d_heads + piece
    d_heads = d_heads.astype(BF16)
    qkv = flat(qkv_ref)
    cosines, sines, bias = cos_ref[...], sin_ref[...], bias_ref[0]
    gain_q, gain_k = gain_q_ref[...], gain_k_ref[...]
    k_pre = qkv[:, heads * size : (heads + 1) * size]
    inverse_k = inverse_rms(k_pre)
    key = rope(k_pre * inverse_k * gain_k, cosines, sines).astype(BF16)
    value = qkv[:, (heads + 1) * size :].astype(BF16)
    d_key = jnp.zeros(k_pre.shape, F32)
    d_value = jnp.zeros(k_pre.shape, F32)
    sum_q = jnp.zeros((1, size), F32)
    for g in range(heads):
        q_pre = qkv[:, g * size : (g + 1) * size]
        inverse_q = inverse_rms(q_pre)
        query = rope(q_pre * inverse_q * gain_q, cosines, sines).astype(BF16)
        logits = against(query, key) * scale + bias
        scaled = jnp.exp(logits - jnp.max(logits, axis=-1, keepdims=True))
        probs = scaled / jnp.sum(scaled, axis=-1, keepdims=True)
        d_head = d_heads[:, g * size : (g + 1) * size]
        d_probs = against(d_head, value)
        d_scores = probs * (d_probs - jnp.sum(probs * d_probs, axis=-1, keepdims=True))
        d_scores = d_scores.astype(BF16)
        d_query = rope_back(matmul(d_scores, key) * scale, cosines, sines)
        d_key = d_key + outer(d_scores, query)
        d_value = d_value + outer(probs.astype(BF16), d_head)
        sum_q = sum_q + jnp.sum(d_query * q_pre * inverse_q, axis=0, keepdims=True)
        d_qkv[:, g * size : (g + 1) * size] = norm_back(d_query, q_pre, inverse_q, gain_q).astype(
            BF16
        )
    d_key = rope_back(d_key * scale, cosines, sines)
    sum_k = jnp.sum(d_key * k_pre * inverse_k, axis=0, keepdims=True)
    d_qkv[:, heads * size : (heads + 1) * size] = norm_back(d_key, k_pre, inverse_k, gain_k).astype(
        BF16
    )
    d_qkv[:, (heads + 1) * size :] = d_value.astype(BF16)
    grads = d_qkv[...]
    put(d_qkv_ref, grads)
    part = against(grads, chunks(w_ref, width))
    x = flat(x_ref).astype(F32)
    sum_x_ref[0:1, :] += jnp.sum(part * (x * inverse_rms(x)), axis=0, keepdims=True)
    sum_q_ref[0:1, :] += sum_q
    sum_k_ref[0:1, :] += sum_k

    @pl.when(step < 2)
    def _():
        put(theirs_ref, part)

    @pl.when(step >= 2)
    def _():
        put(mine_ref, part)


def attend_call(kernel, operands, extra, outputs, scratch, shape, name, cost):
    ring, micro, row_count, width = shape

    def rows_spec(last):
        return pl.BlockSpec(
            (1, ring, 1, row_count, last), lambda b: (1 - b // 2, 0, b % 2, 0, 0)
        )

    def whole(v):
        return pl.BlockSpec(v.shape, lambda b: (0,) * v.ndim)

    def slot_spec(v, kind):
        block = (1, ring, 1, row_count, v.shape[-1])
        if kind == "theirs":
            return pl.BlockSpec(block, lambda b: (0, 0, jnp.minimum(b, 1), 0, 0))
        return pl.BlockSpec(block, lambda b: (0, 0, jnp.maximum(b - 2, 0), 0, 0))

    in_specs = [
        rows_spec(v.shape[-1])
        if kind == "rows"
        else slot_spec(v, kind)
        if kind in ("theirs", "mine")
        else pl.BlockSpec((1,) + v.shape[1:], lambda b: ((1 - b // 2) * micro + b % 2, 0, 0))
        if kind == "bias"
        else pl.BlockSpec(memory_space=pl.ANY)
        if kind == "token"
        else whole(v)
        for v, kind in zip(operands, extra)
    ]
    out_shape, out_specs = [], []
    for kind, last, dtype in outputs:
        if kind == "rows":
            out_shape.append(jax.ShapeDtypeStruct((2, ring, micro, row_count, last), dtype))
            out_specs.append(rows_spec(last))
        elif kind == "parts":
            one = jax.ShapeDtypeStruct((1, ring, micro, row_count, last), dtype)
            out_shape += [one, one]
            block = (1, ring, 1, row_count, last)
            out_specs.append(pl.BlockSpec(block, lambda b: (0, 0, jnp.minimum(b, 1), 0, 0)))
            out_specs.append(pl.BlockSpec(block, lambda b: (0, 0, jnp.maximum(b - 2, 0), 0, 0)))
        else:
            out_shape.append(jax.ShapeDtypeStruct((8, last), dtype))
            out_specs.append(pl.BlockSpec((8, last), lambda b: (0, 0)))
    return pl.pallas_call(
        kernel,
        grid=(2 * micro,),
        in_specs=in_specs,
        out_specs=out_specs,
        out_shape=out_shape,
        scratch_shapes=scratch,
        compiler_params=pltpu.CompilerParams(vmem_limit_bytes=VMEM),
        cost_estimate=cost,
        name=name,
    )(*operands)


def experts_kernel(
    part, h2_ref, dy_ref, w_ref, spread_ref, dg_ref, du_ref, hid_ref, theirs_ref, mine_ref, acc
):
    chunk, block = pl.program_id(0), pl.program_id(1)
    width = h2_ref.shape[1]
    count = w_ref.shape[0] * part
    gate_w = w_ref[:, :part].reshape(count, width)
    up_w = w_ref[:, part : 2 * part].reshape(count, width)
    down_w = w_ref[:, 2 * part :].reshape(count, width)
    h2 = h2_ref[...]
    mix = matmul(dy_ref[:, width:], spread_ref[...])
    gate = against(h2, gate_w)
    up = against(h2, up_w)
    d_hidden = against(dy_ref[:, :width], down_w) * mix
    sigma = jax.nn.sigmoid(gate)
    silu = gate * sigma
    hid_ref[...] = (silu * up * mix).astype(BF16)
    d_gate = (d_hidden * up * sigma * (1.0 + gate * (1.0 - sigma))).astype(BF16)
    d_up = (d_hidden * silu).astype(BF16)
    dg_ref[...] = d_gate
    du_ref[...] = d_up
    total = matmul(d_gate, gate_w) + matmul(d_up, up_w)

    @pl.when(chunk == 0)
    def _():
        acc[block] = total

    @pl.when((chunk == 1) & (block < 2))
    def _():
        theirs_ref[...] = (acc[block] + total).astype(BF16)

    @pl.when((chunk == 1) & (block >= 2))
    def _():
        mine_ref[...] = (acc[block] + total).astype(BF16)


def experts_call(h2, dy, weights, spread, part):
    rows, width = h2.shape
    owners, depth, _ = weights.shape
    hidden = owners * part
    n, blocks = 2, 4
    step, wide = rows // blocks, hidden // n
    half = jax.ShapeDtypeStruct((rows // 2, width), BF16)
    wide_shape = jax.ShapeDtypeStruct((rows, hidden), BF16)

    def row(c, b):
        return (b + blocks // 2) % blocks

    wide_spec = pl.BlockSpec((step, wide), lambda c, b: (row(c, b), c))
    return pl.pallas_call(
        functools.partial(experts_kernel, part),
        grid=(n, blocks),
        in_specs=[
            pl.BlockSpec((step, width), lambda c, b: (row(c, b), 0)),
            pl.BlockSpec((step, dy.shape[1]), lambda c, b: (row(c, b), 0)),
            pl.BlockSpec((owners // n, depth, width), lambda c, b: (c, 0, 0)),
            pl.BlockSpec((spread.shape[0], wide), lambda c, b: (0, c)),
        ],
        out_specs=[
            wide_spec,
            wide_spec,
            wide_spec,
            pl.BlockSpec((step, width), lambda c, b: (c * jnp.minimum(b, 1), 0)),
            pl.BlockSpec((step, width), lambda c, b: (c * jnp.maximum(b - 2, 0), 0)),
        ],
        out_shape=[wide_shape, wide_shape, wide_shape, half, half],
        scratch_shapes=[pltpu.VMEM((blocks, step, width), F32)],
        compiler_params=pltpu.CompilerParams(vmem_limit_bytes=VMEM),
        cost_estimate=TINY,
        name="experts_rows",
    )(h2, dy, weights, spread)


def expert_grads_kernel(
    part, dg_ref, du_ref, hid_ref, h2_ref, dy_ref, out_ref, token_ref
):
    width = h2_ref.shape[1]
    group = out_ref.shape[0]
    h2 = h2_ref[...]
    out_ref[:, :part] = outer(dg_ref[...], h2).astype(BF16).reshape(group, part, width)
    out_ref[:, part : 2 * part] = outer(du_ref[...], h2).astype(BF16).reshape(group, part, width)
    out_ref[:, 2 * part :] = (
        outer(hid_ref[...], dy_ref[:, :width]).astype(BF16).reshape(group, part, width)
    )
    token_ref[...] = jnp.zeros_like(token_ref)


def expert_grads_call(d_gate, d_up, hidden, h2, dy, owners, part):
    rows, width = h2.shape
    n = 4
    wide = d_gate.shape[1] // n
    wide_spec = pl.BlockSpec((rows, wide), lambda c: (0, c))
    return pl.pallas_call(
        functools.partial(expert_grads_kernel, part),
        grid=(n,),
        in_specs=[
            wide_spec,
            wide_spec,
            wide_spec,
            pl.BlockSpec((rows, width), lambda c: (0, 0)),
            pl.BlockSpec((rows, dy.shape[1]), lambda c: (0, 0)),
        ],
        out_specs=[
            pl.BlockSpec((owners // n, 3 * part, width), lambda c: (c, 0, 0)),
            pl.BlockSpec((8, 128), lambda c: (0, 0)),
        ],
        out_shape=[
            jax.ShapeDtypeStruct((owners, 3 * part, width), BF16),
            jax.ShapeDtypeStruct((8, 128), F32),
        ],
        compiler_params=pltpu.CompilerParams(vmem_limit_bytes=VMEM),
        cost_estimate=TINY,
        name="experts_weights",
    )(d_gate, d_up, hidden, h2, dy)


def add_placed_kernel(where_ref, theirs_ref, mine_ref, token_ref, out_ref):
    ring = mine_ref.shape[0]
    for k in range(ring):
        out_ref[lax.rem(where_ref[0] + k, ring)] = (
            theirs_ref[k].astype(F32) + mine_ref[k].astype(F32)
        ).astype(BF16)


def add_placed_call(where, theirs, mine, token):
    vmem = pl.BlockSpec(memory_space=pltpu.VMEM)
    return pl.pallas_call(
        add_placed_kernel,
        grid_spec=pltpu.PrefetchScalarGridSpec(
            num_scalar_prefetch=1,
            grid=(),
            in_specs=[vmem, vmem, pl.BlockSpec(memory_space=pl.ANY)],
            out_specs=vmem,
        ),
        out_shape=jax.ShapeDtypeStruct(mine.shape, BF16),
        compiler_params=pltpu.CompilerParams(vmem_limit_bytes=VMEM),
        cost_estimate=TINY,
        name="add_cores_placed",
    )(where, theirs, mine, token)


def exchange_sum(pieces, token=None):
    got = lax.all_to_all(pieces, "context", split_axis=0, concat_axis=0, tiled=True)
    if token is not None:
        got = after_call(got, token)
    return jnp.sum(got.astype(F32), axis=0)


def add_kernel(theirs_ref, mine_ref, token_ref, *out_refs):
    for k, out_ref in enumerate(out_refs):
        out_ref[...] = (theirs_ref[k].astype(F32) + mine_ref[k].astype(F32)).astype(BF16)


def add_call(theirs, mine, token):
    shape = theirs.shape
    one = jax.ShapeDtypeStruct(shape[1:], BF16)
    vmem = pl.BlockSpec(memory_space=pltpu.VMEM)
    return pl.pallas_call(
        add_kernel,
        in_specs=[vmem, vmem, pl.BlockSpec(memory_space=pl.ANY)],
        out_specs=[vmem] * shape[0],
        out_shape=[one] * shape[0],
        compiler_params=pltpu.CompilerParams(vmem_limit_bytes=VMEM),
        cost_estimate=TINY,
        name="add_cores",
    )(theirs, mine, token)


def gate_up_down_kernel(part, in_ref, gate_ref, up_ref, down_ref):
    last = in_ref.shape[2]
    count = in_ref.shape[0] * part
    gate_ref[...] = in_ref[:, :part].reshape(count, last).astype(F32).T
    up_ref[...] = in_ref[:, part : 2 * part].reshape(count, last).astype(F32).T
    down_ref[...] = in_ref[:, 2 * part :].reshape(count, last).astype(F32)


def gate_up_down_call(gathered, part):
    members, depth, width = gathered.shape
    ff = members * part
    n = 8
    step = width // n
    return pl.pallas_call(
        functools.partial(gate_up_down_kernel, part),
        grid=(n,),
        in_specs=[pl.BlockSpec((members, depth, step), lambda c: (0, 0, c))],
        out_specs=[
            pl.BlockSpec((step, ff), lambda c: (c, 0)),
            pl.BlockSpec((step, ff), lambda c: (c, 0)),
            pl.BlockSpec((ff, step), lambda c: (0, c)),
        ],
        out_shape=[
            jax.ShapeDtypeStruct((width, ff), F32),
            jax.ShapeDtypeStruct((width, ff), F32),
            jax.ShapeDtypeStruct((ff, width), F32),
        ],
        compiler_params=pltpu.CompilerParams(vmem_limit_bytes=VMEM),
        cost_estimate=TINY,
        name="experts_results",
    )(gathered)


def out_grads_kernel(heads_ref, mine_ref, theirs_ref, out_ref):
    total = outer(heads_ref[0], mine_ref[...]) + outer(heads_ref[1], theirs_ref[...])
    out_ref[...] = total.astype(BF16)


def out_grads_call(heads_out, mine, theirs):
    _, half, columns = heads_out.shape
    width = mine.shape[1]
    n = 4
    spec = pl.BlockSpec((half, width // n), lambda c: (0, c))
    return pl.pallas_call(
        out_grads_kernel,
        grid=(n,),
        in_specs=[pl.BlockSpec(heads_out.shape, lambda c: (0, 0, 0)), spec, spec],
        out_specs=pl.BlockSpec((columns, width // n), lambda c: (0, c)),
        out_shape=jax.ShapeDtypeStruct((columns, width), BF16),
        compiler_params=pltpu.CompilerParams(vmem_limit_bytes=VMEM),
        cost_estimate=TINY,
        name="out_weights",
    )(heads_out, mine, theirs)


def attend_grads_kernel(
    cut, place_ref, h1_ref, d_qkv_ref, out_ref, gains_ref, token_ref, *refs
):
    firsts, seconds, share = refs[:SIDE], refs[SIDE : 2 * SIDE], refs[-1]
    step = pl.program_id(0)
    last = d_qkv_ref.shape[1]
    depth = share.shape[1] - 16
    grad = outer(h1_ref[...], d_qkv_ref[...]).astype(BF16)
    share[:, :depth, :last] = grad.reshape(SIDE, depth, last)
    rows, columns = out_ref.shape[1], share.shape[2] - last
    for k in range(depth // rows):
        share[:, k * rows : (k + 1) * rows, last:] = out_ref[:, :, k * columns : (k + 1) * columns]
    share[:, depth:] = gains_ref[...]
    for k in range(SIDE):

        @pl.when(step == k)
        def _():
            firsts[k][...] = share[:, :cut]

        seconds[k][0] = share[lax.rem(place_ref[1] + k, SIDE), cut:]


def attend_grads_call(place, h1, d_qkv, grad_out, gains, token, cut):
    rows, width = h1.shape
    owners, extra, columns = gains.shape
    depth = width // owners
    last = d_qkv.shape[1]

    def at(i, place):
        return lax.rem(place[0] + i, SIDE)

    first = jax.ShapeDtypeStruct((SIDE, cut, columns), BF16)
    second = jax.ShapeDtypeStruct((SIDE, depth + extra - cut, columns), BF16)
    outs = pl.pallas_call(
        functools.partial(attend_grads_kernel, cut),
        grid_spec=pltpu.PrefetchScalarGridSpec(
            num_scalar_prefetch=1,
            grid=(SIDE,),
            in_specs=[
                pl.BlockSpec((rows, width // SIDE), lambda i, place: (0, at(i, place))),
                pl.BlockSpec((rows, last), lambda i, place: (0, 0)),
                pl.BlockSpec((SIDE,) + grad_out.shape[1:], lambda i, place: (at(i, place), 0, 0)),
                pl.BlockSpec((SIDE, extra, columns), lambda i, place: (at(i, place), 0, 0)),
                pl.BlockSpec(memory_space=pl.ANY),
            ],
            out_specs=[pl.BlockSpec(first.shape, lambda i, place: (0, 0, 0))] * SIDE
            + [pl.BlockSpec((1,) + second.shape[1:], lambda i, place: (i, 0, 0))] * SIDE,
            scratch_shapes=[pltpu.VMEM((SIDE, depth + extra, columns), BF16)],
        ),
        out_shape=[first] * SIDE + [second] * SIDE,
        compiler_params=pltpu.CompilerParams(vmem_limit_bytes=VMEM),
        cost_estimate=TINY,
        name="attention_weights",
    )(place, h1, d_qkv, grad_out, gains, token)
    return outs[:SIDE], outs[SIDE:]


def total_of(refs):
    total = refs[0][...].astype(F32)
    for ref in refs[1:]:
        total = total + ref[...].astype(F32)
    return total.astype(BF16)


def half_sum_kernel(place_ref, *refs):
    outs, total = refs[2 * SIDE + 1 : -1], refs[-1]
    firsts, seconds = outs[:SIDE], outs[SIDE:]
    total[...] = total_of(refs[:SIDE])
    other = total_of(refs[SIDE : 2 * SIDE])
    for k in range(SIDE):
        firsts[k][...] = total[lax.rem(place_ref[1] + k, SIDE)]
        seconds[k][...] = other[k]


def half_sum_call(place, firsts, seconds, token):
    vmem = pl.BlockSpec(memory_space=pltpu.VMEM)
    outs = pl.pallas_call(
        half_sum_kernel,
        grid_spec=pltpu.PrefetchScalarGridSpec(
            num_scalar_prefetch=1,
            grid=(),
            in_specs=[vmem] * (2 * SIDE) + [pl.BlockSpec(memory_space=pl.ANY)],
            out_specs=[vmem] * (2 * SIDE),
            scratch_shapes=[pltpu.VMEM(firsts[0].shape, BF16)],
        ),
        out_shape=[jax.ShapeDtypeStruct(v.shape[1:], BF16) for v in (*firsts, *seconds)],
        compiler_params=pltpu.CompilerParams(vmem_limit_bytes=VMEM),
        cost_estimate=TINY,
        name="half_sum",
    )(place, *firsts, *seconds, token)
    return outs[:SIDE], outs[SIDE:]


def last_sum_kernel(token_ref, *refs):
    out = refs[-1]
    cut = refs[0].shape[0]
    out[:cut] = total_of(refs[:SIDE])
    out[cut:] = total_of(refs[SIDE : 2 * SIDE])


def last_sum_call(firsts, seconds, token):
    rows, columns = firsts[0].shape[0] + seconds[0].shape[0], firsts[0].shape[1]
    vmem = pl.BlockSpec(memory_space=pltpu.VMEM)
    return pl.pallas_call(
        last_sum_kernel,
        in_specs=[pl.BlockSpec(memory_space=pl.ANY)] + [vmem] * (2 * SIDE),
        out_specs=vmem,
        out_shape=jax.ShapeDtypeStruct((rows, columns), BF16),
        compiler_params=pltpu.CompilerParams(vmem_limit_bytes=VMEM),
        cost_estimate=TINY,
        name="last_sum",
    )(token, *firsts, *seconds)


def plane_send(pieces, dx, dz):
    return [pieces[0]] + [plane(pieces[k], -k * dx, -k * dz) for k in range(1, SIDE)]


def columns_kernel(heads_width, size, where_ref, mine_ref, theirs_ref, q_ref, k_ref, v_ref, sum_ref):
    depth = q_ref.shape[0]
    mine, theirs = mine_ref[0].astype(F32), theirs_ref[0].astype(F32)
    first = where_ref[1] == 0
    q_ref[:, :heads_width] = jnp.where(first, mine[:depth, :heads_width], theirs[:depth, :heads_width])
    q_ref[:, heads_width:] = jnp.where(first, theirs[:depth, :heads_width], mine[:depth, :heads_width])
    both = mine + theirs
    k_ref[...] = both[:depth, heads_width : heads_width + size]
    v_ref[...] = both[:depth, heads_width + size :]

    @pl.when(pl.program_id(0) == 0)
    def _():
        sum_ref[...] = jnp.zeros_like(sum_ref)

    sum_ref[...] += both[depth:]


def columns_call(where, mine, theirs, depth, heads_width, size):
    ring, rows, last = mine.shape
    cores = 2

    def at(k, where):
        return (0, lax.rem(where[0] + k, ring))

    return pl.pallas_call(
        functools.partial(columns_kernel, heads_width, size),
        grid_spec=pltpu.PrefetchScalarGridSpec(
            num_scalar_prefetch=1,
            grid=(ring,),
            in_specs=[pl.BlockSpec((1, rows, last), lambda k, where: (k, 0, 0))] * 2,
            out_specs=[
                pl.BlockSpec((depth, cores * heads_width), at),
                pl.BlockSpec((depth, size), at),
                pl.BlockSpec((depth, size), at),
                pl.BlockSpec((rows - depth, last), lambda k, where: (0, 0)),
            ],
        ),
        out_shape=[
            jax.ShapeDtypeStruct((depth, ring * cores * heads_width), F32),
            jax.ShapeDtypeStruct((depth, ring * size), F32),
            jax.ShapeDtypeStruct((depth, ring * size), F32),
            jax.ShapeDtypeStruct((rows - depth, last), F32),
        ],
        compiler_params=pltpu.CompilerParams(vmem_limit_bytes=VMEM),
        cost_estimate=TINY,
        name="columns_results",
    )(where, mine, theirs)


def rows_kernel(where_ref, mine_ref, theirs_ref, out_ref):
    count = mine_ref.shape[1]
    mine, theirs = mine_ref[0].astype(F32), theirs_ref[0].astype(F32)
    first = where_ref[1] == 0
    out_ref[:count] = jnp.where(first, mine, theirs)
    out_ref[count:] = jnp.where(first, theirs, mine)


def rows_call(where, mine, theirs):
    ring, count, width = mine.shape
    cores = 2
    return pl.pallas_call(
        rows_kernel,
        grid_spec=pltpu.PrefetchScalarGridSpec(
            num_scalar_prefetch=1,
            grid=(ring,),
            in_specs=[pl.BlockSpec((1, count, width), lambda k, where: (k, 0, 0))] * 2,
            out_specs=pl.BlockSpec(
                (cores * count, width), lambda k, where: (lax.rem(where[0] + k, ring), 0)
            ),
        ),
        out_shape=jax.ShapeDtypeStruct((ring * cores * count, width), F32),
        compiler_params=pltpu.CompilerParams(vmem_limit_bytes=VMEM),
        cost_estimate=TINY,
        name="rows_results",
    )(where, mine, theirs)


def expert_out_kernel(part, hid_ref, w_ref, token_ref, theirs_ref, mine_ref):
    width = w_ref.shape[2]
    block = pl.program_id(0)
    total = matmul(hid_ref[...], w_ref[...].reshape(w_ref.shape[0] * part, width)).astype(BF16)

    @pl.when(block < 2)
    def _():
        theirs_ref[...] = total

    @pl.when(block >= 2)
    def _():
        mine_ref[...] = total


def expert_out_call(hidden, weights, token, part):
    rows, wide = hidden.shape
    owners, _, width = weights.shape
    blocks = 4
    step = rows // blocks
    half = jax.ShapeDtypeStruct((rows // 2, width), BF16)
    return pl.pallas_call(
        functools.partial(expert_out_kernel, part),
        grid=(blocks,),
        in_specs=[
            pl.BlockSpec((step, wide), lambda b: ((b + blocks // 2) % blocks, 0)),
            pl.BlockSpec((owners, part, width), lambda b: (0, 2, 0)),
            pl.BlockSpec(memory_space=pl.ANY),
        ],
        out_specs=[
            pl.BlockSpec((step, width), lambda b: (jnp.minimum(b, 1), 0)),
            pl.BlockSpec((step, width), lambda b: (jnp.maximum(b - 2, 0), 0)),
        ],
        out_shape=[half, half],
        compiler_params=pltpu.CompilerParams(vmem_limit_bytes=VMEM),
        cost_estimate=pl.CostEstimate(
            flops=2 * rows * wide * width, bytes_accessed=20_000_000, transcendentals=0
        ),
        name="experts_out",
    )(hidden, weights, token)


def local(
    tokens,
    lengths,
    routes,
    mix_weights,
    cotangent,
    w_query,
    key_weight,
    value_weight,
    w_out,
    norm_attn,
    norm_moe,
    norm_query,
    norm_key,
    w_gate,
    w_up,
    w_down,
):
    owners = lax.axis_size("experts")
    ring = lax.axis_size("context")
    cores = lax.axis_size("dp")
    members = ring * cores
    y = lax.axis_index("context")
    d = lax.axis_index("dp")
    j = y * cores + d
    micro, _, row_count, width = tokens.shape
    head = norm_query.shape[0] * owners
    q_width = w_query.shape[1] // members
    q_heads = q_width // head
    depth = w_query.shape[0]
    ff = w_gate.shape[2]
    ff_part = ff // members
    out_rows = w_out.shape[0]
    out_part = out_rows // members
    seqs = cores * micro
    span = ring * row_count
    rows = seqs * span
    scale = head ** (-0.5)

    forth = [
        (es * members + k, ((es % cores) * members + k) * members + es // cores)
        for es in range(owners)
        for k in range(members)
    ]
    back = [(b, a) for a, b in forth]
    out_chunk = lax.ppermute(
        lax.dynamic_slice_in_dim(w_out, j * out_part, out_part, axis=0), EVERY, forth
    )
    expert_pack = jnp.concatenate(
        [
            lax.dynamic_slice_in_dim(w_gate[0], j * ff_part, ff_part, axis=1).T,
            lax.dynamic_slice_in_dim(w_up[0], j * ff_part, ff_part, axis=1).T,
            lax.dynamic_slice_in_dim(w_down[0], j * ff_part, ff_part, axis=0),
        ],
        axis=0,
    )
    gains = jnp.concatenate([norm_attn, norm_moe, norm_query, norm_key])
    packed = jnp.concatenate(
        [
            lax.dynamic_slice_in_dim(w_query, j * q_width, q_width, axis=1),
            lax.dynamic_slice_in_dim(key_weight, y * head, head, axis=1),
            lax.dynamic_slice_in_dim(value_weight, y * head, head, axis=1),
            jnp.concatenate(jnp.split(out_chunk, depth // out_part, axis=1), axis=0),
        ],
        axis=1,
    )
    qkv_width = q_width + 2 * head
    gain_rows = jnp.pad(gains[None], ((0, 15), (0, packed.shape[1] - gains.shape[0])))
    shared = lax.all_gather(
        jnp.concatenate([packed, gain_rows]), "experts", axis=0, tiled=False
    )
    expert_all = lax.all_gather(expert_pack, "experts", axis=0, tiled=False)
    gain_row = shared[:, depth]
    gain_row = gain_row.astype(F32)
    gain_attn = gain_row[:, :depth].reshape(-1)
    gain_moe = gain_row[:, depth : 2 * depth].reshape(-1)
    eighth = norm_query.shape[0]
    gain_query = gain_row[:, 2 * depth : 2 * depth + eighth].reshape(-1)
    gain_key = gain_row[:, 2 * depth + eighth : 2 * depth + 2 * eighth].reshape(-1)
    hidden_width = owners * ff_part

    where = jnp.stack([y, d]).astype(jnp.int32)
    x_own = tokens[:, 0]
    x_rows = gather_rows(x_own, ring)
    len_all = jnp.stack([lengths[:, 0], swap(lengths[:, 0])]).reshape(seqs)
    own_pos = y * row_count + jnp.arange(row_count, dtype=jnp.int32)
    valid = (own_pos[None, :] < lengths[:, 0][:, None]).astype(F32)
    dy_own = (cotangent[:, 0].astype(F32) * valid[:, :, None]).astype(BF16)
    ids = jnp.arange(owners, dtype=jnp.int32)
    mix_own = jnp.sum(
        jnp.where(routes[:, 0][..., None] == ids, mix_weights[:, 0][..., None], 0.0), axis=2
    )
    mix_high = mix_own.astype(BF16)
    mix_low = (mix_own - mix_high.astype(F32)).astype(BF16)
    lanes = 128
    mix_pad = jnp.zeros((micro, row_count, lanes - 2 * owners), BF16)
    dy_mix = gather_rows(jnp.concatenate([dy_own, mix_high, mix_low, mix_pad], axis=-1), ring)
    dy_mix = dy_mix.reshape(rows, width + lanes)
    lane = jnp.arange(lanes, dtype=jnp.int32)
    spread = (
        (jnp.arange(hidden_width, dtype=jnp.int32)[None, :] // ff_part == (lane % owners)[:, None])
        & (lane < 2 * owners)[:, None]
    ).astype(BF16)

    k_index = jnp.arange(span, dtype=jnp.int32)
    pos = ((y + k_index // row_count) % ring) * row_count + k_index % row_count
    frequency = ROPE_BASE ** (-jnp.arange(head // 2, dtype=F32) * 2.0 / head)
    phase = pos.astype(F32)[:, None] * frequency[None, :]
    cosines, sines = jnp.cos(phase), jnp.sin(phase)
    cosines = jnp.concatenate([cosines, cosines], axis=1)
    sines = jnp.concatenate([-sines, sines], axis=1)
    allowed = (pos[None, None, :] <= pos[None, :, None]) & (
        pos[None, None, :] < len_all[:, None, None]
    )
    bias = jnp.where(allowed, 0.0, -1e30).astype(F32)

    shape = (ring, micro, row_count, width)
    head_gains = (gain_query[None], gain_key[None])
    h1, qkv, heads_out, theirs, mine = attend_call(
        functools.partial(attend_kernel, q_heads, scale),
        (x_rows, gain_attn[None], shared, cosines, sines, bias, *head_gains, dy_mix),
        ("rows", "", "", "", "", "bias", "", "", "token"),
        (
            ("rows", width, BF16),
            ("rows", qkv_width, F32),
            ("rows", q_width, BF16),
            ("parts", width, BF16),
        ),
        [pltpu.VMEM((span, q_width), BF16), pltpu.VMEM((span, width), BF16)],
        shape,
        "attention",
        TINY,
    )
    attn_own = scatter_rows(theirs[0], mine[0])
    x1 = x_own.astype(F32) + attn_own
    inverse_mid = inverse_rms(x1)
    h2 = gather_rows((x1 * inverse_mid * gain_moe).astype(BF16), ring).reshape(rows, width)

    d_gate, d_up, hidden, theirs, mine = experts_call(h2, dy_mix, expert_all, spread, ff_part)
    grad_experts, token = expert_grads_call(
        d_gate, d_up, hidden, h2, dy_mix, owners, ff_part
    )
    pieces = add_call(swap(theirs.reshape(shape)), mine.reshape(shape), token)
    d_h2 = ring_sum(pieces)
    moe_theirs, moe_mine = expert_out_call(hidden, expert_all, token, ff_part)

    grad_gain_moe = jnp.sum(d_h2 * x1 * inverse_mid, axis=(0, 1))
    d_x1 = dy_own.astype(F32) + norm_back(d_h2, x1, inverse_mid, gain_moe)
    grad_experts = lax.psum_scatter(
        grad_experts, "experts", scatter_dimension=0, tiled=False
    )
    moe_pieces = add_placed_call(
        where, swap(moe_theirs.reshape(shape)), moe_mine.reshape(shape), hidden
    )
    d_mine = after_call(ring_stack(d_x1.astype(BF16), ring), moe_pieces)
    d_theirs = swap(d_mine)
    grad_out = out_grads_call(
        heads_out.reshape(2, rows // 2, q_width),
        d_mine.reshape(-1, width),
        d_theirs.reshape(-1, width),
    )
    grad_out = grad_out.reshape(owners, out_part, width)
    d_qkv, theirs, mine, sum_q, sum_k, sum_x = attend_call(
        functools.partial(attend_back_kernel, q_heads, scale),
        (
            d_theirs[None],
            d_mine[None],
            x_rows,
            gain_attn[None],
            shared,
            cosines,
            sines,
            bias,
            *head_gains,
            qkv,
            moe_pieces,
            grad_out,
        ),
        (
            "theirs",
            "mine",
            "rows",
            "",
            "",
            "",
            "",
            "bias",
            "",
            "",
            "rows",
            "token",
            "token",
        ),
        (
            ("rows", qkv_width, BF16),
            ("parts", width, BF16),
            ("sum", head, F32),
            ("sum", head, F32),
            ("sum", width, F32),
        ),
        [pltpu.VMEM((span, qkv_width), BF16)],
        shape,
        "attention_back",
        pl.CostEstimate(flops=9_000_000_000, bytes_accessed=90_000_000, transcendentals=0),
    )
    output = (x1 + exchange_sum(moe_pieces, d_qkv)).astype(BF16)[:, None]
    grad_gain_query, grad_gain_key, grad_gain_attn = sum_q[0], sum_k[0], sum_x[0]
    h1, d_qkv = h1.reshape(rows, width), d_qkv.reshape(rows, qkv_width)

    grad_gains = jnp.concatenate(
        [
            grad_gain_attn.reshape(owners, depth),
            grad_gain_moe.reshape(owners, depth),
            grad_gain_query.reshape(owners, eighth),
            grad_gain_key.reshape(owners, eighth),
        ],
        axis=1,
    ).astype(BF16)
    grad_gains = jnp.pad(
        grad_gains[:, None], ((0, 0), (0, 15), (0, shared.shape[2] - grad_gains.shape[1]))
    )
    index = lax.axis_index("experts")
    place = jnp.stack([index // SIDE, index % SIDE]).astype(jnp.int32)
    firsts, seconds = attend_grads_call(
        place, h1, d_qkv, grad_out, grad_gains, output, depth // 2 + 16
    )
    d_h1 = exchange_sum(add_placed_call(where, swap(theirs[0]), mine[0], firsts[1]))
    x_f32 = x_own.astype(F32)
    input_grad = (d_x1 + norm_back(d_h1, x_f32, inverse_rms(x_f32), gain_attn))[:, None]
    grad_experts = after_call(grad_experts, firsts[1])
    all_experts = lax.all_gather(grad_experts, GROUP, axis=0, tiled=False)
    firsts, seconds = plane_send(firsts, 1, 0), plane_send(seconds, 0, 1)
    firsts, seconds = half_sum_call(place, firsts, seconds, grad_out)
    grads = last_sum_call(plane_send(firsts, 0, 1), plane_send(seconds, 1, 0), d_h1)
    result_gate, result_up, result_down = gate_up_down_call(all_experts, ff_part)
    out_sum = jnp.concatenate(
        [grads[k * out_part : (k + 1) * out_part, qkv_width:] for k in range(depth // out_part)],
        axis=1,
    )
    result_q, result_k, result_v, gain_sum = columns_call(
        where, *gather_members(grads[:, :qkv_width]), depth, q_width, head
    )
    out_sum = after_call(lax.ppermute(out_sum, EVERY, back), result_down)
    result_out = rows_call(where, *gather_members(out_sum))
    gain_sum = gain_sum[0]
    return (
        output,
        input_grad,
        result_q,
        result_k,
        result_v,
        result_out,
        gain_sum[:depth],
        gain_sum[depth : 2 * depth],
        gain_sum[2 * depth : 2 * depth + eighth],
        gain_sum[2 * depth + eighth : 2 * depth + 2 * eighth],
        result_gate[None],
        result_up[None],
        result_down[None],
    )


def solution(mesh):
    rows = P(None, ("experts", "dp"), "context", None)
    in_specs = (
        rows,
        P(None, ("experts", "dp")),
        rows,
        rows,
        rows,
        P("experts", None),
        P("experts", None),
        P("experts", None),
        P("experts", None),
        P("experts"),
        P("experts"),
        P("experts"),
        P("experts"),
        P("experts", None, None),
        P("experts", None, None),
        P("experts", None, None),
    )
    out_specs = (
        rows,
        rows,
        P("experts", None),
        P("experts", None),
        P("experts", None),
        P("experts", None),
        P("experts"),
        P("experts"),
        P("experts"),
        P("experts"),
        P("experts", None, None),
        P("experts", None, None),
        P("experts", None, None),
    )
    return jax.shard_map(local, mesh=mesh, in_specs=in_specs, out_specs=out_specs, check_vma=False)
```

```python
import functools

import jax
import jax.numpy as jnp
from jax import lax
from jax.experimental import pallas as pl
from jax.experimental.pallas import tpu as pltpu
from jax.sharding import PartitionSpec as P

EPS = 1e-06
ROPE_BASE = 1000000.0
F32 = jnp.float32
BF16 = jnp.bfloat16
GROUP = ("context", "dp")
EVERY = ("experts", "context", "dp")
VMEM = 60 * 1024 * 1024
SIDE = 4
TINY = pl.CostEstimate(flops=0, bytes_accessed=1000, transcendentals=0)


def inverse_rms(v):
    return lax.rsqrt(jnp.mean(v * v, axis=-1, keepdims=True) + EPS)


def norm_back(grad_in, v, inverse, gain):
    scaled = grad_in * gain
    return inverse * scaled - v * inverse**3 * jnp.mean(scaled * v, axis=-1, keepdims=True)


def matmul(left, right):
    return jnp.dot(left, right, preferred_element_type=F32)


def against(left, right):
    return lax.dot_general(left, right, (((1,), (1,)), ((), ())), preferred_element_type=F32)


def outer(left, right):
    return lax.dot_general(left, right, (((0,), (0,)), ((), ())), preferred_element_type=F32)


def swap(v):
    return lax.ppermute(v, "dp", [(0, 1), (1, 0)])


def ring_stack(own, ring):
    pieces = [own]
    for k in range(1, ring):
        pieces.append(lax.ppermute(own, "context", [((i + k) % ring, i) for i in range(ring)]))
    return jnp.stack(pieces)


def gather_rows(own, ring):
    mine = ring_stack(own, ring)
    return jnp.stack([mine, swap(mine)])


def ring_sum(pieces):
    ring = len(pieces)
    total = pieces[0].astype(F32)
    for k in range(1, ring):
        got = lax.ppermute(pieces[k], "context", [(i, (i + k) % ring) for i in range(ring)])
        total = total + got.astype(F32)
    return total


def add_cores(theirs, mine):
    other = swap(theirs)
    return [
        (mine[k].astype(F32) + other[k].astype(F32)).astype(BF16) for k in range(mine.shape[0])
    ]


def scatter_rows(theirs, mine):
    return ring_sum(add_cores(theirs, mine))


def gather_members(v):
    ring = lax.axis_size("context")
    pieces = [v]
    for k in range(1, ring):
        pieces.append(lax.ppermute(v, "context", [((i + k) % ring, i) for i in range(ring)]))
    mine = jnp.stack(pieces)
    return mine, swap(mine)


def plane(v, dx, dz):
    moves = [
        (((i // SIDE + dx) % SIDE) * SIDE + (i % SIDE + dz) % SIDE, i) for i in range(SIDE * SIDE)
    ]
    return lax.ppermute(v, "experts", moves)


def after_kernel(v_ref, *refs):
    pass


def after_call(v, *tokens):
    anywhere = pl.BlockSpec(memory_space=pl.ANY)
    return pl.pallas_call(
        after_kernel,
        in_specs=[anywhere] * (1 + len(tokens)),
        out_specs=anywhere,
        out_shape=jax.ShapeDtypeStruct(v.shape, v.dtype),
        input_output_aliases={0: 0},
        cost_estimate=TINY,
        name="after",
    )(v, *tokens)


def rope(v, cosines, sines):
    return v * cosines + pltpu.roll(v, v.shape[-1] // 2, 1) * sines


def rope_back(v, cosines, sines):
    return v * cosines + pltpu.roll(v * sines, v.shape[-1] // 2, 1)


def flat(ref):
    v = ref[...]
    return v.reshape(v.shape[1] * v.shape[3], v.shape[4])


def chunks(ref, columns):
    v = ref[:, :-16, :columns]
    return v.reshape(v.shape[0] * v.shape[1], columns)


def out_blocks(ref, first):
    last = ref.shape[2] - first
    rows = last // ref.shape[0]
    for k in range((ref.shape[1] - 16) // rows):
        yield k * last, (k + 1) * last, ref[:, k * rows : (k + 1) * rows, first:].reshape(last, last)


def put(ref, v):
    ref[...] = v.reshape(ref.shape).astype(ref.dtype)


def attend_kernel(
    heads,
    scale,
    x_ref,
    gain_ref,
    w_ref,
    cos_ref,
    sin_ref,
    bias_ref,
    gain_q_ref,
    gain_k_ref,
    token_ref,
    h1_ref,
    qkv_ref,
    heads_ref,
    theirs_ref,
    mine_ref,
    heads_out,
    total,
):
    size = cos_ref.shape[1]
    x = flat(x_ref).astype(F32)
    h1 = (x * inverse_rms(x) * gain_ref[...]).astype(BF16)
    put(h1_ref, h1)
    width = (heads + 2) * size
    qkv = matmul(h1, chunks(w_ref, width))
    put(qkv_ref, qkv)
    cosines, sines, bias = cos_ref[...], sin_ref[...], bias_ref[0]
    k_pre = qkv[:, heads * size : (heads + 1) * size]
    key = rope(k_pre * inverse_rms(k_pre) * gain_k_ref[...], cosines, sines).astype(BF16)
    value = qkv[:, (heads + 1) * size :].astype(BF16)
    for g in range(heads):
        q_pre = qkv[:, g * size : (g + 1) * size]
        query = rope(q_pre * inverse_rms(q_pre) * gain_q_ref[...], cosines, sines).astype(BF16)
        logits = against(query, key) * scale + bias
        scaled = jnp.exp(logits - jnp.max(logits, axis=-1, keepdims=True))
        soft = (scaled / jnp.sum(scaled, axis=-1, keepdims=True)).astype(BF16)
        heads_out[:, g * size : (g + 1) * size] = matmul(soft, value).astype(BF16)
    out = heads_out[...]
    put(heads_ref, out)
    for first, last, block in out_blocks(w_ref, width):
        total[:, first:last] = matmul(out, block).astype(BF16)

    @pl.when(pl.program_id(0) < 2)
    def _():
        put(theirs_ref, total[...])

    @pl.when(pl.program_id(0) >= 2)
    def _():
        put(mine_ref, total[...])


def attend_back_kernel(
    heads,
    scale,
    theirs_da_ref,
    mine_da_ref,
    x_ref,
    gain_ref,
    w_ref,
    cos_ref,
    sin_ref,
    bias_ref,
    gain_q_ref,
    gain_k_ref,
    qkv_ref,
    token_ref,
    other_token_ref,
    d_qkv_ref,
    theirs_ref,
    mine_ref,
    sum_q_ref,
    sum_k_ref,
    sum_x_ref,
    d_qkv,
):
    size = cos_ref.shape[1]
    step = pl.program_id(0)

    @pl.when(step == 0)
    def _():
        sum_q_ref[...] = jnp.zeros_like(sum_q_ref)
        sum_k_ref[...] = jnp.zeros_like(sum_k_ref)
        sum_x_ref[...] = jnp.zeros_like(sum_x_ref)

    width = (heads + 2) * size
    da = jnp.where(step < 2, flat(theirs_da_ref), flat(mine_da_ref))
    d_heads = None
    for first, last, block in out_blocks(w_ref, width):
        piece = against(da[:, first:last], block)
        d_heads = piece if d_heads is None else d_heads + piece
    d_heads = d_heads.astype(BF16)
    qkv = flat(qkv_ref)
    cosines, sines, bias = cos_ref[...], sin_ref[...], bias_ref[0]
    gain_q, gain_k = gain_q_ref[...], gain_k_ref[...]
    k_pre = qkv[:, heads * size : (heads + 1) * size]
    inverse_k = inverse_rms(k_pre)
    key = rope(k_pre * inverse_k * gain_k, cosines, sines).astype(BF16)
    value = qkv[:, (heads + 1) * size :].astype(BF16)
    d_key = jnp.zeros(k_pre.shape, F32)
    d_value = jnp.zeros(k_pre.shape, F32)
    sum_q = jnp.zeros((1, size), F32)
    for g in range(heads):
        q_pre = qkv[:, g * size : (g + 1) * size]
        inverse_q = inverse_rms(q_pre)
        query = rope(q_pre * inverse_q * gain_q, cosines, sines).astype(BF16)
        logits = against(query, key) * scale + bias
        scaled = jnp.exp(logits - jnp.max(logits, axis=-1, keepdims=True))
        probs = scaled / jnp.sum(scaled, axis=-1, keepdims=True)
        d_head = d_heads[:, g * size : (g + 1) * size]
        d_probs = against(d_head, value)
        d_scores = probs * (d_probs - jnp.sum(probs * d_probs, axis=-1, keepdims=True))
        d_scores = d_scores.astype(BF16)
        d_query = rope_back(matmul(d_scores, key) * scale, cosines, sines)
        d_key = d_key + outer(d_scores, query)
        d_value = d_value + outer(probs.astype(BF16), d_head)
        sum_q = sum_q + jnp.sum(d_query * q_pre * inverse_q, axis=0, keepdims=True)
        d_qkv[:, g * size : (g + 1) * size] = norm_back(d_query, q_pre, inverse_q, gain_q).astype(
            BF16
        )
    d_key = rope_back(d_key * scale, cosines, sines)
    sum_k = jnp.sum(d_key * k_pre * inverse_k, axis=0, keepdims=True)
    d_qkv[:, heads * size : (heads + 1) * size] = norm_back(d_key, k_pre, inverse_k, gain_k).astype(
        BF16
    )
    d_qkv[:, (heads + 1) * size :] = d_value.astype(BF16)
    grads = d_qkv[...]
    put(d_qkv_ref, grads)
    part = against(grads, chunks(w_ref, width))
    x = flat(x_ref).astype(F32)
    sum_x_ref[0:1, :] += jnp.sum(part * (x * inverse_rms(x)), axis=0, keepdims=True)
    sum_q_ref[0:1, :] += sum_q
    sum_k_ref[0:1, :] += sum_k

    @pl.when(step < 2)
    def _():
        put(theirs_ref, part)

    @pl.when(step >= 2)
    def _():
        put(mine_ref, part)


def attend_call(kernel, operands, extra, outputs, scratch, shape, name, cost):
    ring, micro, row_count, width = shape

    def rows_spec(last):
        return pl.BlockSpec(
            (1, ring, 1, row_count, last), lambda b: (1 - b // 2, 0, b % 2, 0, 0)
        )

    def whole(v):
        return pl.BlockSpec(v.shape, lambda b: (0,) * v.ndim)

    def slot_spec(v, kind):
        block = (1, ring, 1, row_count, v.shape[-1])
        if kind == "theirs":
            return pl.BlockSpec(block, lambda b: (0, 0, jnp.minimum(b, 1), 0, 0))
        return pl.BlockSpec(block, lambda b: (0, 0, jnp.maximum(b - 2, 0), 0, 0))

    in_specs = [
        rows_spec(v.shape[-1])
        if kind == "rows"
        else slot_spec(v, kind)
        if kind in ("theirs", "mine")
        else pl.BlockSpec((1,) + v.shape[1:], lambda b: ((1 - b // 2) * micro + b % 2, 0, 0))
        if kind == "bias"
        else pl.BlockSpec(memory_space=pl.ANY)
        if kind == "token"
        else whole(v)
        for v, kind in zip(operands, extra)
    ]
    out_shape, out_specs = [], []
    for kind, last, dtype in outputs:
        if kind == "rows":
            out_shape.append(jax.ShapeDtypeStruct((2, ring, micro, row_count, last), dtype))
            out_specs.append(rows_spec(last))
        elif kind == "parts":
            one = jax.ShapeDtypeStruct((1, ring, micro, row_count, last), dtype)
            out_shape += [one, one]
            block = (1, ring, 1, row_count, last)
            out_specs.append(pl.BlockSpec(block, lambda b: (0, 0, jnp.minimum(b, 1), 0, 0)))
            out_specs.append(pl.BlockSpec(block, lambda b: (0, 0, jnp.maximum(b - 2, 0), 0, 0)))
        else:
            out_shape.append(jax.ShapeDtypeStruct((8, last), dtype))
            out_specs.append(pl.BlockSpec((8, last), lambda b: (0, 0)))
    return pl.pallas_call(
        kernel,
        grid=(2 * micro,),
        in_specs=in_specs,
        out_specs=out_specs,
        out_shape=out_shape,
        scratch_shapes=scratch,
        compiler_params=pltpu.CompilerParams(vmem_limit_bytes=VMEM),
        cost_estimate=cost,
        name=name,
    )(*operands)


def experts_kernel(
    part, h2_ref, dy_ref, w_ref, spread_ref, dg_ref, du_ref, hid_ref, theirs_ref, mine_ref, acc
):
    chunk, block = pl.program_id(0), pl.program_id(1)
    width = h2_ref.shape[1]
    count = w_ref.shape[0] * part
    gate_w = w_ref[:, :part].reshape(count, width)
    up_w = w_ref[:, part : 2 * part].reshape(count, width)
    down_w = w_ref[:, 2 * part :].reshape(count, width)
    h2 = h2_ref[...]
    mix = matmul(dy_ref[:, width:], spread_ref[...])
    gate = against(h2, gate_w)
    up = against(h2, up_w)
    d_hidden = against(dy_ref[:, :width], down_w) * mix
    sigma = jax.nn.sigmoid(gate)
    silu = gate * sigma
    hid_ref[...] = (silu * up * mix).astype(BF16)
    d_gate = (d_hidden * up * sigma * (1.0 + gate * (1.0 - sigma))).astype(BF16)
    d_up = (d_hidden * silu).astype(BF16)
    dg_ref[...] = d_gate
    du_ref[...] = d_up
    total = matmul(d_gate, gate_w) + matmul(d_up, up_w)

    @pl.when(chunk == 0)
    def _():
        acc[block] = total

    @pl.when((chunk == 1) & (block < 2))
    def _():
        theirs_ref[...] = (acc[block] + total).astype(BF16)

    @pl.when((chunk == 1) & (block >= 2))
    def _():
        mine_ref[...] = (acc[block] + total).astype(BF16)


def experts_call(h2, dy, weights, spread, part):
    rows, width = h2.shape
    owners, depth, _ = weights.shape
    hidden = owners * part
    n, blocks = 2, 4
    step, wide = rows // blocks, hidden // n
    half = jax.ShapeDtypeStruct((rows // 2, width), BF16)
    wide_shape = jax.ShapeDtypeStruct((rows, hidden), BF16)

    def row(c, b):
        return (b + blocks // 2) % blocks

    wide_spec = pl.BlockSpec((step, wide), lambda c, b: (row(c, b), c))
    return pl.pallas_call(
        functools.partial(experts_kernel, part),
        grid=(n, blocks),
        in_specs=[
            pl.BlockSpec((step, width), lambda c, b: (row(c, b), 0)),
            pl.BlockSpec((step, dy.shape[1]), lambda c, b: (row(c, b), 0)),
            pl.BlockSpec((owners // n, depth, width), lambda c, b: (c, 0, 0)),
            pl.BlockSpec((spread.shape[0], wide), lambda c, b: (0, c)),
        ],
        out_specs=[
            wide_spec,
            wide_spec,
            wide_spec,
            pl.BlockSpec((step, width), lambda c, b: (c * jnp.minimum(b, 1), 0)),
            pl.BlockSpec((step, width), lambda c, b: (c * jnp.maximum(b - 2, 0), 0)),
        ],
        out_shape=[wide_shape, wide_shape, wide_shape, half, half],
        scratch_shapes=[pltpu.VMEM((blocks, step, width), F32)],
        compiler_params=pltpu.CompilerParams(vmem_limit_bytes=VMEM),
        cost_estimate=TINY,
        name="experts_rows",
    )(h2, dy, weights, spread)


def expert_grads_kernel(
    part, dg_ref, du_ref, hid_ref, h2_ref, dy_ref, out_ref, token_ref
):
    width = h2_ref.shape[1]
    group = out_ref.shape[0]
    h2 = h2_ref[...]
    out_ref[:, :part] = outer(dg_ref[...], h2).astype(BF16).reshape(group, part, width)
    out_ref[:, part : 2 * part] = outer(du_ref[...], h2).astype(BF16).reshape(group, part, width)
    out_ref[:, 2 * part :] = (
        outer(hid_ref[...], dy_ref[:, :width]).astype(BF16).reshape(group, part, width)
    )
    token_ref[...] = jnp.zeros_like(token_ref)


def expert_grads_call(d_gate, d_up, hidden, h2, dy, owners, part):
    rows, width = h2.shape
    n = 4
    wide = d_gate.shape[1] // n
    wide_spec = pl.BlockSpec((rows, wide), lambda c: (0, c))
    return pl.pallas_call(
        functools.partial(expert_grads_kernel, part),
        grid=(n,),
        in_specs=[
            wide_spec,
            wide_spec,
            wide_spec,
            pl.BlockSpec((rows, width), lambda c: (0, 0)),
            pl.BlockSpec((rows, dy.shape[1]), lambda c: (0, 0)),
        ],
        out_specs=[
            pl.BlockSpec((owners // n, 3 * part, width), lambda c: (c, 0, 0)),
            pl.BlockSpec((8, 128), lambda c: (0, 0)),
        ],
        out_shape=[
            jax.ShapeDtypeStruct((owners, 3 * part, width), BF16),
            jax.ShapeDtypeStruct((8, 128), F32),
        ],
        compiler_params=pltpu.CompilerParams(vmem_limit_bytes=VMEM),
        cost_estimate=TINY,
        name="experts_weights",
    )(d_gate, d_up, hidden, h2, dy)


def add_placed_kernel(where_ref, theirs_ref, mine_ref, token_ref, out_ref):
    ring = mine_ref.shape[0]
    for k in range(ring):
        out_ref[lax.rem(where_ref[0] + k, ring)] = (
            theirs_ref[k].astype(F32) + mine_ref[k].astype(F32)
        ).astype(BF16)


def add_placed_call(where, theirs, mine, token):
    vmem = pl.BlockSpec(memory_space=pltpu.VMEM)
    return pl.pallas_call(
        add_placed_kernel,
        grid_spec=pltpu.PrefetchScalarGridSpec(
            num_scalar_prefetch=1,
            grid=(),
            in_specs=[vmem, vmem, pl.BlockSpec(memory_space=pl.ANY)],
            out_specs=vmem,
        ),
        out_shape=jax.ShapeDtypeStruct(mine.shape, BF16),
        compiler_params=pltpu.CompilerParams(vmem_limit_bytes=VMEM),
        cost_estimate=TINY,
        name="add_cores_placed",
    )(where, theirs, mine, token)


def exchange_sum(pieces, token=None):
    got = lax.all_to_all(pieces, "context", split_axis=0, concat_axis=0, tiled=True)
    if token is not None:
        got = after_call(got, token)
    return jnp.sum(got.astype(F32), axis=0)


def add_kernel(theirs_ref, mine_ref, token_ref, *out_refs):
    for k, out_ref in enumerate(out_refs):
        out_ref[...] = (theirs_ref[k].astype(F32) + mine_ref[k].astype(F32)).astype(BF16)


def add_call(theirs, mine, token):
    shape = theirs.shape
    one = jax.ShapeDtypeStruct(shape[1:], BF16)
    vmem = pl.BlockSpec(memory_space=pltpu.VMEM)
    return pl.pallas_call(
        add_kernel,
        in_specs=[vmem, vmem, pl.BlockSpec(memory_space=pl.ANY)],
        out_specs=[vmem] * shape[0],
        out_shape=[one] * shape[0],
        compiler_params=pltpu.CompilerParams(vmem_limit_bytes=VMEM),
        cost_estimate=TINY,
        name="add_cores",
    )(theirs, mine, token)


def gate_up_down_kernel(part, in_ref, gate_ref, up_ref, down_ref):
    last = in_ref.shape[2]
    count = in_ref.shape[0] * part
    gate_ref[...] = in_ref[:, :part].reshape(count, last).astype(F32).T
    up_ref[...] = in_ref[:, part : 2 * part].reshape(count, last).astype(F32).T
    down_ref[...] = in_ref[:, 2 * part :].reshape(count, last).astype(F32)


def gate_up_down_call(gathered, part):
    members, depth, width = gathered.shape
    ff = members * part
    n = 8
    step = width // n
    return pl.pallas_call(
        functools.partial(gate_up_down_kernel, part),
        grid=(n,),
        in_specs=[pl.BlockSpec((members, depth, step), lambda c: (0, 0, c))],
        out_specs=[
            pl.BlockSpec((step, ff), lambda c: (c, 0)),
            pl.BlockSpec((step, ff), lambda c: (c, 0)),
            pl.BlockSpec((ff, step), lambda c: (0, c)),
        ],
        out_shape=[
            jax.ShapeDtypeStruct((width, ff), F32),
            jax.ShapeDtypeStruct((width, ff), F32),
            jax.ShapeDtypeStruct((ff, width), F32),
        ],
        compiler_params=pltpu.CompilerParams(vmem_limit_bytes=VMEM),
        cost_estimate=TINY,
        name="experts_results",
    )(gathered)


def out_grads_kernel(heads_ref, mine_ref, theirs_ref, out_ref):
    total = outer(heads_ref[0], mine_ref[...]) + outer(heads_ref[1], theirs_ref[...])
    out_ref[...] = total.astype(BF16)


def out_grads_call(heads_out, mine, theirs):
    _, half, columns = heads_out.shape
    width = mine.shape[1]
    n = 4
    spec = pl.BlockSpec((half, width // n), lambda c: (0, c))
    return pl.pallas_call(
        out_grads_kernel,
        grid=(n,),
        in_specs=[pl.BlockSpec(heads_out.shape, lambda c: (0, 0, 0)), spec, spec],
        out_specs=pl.BlockSpec((columns, width // n), lambda c: (0, c)),
        out_shape=jax.ShapeDtypeStruct((columns, width), BF16),
        compiler_params=pltpu.CompilerParams(vmem_limit_bytes=VMEM),
        cost_estimate=TINY,
        name="out_weights",
    )(heads_out, mine, theirs)


def attend_grads_kernel(
    cut, place_ref, h1_ref, d_qkv_ref, out_ref, gains_ref, token_ref, *refs
):
    firsts, seconds, share = refs[:SIDE], refs[SIDE : 2 * SIDE], refs[-1]
    step = pl.program_id(0)
    last = d_qkv_ref.shape[1]
    depth = share.shape[1] - 16
    grad = outer(h1_ref[...], d_qkv_ref[...]).astype(BF16)
    share[:, :depth, :last] = grad.reshape(SIDE, depth, last)
    rows, columns = out_ref.shape[1], share.shape[2] - last
    for k in range(depth // rows):
        share[:, k * rows : (k + 1) * rows, last:] = out_ref[:, :, k * columns : (k + 1) * columns]
    share[:, depth:] = gains_ref[...]
    for k in range(SIDE):

        @pl.when(step == k)
        def _():
            firsts[k][...] = share[:, :cut]

        seconds[k][0] = share[lax.rem(place_ref[1] + k, SIDE), cut:]


def attend_grads_call(place, h1, d_qkv, grad_out, gains, token, cut):
    rows, width = h1.shape
    owners, extra, columns = gains.shape
    depth = width // owners
    last = d_qkv.shape[1]

    def at(i, place):
        return lax.rem(place[0] + i, SIDE)

    first = jax.ShapeDtypeStruct((SIDE, cut, columns), BF16)
    second = jax.ShapeDtypeStruct((SIDE, depth + extra - cut, columns), BF16)
    outs = pl.pallas_call(
        functools.partial(attend_grads_kernel, cut),
        grid_spec=pltpu.PrefetchScalarGridSpec(
            num_scalar_prefetch=1,
            grid=(SIDE,),
            in_specs=[
                pl.BlockSpec((rows, width // SIDE), lambda i, place: (0, at(i, place))),
                pl.BlockSpec((rows, last), lambda i, place: (0, 0)),
                pl.BlockSpec((SIDE,) + grad_out.shape[1:], lambda i, place: (at(i, place), 0, 0)),
                pl.BlockSpec((SIDE, extra, columns), lambda i, place: (at(i, place), 0, 0)),
                pl.BlockSpec(memory_space=pl.ANY),
            ],
            out_specs=[pl.BlockSpec(first.shape, lambda i, place: (0, 0, 0))] * SIDE
            + [pl.BlockSpec((1,) + second.shape[1:], lambda i, place: (i, 0, 0))] * SIDE,
            scratch_shapes=[pltpu.VMEM((SIDE, depth + extra, columns), BF16)],
        ),
        out_shape=[first] * SIDE + [second] * SIDE,
        compiler_params=pltpu.CompilerParams(vmem_limit_bytes=VMEM),
        cost_estimate=TINY,
        name="attention_weights",
    )(place, h1, d_qkv, grad_out, gains, token)
    return outs[:SIDE], outs[SIDE:]


def total_of(refs):
    total = refs[0][...].astype(F32)
    for ref in refs[1:]:
        total = total + ref[...].astype(F32)
    return total.astype(BF16)


def half_sum_kernel(place_ref, *refs):
    outs, total = refs[2 * SIDE + 1 : -1], refs[-1]
    firsts, seconds = outs[:SIDE], outs[SIDE:]
    total[...] = total_of(refs[:SIDE])
    other = total_of(refs[SIDE : 2 * SIDE])
    for k in range(SIDE):
        firsts[k][...] = total[lax.rem(place_ref[1] + k, SIDE)]
        seconds[k][...] = other[k]


def half_sum_call(place, firsts, seconds, token):
    vmem = pl.BlockSpec(memory_space=pltpu.VMEM)
    outs = pl.pallas_call(
        half_sum_kernel,
        grid_spec=pltpu.PrefetchScalarGridSpec(
            num_scalar_prefetch=1,
            grid=(),
            in_specs=[vmem] * (2 * SIDE) + [pl.BlockSpec(memory_space=pl.ANY)],
            out_specs=[vmem] * (2 * SIDE),
            scratch_shapes=[pltpu.VMEM(firsts[0].shape, BF16)],
        ),
        out_shape=[jax.ShapeDtypeStruct(v.shape[1:], BF16) for v in (*firsts, *seconds)],
        compiler_params=pltpu.CompilerParams(vmem_limit_bytes=VMEM),
        cost_estimate=TINY,
        name="half_sum",
    )(place, *firsts, *seconds, token)
    return outs[:SIDE], outs[SIDE:]


def last_sum_kernel(token_ref, other_token_ref, *refs):
    out = refs[-1]
    cut = refs[0].shape[0]
    out[:cut] = total_of(refs[:SIDE])
    out[cut:] = total_of(refs[SIDE : 2 * SIDE])


def last_sum_call(firsts, seconds, *tokens):
    rows, columns = firsts[0].shape[0] + seconds[0].shape[0], firsts[0].shape[1]
    vmem = pl.BlockSpec(memory_space=pltpu.VMEM)
    return pl.pallas_call(
        last_sum_kernel,
        in_specs=[pl.BlockSpec(memory_space=pl.ANY)] * 2 + [vmem] * (2 * SIDE),
        out_specs=vmem,
        out_shape=jax.ShapeDtypeStruct((rows, columns), BF16),
        compiler_params=pltpu.CompilerParams(vmem_limit_bytes=VMEM),
        cost_estimate=TINY,
        name="last_sum",
    )(*tokens, *firsts, *seconds)


def plane_send(pieces, dx, dz):
    return [pieces[0]] + [plane(pieces[k], -k * dx, -k * dz) for k in range(1, SIDE)]


def columns_kernel(heads_width, size, where_ref, mine_ref, theirs_ref, q_ref, k_ref, v_ref, sum_ref):
    depth = q_ref.shape[0]
    mine, theirs = mine_ref[0].astype(F32), theirs_ref[0].astype(F32)
    first = where_ref[1] == 0
    q_ref[:, :heads_width] = jnp.where(first, mine[:depth, :heads_width], theirs[:depth, :heads_width])
    q_ref[:, heads_width:] = jnp.where(first, theirs[:depth, :heads_width], mine[:depth, :heads_width])
    both = mine + theirs
    k_ref[...] = both[:depth, heads_width : heads_width + size]
    v_ref[...] = both[:depth, heads_width + size :]

    @pl.when(pl.program_id(0) == 0)
    def _():
        sum_ref[...] = jnp.zeros_like(sum_ref)

    sum_ref[...] += both[depth:]


def columns_call(where, mine, theirs, depth, heads_width, size):
    ring, rows, last = mine.shape
    cores = 2

    def at(k, where):
        return (0, lax.rem(where[0] + k, ring))

    return pl.pallas_call(
        functools.partial(columns_kernel, heads_width, size),
        grid_spec=pltpu.PrefetchScalarGridSpec(
            num_scalar_prefetch=1,
            grid=(ring,),
            in_specs=[pl.BlockSpec((1, rows, last), lambda k, where: (k, 0, 0))] * 2,
            out_specs=[
                pl.BlockSpec((depth, cores * heads_width), at),
                pl.BlockSpec((depth, size), at),
                pl.BlockSpec((depth, size), at),
                pl.BlockSpec((rows - depth, last), lambda k, where: (0, 0)),
            ],
        ),
        out_shape=[
            jax.ShapeDtypeStruct((depth, ring * cores * heads_width), F32),
            jax.ShapeDtypeStruct((depth, ring * size), F32),
            jax.ShapeDtypeStruct((depth, ring * size), F32),
            jax.ShapeDtypeStruct((rows - depth, last), F32),
        ],
        compiler_params=pltpu.CompilerParams(vmem_limit_bytes=VMEM),
        cost_estimate=TINY,
        name="columns_results",
    )(where, mine, theirs)


def rows_kernel(where_ref, mine_ref, theirs_ref, out_ref):
    count = mine_ref.shape[1]
    mine, theirs = mine_ref[0].astype(F32), theirs_ref[0].astype(F32)
    first = where_ref[1] == 0
    out_ref[:count] = jnp.where(first, mine, theirs)
    out_ref[count:] = jnp.where(first, theirs, mine)


def rows_call(where, mine, theirs):
    ring, count, width = mine.shape
    cores = 2
    return pl.pallas_call(
        rows_kernel,
        grid_spec=pltpu.PrefetchScalarGridSpec(
            num_scalar_prefetch=1,
            grid=(ring,),
            in_specs=[pl.BlockSpec((1, count, width), lambda k, where: (k, 0, 0))] * 2,
            out_specs=pl.BlockSpec(
                (cores * count, width), lambda k, where: (lax.rem(where[0] + k, ring), 0)
            ),
        ),
        out_shape=jax.ShapeDtypeStruct((ring * cores * count, width), F32),
        compiler_params=pltpu.CompilerParams(vmem_limit_bytes=VMEM),
        cost_estimate=TINY,
        name="rows_results",
    )(where, mine, theirs)


def expert_out_kernel(part, hid_ref, w_ref, token_ref, theirs_ref, mine_ref):
    width = w_ref.shape[2]
    block = pl.program_id(0)
    total = matmul(hid_ref[...], w_ref[...].reshape(w_ref.shape[0] * part, width)).astype(BF16)

    @pl.when(block < 2)
    def _():
        theirs_ref[...] = total

    @pl.when(block >= 2)
    def _():
        mine_ref[...] = total


def expert_out_call(hidden, weights, token, part):
    rows, wide = hidden.shape
    owners, _, width = weights.shape
    blocks = 4
    step = rows // blocks
    half = jax.ShapeDtypeStruct((rows // 2, width), BF16)
    return pl.pallas_call(
        functools.partial(expert_out_kernel, part),
        grid=(blocks,),
        in_specs=[
            pl.BlockSpec((step, wide), lambda b: ((b + blocks // 2) % blocks, 0)),
            pl.BlockSpec((owners, part, width), lambda b: (0, 2, 0)),
            pl.BlockSpec(memory_space=pl.ANY),
        ],
        out_specs=[
            pl.BlockSpec((step, width), lambda b: (jnp.minimum(b, 1), 0)),
            pl.BlockSpec((step, width), lambda b: (jnp.maximum(b - 2, 0), 0)),
        ],
        out_shape=[half, half],
        compiler_params=pltpu.CompilerParams(vmem_limit_bytes=VMEM),
        cost_estimate=pl.CostEstimate(
            flops=2 * rows * wide * width, bytes_accessed=20_000_000, transcendentals=0
        ),
        name="experts_out",
    )(hidden, weights, token)


def local(
    tokens,
    lengths,
    routes,
    mix_weights,
    cotangent,
    w_query,
    key_weight,
    value_weight,
    w_out,
    norm_attn,
    norm_moe,
    norm_query,
    norm_key,
    w_gate,
    w_up,
    w_down,
):
    owners = lax.axis_size("experts")
    ring = lax.axis_size("context")
    cores = lax.axis_size("dp")
    members = ring * cores
    y = lax.axis_index("context")
    d = lax.axis_index("dp")
    j = y * cores + d
    micro, _, row_count, width = tokens.shape
    head = norm_query.shape[0] * owners
    q_width = w_query.shape[1] // members
    q_heads = q_width // head
    depth = w_query.shape[0]
    ff = w_gate.shape[2]
    ff_part = ff // members
    out_rows = w_out.shape[0]
    out_part = out_rows // members
    seqs = cores * micro
    span = ring * row_count
    rows = seqs * span
    scale = head ** (-0.5)

    forth = [
        (es * members + k, ((es % cores) * members + k) * members + es // cores)
        for es in range(owners)
        for k in range(members)
    ]
    back = [(b, a) for a, b in forth]
    out_chunk = lax.ppermute(
        lax.dynamic_slice_in_dim(w_out, j * out_part, out_part, axis=0), EVERY, forth
    )
    expert_pack = jnp.concatenate(
        [
            lax.dynamic_slice_in_dim(w_gate[0], j * ff_part, ff_part, axis=1).T,
            lax.dynamic_slice_in_dim(w_up[0], j * ff_part, ff_part, axis=1).T,
            lax.dynamic_slice_in_dim(w_down[0], j * ff_part, ff_part, axis=0),
        ],
        axis=0,
    )
    gains = jnp.concatenate([norm_attn, norm_moe, norm_query, norm_key])
    packed = jnp.concatenate(
        [
            lax.dynamic_slice_in_dim(w_query, j * q_width, q_width, axis=1),
            lax.dynamic_slice_in_dim(key_weight, y * head, head, axis=1),
            lax.dynamic_slice_in_dim(value_weight, y * head, head, axis=1),
            jnp.concatenate(jnp.split(out_chunk, depth // out_part, axis=1), axis=0),
        ],
        axis=1,
    )
    qkv_width = q_width + 2 * head
    gain_rows = jnp.pad(gains[None], ((0, 15), (0, packed.shape[1] - gains.shape[0])))
    shared = lax.all_gather(
        jnp.concatenate([packed, gain_rows]), "experts", axis=0, tiled=False
    )
    expert_all = lax.all_gather(expert_pack, "experts", axis=0, tiled=False)
    gain_row = shared[:, depth]
    gain_row = gain_row.astype(F32)
    gain_attn = gain_row[:, :depth].reshape(-1)
    gain_moe = gain_row[:, depth : 2 * depth].reshape(-1)
    eighth = norm_query.shape[0]
    gain_query = gain_row[:, 2 * depth : 2 * depth + eighth].reshape(-1)
    gain_key = gain_row[:, 2 * depth + eighth : 2 * depth + 2 * eighth].reshape(-1)
    hidden_width = owners * ff_part

    where = jnp.stack([y, d]).astype(jnp.int32)
    x_own = tokens[:, 0]
    x_rows = gather_rows(x_own, ring)
    len_all = jnp.stack([lengths[:, 0], swap(lengths[:, 0])]).reshape(seqs)
    own_pos = y * row_count + jnp.arange(row_count, dtype=jnp.int32)
    valid = (own_pos[None, :] < lengths[:, 0][:, None]).astype(F32)
    dy_own = (cotangent[:, 0].astype(F32) * valid[:, :, None]).astype(BF16)
    ids = jnp.arange(owners, dtype=jnp.int32)
    mix_own = jnp.sum(
        jnp.where(routes[:, 0][..., None] == ids, mix_weights[:, 0][..., None], 0.0), axis=2
    )
    mix_high = mix_own.astype(BF16)
    mix_low = (mix_own - mix_high.astype(F32)).astype(BF16)
    lanes = 128
    mix_pad = jnp.zeros((micro, row_count, lanes - 2 * owners), BF16)
    dy_mix = gather_rows(jnp.concatenate([dy_own, mix_high, mix_low, mix_pad], axis=-1), ring)
    dy_mix = dy_mix.reshape(rows, width + lanes)
    lane = jnp.arange(lanes, dtype=jnp.int32)
    spread = (
        (jnp.arange(hidden_width, dtype=jnp.int32)[None, :] // ff_part == (lane % owners)[:, None])
        & (lane < 2 * owners)[:, None]
    ).astype(BF16)

    k_index = jnp.arange(span, dtype=jnp.int32)
    pos = ((y + k_index // row_count) % ring) * row_count + k_index % row_count
    frequency = ROPE_BASE ** (-jnp.arange(head // 2, dtype=F32) * 2.0 / head)
    phase = pos.astype(F32)[:, None] * frequency[None, :]
    cosines, sines = jnp.cos(phase), jnp.sin(phase)
    cosines = jnp.concatenate([cosines, cosines], axis=1)
    sines = jnp.concatenate([-sines, sines], axis=1)
    allowed = (pos[None, None, :] <= pos[None, :, None]) & (
        pos[None, None, :] < len_all[:, None, None]
    )
    bias = jnp.where(allowed, 0.0, -1e30).astype(F32)

    shape = (ring, micro, row_count, width)
    head_gains = (gain_query[None], gain_key[None])
    h1, qkv, heads_out, theirs, mine = attend_call(
        functools.partial(attend_kernel, q_heads, scale),
        (x_rows, gain_attn[None], shared, cosines, sines, bias, *head_gains, dy_mix),
        ("rows", "", "", "", "", "bias", "", "", "token"),
        (
            ("rows", width, BF16),
            ("rows", qkv_width, F32),
            ("rows", q_width, BF16),
            ("parts", width, BF16),
        ),
        [pltpu.VMEM((span, q_width), BF16), pltpu.VMEM((span, width), BF16)],
        shape,
        "attention",
        TINY,
    )
    attn_own = scatter_rows(theirs[0], mine[0])
    x1 = x_own.astype(F32) + attn_own
    inverse_mid = inverse_rms(x1)
    h2 = gather_rows((x1 * inverse_mid * gain_moe).astype(BF16), ring).reshape(rows, width)

    d_gate, d_up, hidden, theirs, mine = experts_call(h2, dy_mix, expert_all, spread, ff_part)
    grad_experts, token = expert_grads_call(
        d_gate, d_up, hidden, h2, dy_mix, owners, ff_part
    )
    pieces = add_call(swap(theirs.reshape(shape)), mine.reshape(shape), token)
    d_h2 = ring_sum(pieces)
    moe_theirs, moe_mine = expert_out_call(hidden, expert_all, token, ff_part)

    grad_gain_moe = jnp.sum(d_h2 * x1 * inverse_mid, axis=(0, 1))
    d_x1 = dy_own.astype(F32) + norm_back(d_h2, x1, inverse_mid, gain_moe)
    grad_experts = lax.psum_scatter(
        after_call(grad_experts, pieces[1]), "experts", scatter_dimension=0, tiled=False
    )
    moe_pieces = add_placed_call(
        where, swap(moe_theirs.reshape(shape)), moe_mine.reshape(shape), hidden
    )
    d_mine = after_call(ring_stack(d_x1.astype(BF16), ring), moe_pieces)
    d_theirs = swap(d_mine)
    grad_out = out_grads_call(
        heads_out.reshape(2, rows // 2, q_width),
        d_mine.reshape(-1, width),
        d_theirs.reshape(-1, width),
    )
    grad_out = grad_out.reshape(owners, out_part, width)
    d_qkv, theirs, mine, sum_q, sum_k, sum_x = attend_call(
        functools.partial(attend_back_kernel, q_heads, scale),
        (
            d_theirs[None],
            d_mine[None],
            x_rows,
            gain_attn[None],
            shared,
            cosines,
            sines,
            bias,
            *head_gains,
            qkv,
            moe_pieces,
            grad_out,
        ),
        (
            "theirs",
            "mine",
            "rows",
            "",
            "",
            "",
            "",
            "bias",
            "",
            "",
            "rows",
            "token",
            "token",
        ),
        (
            ("rows", qkv_width, BF16),
            ("parts", width, BF16),
            ("sum", head, F32),
            ("sum", head, F32),
            ("sum", width, F32),
        ),
        [pltpu.VMEM((span, qkv_width), BF16)],
        shape,
        "attention_back",
        pl.CostEstimate(flops=9_000_000_000, bytes_accessed=90_000_000, transcendentals=0),
    )
    output = (x1 + exchange_sum(moe_pieces, d_qkv)).astype(BF16)[:, None]
    grad_gain_query, grad_gain_key, grad_gain_attn = sum_q[0], sum_k[0], sum_x[0]
    h1, d_qkv = h1.reshape(rows, width), d_qkv.reshape(rows, qkv_width)

    grad_gains = jnp.concatenate(
        [
            grad_gain_attn.reshape(owners, depth),
            grad_gain_moe.reshape(owners, depth),
            grad_gain_query.reshape(owners, eighth),
            grad_gain_key.reshape(owners, eighth),
        ],
        axis=1,
    ).astype(BF16)
    grad_gains = jnp.pad(
        grad_gains[:, None], ((0, 0), (0, 15), (0, shared.shape[2] - grad_gains.shape[1]))
    )
    index = lax.axis_index("experts")
    place = jnp.stack([index // SIDE, index % SIDE]).astype(jnp.int32)
    firsts, seconds = attend_grads_call(
        place, h1, d_qkv, grad_out, grad_gains, output, depth // 2 + 16
    )
    h1_pieces = add_placed_call(where, swap(theirs[0]), mine[0], firsts[1])
    d_h1 = exchange_sum(h1_pieces)
    x_f32 = x_own.astype(F32)
    input_grad = (d_x1 + norm_back(d_h1, x_f32, inverse_rms(x_f32), gain_attn))[:, None]
    grad_experts = after_call(grad_experts, h1_pieces)
    all_experts = lax.all_gather(grad_experts, GROUP, axis=0, tiled=False)
    firsts, seconds = plane_send(firsts, 1, 0), plane_send(seconds, 0, 1)
    firsts, seconds = half_sum_call(place, firsts, seconds, grad_out)
    result_gate, result_up, result_down = gate_up_down_call(all_experts, ff_part)
    grads = last_sum_call(plane_send(firsts, 0, 1), plane_send(seconds, 1, 0), d_h1, result_down)
    out_sum = jnp.concatenate(
        [grads[k * out_part : (k + 1) * out_part, qkv_width:] for k in range(depth // out_part)],
        axis=1,
    )
    result_q, result_k, result_v, gain_sum = columns_call(
        where, *gather_members(grads[:, :qkv_width]), depth, q_width, head
    )
    out_sum = after_call(lax.ppermute(out_sum, EVERY, back), input_grad)
    result_out = rows_call(where, *gather_members(out_sum))
    gain_sum = gain_sum[0]
    return (
        output,
        input_grad,
        result_q,
        result_k,
        result_v,
        result_out,
        gain_sum[:depth],
        gain_sum[depth : 2 * depth],
        gain_sum[2 * depth : 2 * depth + eighth],
        gain_sum[2 * depth + eighth : 2 * depth + 2 * eighth],
        result_gate[None],
        result_up[None],
        result_down[None],
    )


def solution(mesh):
    rows = P(None, ("experts", "dp"), "context", None)
    in_specs = (
        rows,
        P(None, ("experts", "dp")),
        rows,
        rows,
        rows,
        P("experts", None),
        P("experts", None),
        P("experts", None),
        P("experts", None),
        P("experts"),
        P("experts"),
        P("experts"),
        P("experts"),
        P("experts", None, None),
        P("experts", None, None),
        P("experts", None, None),
    )
    out_specs = (
        rows,
        rows,
        P("experts", None),
        P("experts", None),
        P("experts", None),
        P("experts", None),
        P("experts"),
        P("experts"),
        P("experts"),
        P("experts"),
        P("experts", None, None),
        P("experts", None, None),
        P("experts", None, None),
    )
    return jax.shard_map(local, mesh=mesh, in_specs=in_specs, out_specs=out_specs, check_vma=False)
```

```python
import functools

import jax
import jax.numpy as jnp
from jax import lax
from jax.experimental import pallas as pl
from jax.experimental.pallas import tpu as pltpu
from jax.sharding import PartitionSpec as P

EPS = 1e-06
ROPE_BASE = 1000000.0
F32 = jnp.float32
BF16 = jnp.bfloat16
GROUP = ("context", "dp")
EVERY = ("experts", "context", "dp")
VMEM = 60 * 1024 * 1024
SIDE = 4
TINY = pl.CostEstimate(flops=0, bytes_accessed=1000, transcendentals=0)


def inverse_rms(v):
    return lax.rsqrt(jnp.mean(v * v, axis=-1, keepdims=True) + EPS)


def norm_back(grad_in, v, inverse, gain):
    scaled = grad_in * gain
    return inverse * scaled - v * inverse**3 * jnp.mean(scaled * v, axis=-1, keepdims=True)


def matmul(left, right):
    return jnp.dot(left, right, preferred_element_type=F32)


def against(left, right):
    return lax.dot_general(left, right, (((1,), (1,)), ((), ())), preferred_element_type=F32)


def outer(left, right):
    return lax.dot_general(left, right, (((0,), (0,)), ((), ())), preferred_element_type=F32)


def swap(v):
    return lax.ppermute(v, "dp", [(0, 1), (1, 0)])


def ring_stack(own, ring):
    pieces = [own]
    for k in range(1, ring):
        pieces.append(lax.ppermute(own, "context", [((i + k) % ring, i) for i in range(ring)]))
    return jnp.stack(pieces)


def gather_rows(own, ring):
    mine = ring_stack(own, ring)
    return jnp.stack([mine, swap(mine)])


def ring_sum(pieces):
    ring = len(pieces)
    total = pieces[0].astype(F32)
    for k in range(1, ring):
        got = lax.ppermute(pieces[k], "context", [(i, (i + k) % ring) for i in range(ring)])
        total = total + got.astype(F32)
    return total


def add_cores(theirs, mine):
    other = swap(theirs)
    return [
        (mine[k].astype(F32) + other[k].astype(F32)).astype(BF16) for k in range(mine.shape[0])
    ]


def scatter_rows(theirs, mine):
    return ring_sum(add_cores(theirs, mine))


def gather_members(v):
    ring = lax.axis_size("context")
    pieces = [v]
    for k in range(1, ring):
        pieces.append(lax.ppermute(v, "context", [((i + k) % ring, i) for i in range(ring)]))
    mine = jnp.stack(pieces)
    return mine, swap(mine)


def plane(v, dx, dz):
    moves = [
        (((i // SIDE + dx) % SIDE) * SIDE + (i % SIDE + dz) % SIDE, i) for i in range(SIDE * SIDE)
    ]
    return lax.ppermute(v, "experts", moves)


def after_kernel(v_ref, *refs):
    pass


def after_call(v, *tokens):
    anywhere = pl.BlockSpec(memory_space=pl.ANY)
    return pl.pallas_call(
        after_kernel,
        in_specs=[anywhere] * (1 + len(tokens)),
        out_specs=anywhere,
        out_shape=jax.ShapeDtypeStruct(v.shape, v.dtype),
        input_output_aliases={0: 0},
        cost_estimate=TINY,
        name="after",
    )(v, *tokens)


def rope(v, cosines, sines):
    return v * cosines + pltpu.roll(v, v.shape[-1] // 2, 1) * sines


def rope_back(v, cosines, sines):
    return v * cosines + pltpu.roll(v * sines, v.shape[-1] // 2, 1)


def flat(ref):
    v = ref[...]
    return v.reshape(v.shape[1] * v.shape[3], v.shape[4])


def chunks(ref, columns):
    v = ref[:, :-16, :columns]
    return v.reshape(v.shape[0] * v.shape[1], columns)


def out_blocks(ref, first):
    last = ref.shape[2] - first
    rows = last // ref.shape[0]
    for k in range((ref.shape[1] - 16) // rows):
        yield k * last, (k + 1) * last, ref[:, k * rows : (k + 1) * rows, first:].reshape(last, last)


def put(ref, v):
    ref[...] = v.reshape(ref.shape).astype(ref.dtype)


def attend_kernel(
    heads,
    scale,
    x_ref,
    gain_ref,
    w_ref,
    cos_ref,
    sin_ref,
    bias_ref,
    gain_q_ref,
    gain_k_ref,
    token_ref,
    h1_ref,
    qkv_ref,
    heads_ref,
    theirs_ref,
    mine_ref,
    heads_out,
    total,
):
    size = cos_ref.shape[1]
    x = flat(x_ref).astype(F32)
    h1 = (x * inverse_rms(x) * gain_ref[...]).astype(BF16)
    put(h1_ref, h1)
    width = (heads + 2) * size
    qkv = matmul(h1, chunks(w_ref, width))
    put(qkv_ref, qkv)
    cosines, sines, bias = cos_ref[...], sin_ref[...], bias_ref[0]
    k_pre = qkv[:, heads * size : (heads + 1) * size]
    key = rope(k_pre * inverse_rms(k_pre) * gain_k_ref[...], cosines, sines).astype(BF16)
    value = qkv[:, (heads + 1) * size :].astype(BF16)
    for g in range(heads):
        q_pre = qkv[:, g * size : (g + 1) * size]
        query = rope(q_pre * inverse_rms(q_pre) * gain_q_ref[...], cosines, sines).astype(BF16)
        logits = against(query, key) * scale + bias
        scaled = jnp.exp(logits - jnp.max(logits, axis=-1, keepdims=True))
        soft = (scaled / jnp.sum(scaled, axis=-1, keepdims=True)).astype(BF16)
        heads_out[:, g * size : (g + 1) * size] = matmul(soft, value).astype(BF16)
    out = heads_out[...]
    put(heads_ref, out)
    for first, last, block in out_blocks(w_ref, width):
        total[:, first:last] = matmul(out, block).astype(BF16)

    @pl.when(pl.program_id(0) < 2)
    def _():
        put(theirs_ref, total[...])

    @pl.when(pl.program_id(0) >= 2)
    def _():
        put(mine_ref, total[...])


def attend_back_kernel(
    heads,
    scale,
    theirs_da_ref,
    mine_da_ref,
    x_ref,
    gain_ref,
    w_ref,
    cos_ref,
    sin_ref,
    bias_ref,
    gain_q_ref,
    gain_k_ref,
    qkv_ref,
    token_ref,
    other_token_ref,
    d_qkv_ref,
    theirs_ref,
    mine_ref,
    sum_q_ref,
    sum_k_ref,
    sum_x_ref,
    d_qkv,
):
    size = cos_ref.shape[1]
    step = pl.program_id(0)

    @pl.when(step == 0)
    def _():
        sum_q_ref[...] = jnp.zeros_like(sum_q_ref)
        sum_k_ref[...] = jnp.zeros_like(sum_k_ref)
        sum_x_ref[...] = jnp.zeros_like(sum_x_ref)

    width = (heads + 2) * size
    da = jnp.where(step < 2, flat(theirs_da_ref), flat(mine_da_ref))
    d_heads = None
    for first, last, block in out_blocks(w_ref, width):
        piece = against(da[:, first:last], block)
        d_heads = piece if d_heads is None else d_heads + piece
    d_heads = d_heads.astype(BF16)
    qkv = flat(qkv_ref)
    cosines, sines, bias = cos_ref[...], sin_ref[...], bias_ref[0]
    gain_q, gain_k = gain_q_ref[...], gain_k_ref[...]
    k_pre = qkv[:, heads * size : (heads + 1) * size]
    inverse_k = inverse_rms(k_pre)
    key = rope(k_pre * inverse_k * gain_k, cosines, sines).astype(BF16)
    value = qkv[:, (heads + 1) * size :].astype(BF16)
    d_key = jnp.zeros(k_pre.shape, F32)
    d_value = jnp.zeros(k_pre.shape, F32)
    sum_q = jnp.zeros((1, size), F32)
    for g in range(heads):
        q_pre = qkv[:, g * size : (g + 1) * size]
        inverse_q = inverse_rms(q_pre)
        query = rope(q_pre * inverse_q * gain_q, cosines, sines).astype(BF16)
        logits = against(query, key) * scale + bias
        scaled = jnp.exp(logits - jnp.max(logits, axis=-1, keepdims=True))
        probs = scaled / jnp.sum(scaled, axis=-1, keepdims=True)
        d_head = d_heads[:, g * size : (g + 1) * size]
        d_probs = against(d_head, value)
        d_scores = probs * (d_probs - jnp.sum(probs * d_probs, axis=-1, keepdims=True))
        d_scores = d_scores.astype(BF16)
        d_query = rope_back(matmul(d_scores, key) * scale, cosines, sines)
        d_key = d_key + outer(d_scores, query)
        d_value = d_value + outer(probs.astype(BF16), d_head)
        sum_q = sum_q + jnp.sum(d_query * q_pre * inverse_q, axis=0, keepdims=True)
        d_qkv[:, g * size : (g + 1) * size] = norm_back(d_query, q_pre, inverse_q, gain_q).astype(
            BF16
        )
    d_key = rope_back(d_key * scale, cosines, sines)
    sum_k = jnp.sum(d_key * k_pre * inverse_k, axis=0, keepdims=True)
    d_qkv[:, heads * size : (heads + 1) * size] = norm_back(d_key, k_pre, inverse_k, gain_k).astype(
        BF16
    )
    d_qkv[:, (heads + 1) * size :] = d_value.astype(BF16)
    grads = d_qkv[...]
    put(d_qkv_ref, grads)
    part = against(grads, chunks(w_ref, width))
    x = flat(x_ref).astype(F32)
    sum_x_ref[0:1, :] += jnp.sum(part * (x * inverse_rms(x)), axis=0, keepdims=True)
    sum_q_ref[0:1, :] += sum_q
    sum_k_ref[0:1, :] += sum_k

    @pl.when(step < 2)
    def _():
        put(theirs_ref, part)

    @pl.when(step >= 2)
    def _():
        put(mine_ref, part)


def attend_call(kernel, operands, extra, outputs, scratch, shape, name, cost):
    ring, micro, row_count, width = shape

    def rows_spec(last):
        return pl.BlockSpec(
            (1, ring, 1, row_count, last), lambda b: (1 - b // 2, 0, b % 2, 0, 0)
        )

    def whole(v):
        return pl.BlockSpec(v.shape, lambda b: (0,) * v.ndim)

    def slot_spec(v, kind):
        block = (1, ring, 1, row_count, v.shape[-1])
        if kind == "theirs":
            return pl.BlockSpec(block, lambda b: (0, 0, jnp.minimum(b, 1), 0, 0))
        return pl.BlockSpec(block, lambda b: (0, 0, jnp.maximum(b - 2, 0), 0, 0))

    in_specs = [
        rows_spec(v.shape[-1])
        if kind == "rows"
        else slot_spec(v, kind)
        if kind in ("theirs", "mine")
        else pl.BlockSpec((1,) + v.shape[1:], lambda b: ((1 - b // 2) * micro + b % 2, 0, 0))
        if kind == "bias"
        else pl.BlockSpec(memory_space=pl.ANY)
        if kind == "token"
        else whole(v)
        for v, kind in zip(operands, extra)
    ]
    out_shape, out_specs = [], []
    for kind, last, dtype in outputs:
        if kind == "rows":
            out_shape.append(jax.ShapeDtypeStruct((2, ring, micro, row_count, last), dtype))
            out_specs.append(rows_spec(last))
        elif kind == "parts":
            one = jax.ShapeDtypeStruct((1, ring, micro, row_count, last), dtype)
            out_shape += [one, one]
            block = (1, ring, 1, row_count, last)
            out_specs.append(pl.BlockSpec(block, lambda b: (0, 0, jnp.minimum(b, 1), 0, 0)))
            out_specs.append(pl.BlockSpec(block, lambda b: (0, 0, jnp.maximum(b - 2, 0), 0, 0)))
        else:
            out_shape.append(jax.ShapeDtypeStruct((8, last), dtype))
            out_specs.append(pl.BlockSpec((8, last), lambda b: (0, 0)))
    return pl.pallas_call(
        kernel,
        grid=(2 * micro,),
        in_specs=in_specs,
        out_specs=out_specs,
        out_shape=out_shape,
        scratch_shapes=scratch,
        compiler_params=pltpu.CompilerParams(vmem_limit_bytes=VMEM),
        cost_estimate=cost,
        name=name,
    )(*operands)


def experts_kernel(
    part, h2_ref, dy_ref, w_ref, spread_ref, dg_ref, du_ref, hid_ref, theirs_ref, mine_ref, acc
):
    chunk, block = pl.program_id(0), pl.program_id(1)
    width = h2_ref.shape[1]
    count = w_ref.shape[0] * part
    gate_w = w_ref[:, :part].reshape(count, width)
    up_w = w_ref[:, part : 2 * part].reshape(count, width)
    down_w = w_ref[:, 2 * part :].reshape(count, width)
    h2 = h2_ref[...]
    mix = matmul(dy_ref[:, width:], spread_ref[...])
    gate = against(h2, gate_w)
    up = against(h2, up_w)
    d_hidden = against(dy_ref[:, :width], down_w) * mix
    sigma = jax.nn.sigmoid(gate)
    silu = gate * sigma
    hid_ref[...] = (silu * up * mix).astype(BF16)
    d_gate = (d_hidden * up * sigma * (1.0 + gate * (1.0 - sigma))).astype(BF16)
    d_up = (d_hidden * silu).astype(BF16)
    dg_ref[...] = d_gate
    du_ref[...] = d_up
    total = matmul(d_gate, gate_w) + matmul(d_up, up_w)

    @pl.when(chunk == 0)
    def _():
        acc[block] = total

    @pl.when((chunk == 1) & (block < 2))
    def _():
        theirs_ref[...] = (acc[block] + total).astype(BF16)

    @pl.when((chunk == 1) & (block >= 2))
    def _():
        mine_ref[...] = (acc[block] + total).astype(BF16)


def experts_call(h2, dy, weights, spread, part):
    rows, width = h2.shape
    owners, depth, _ = weights.shape
    hidden = owners * part
    n, blocks = 2, 4
    step, wide = rows // blocks, hidden // n
    half = jax.ShapeDtypeStruct((rows // 2, width), BF16)
    wide_shape = jax.ShapeDtypeStruct((rows, hidden), BF16)

    def row(c, b):
        return (b + blocks // 2) % blocks

    wide_spec = pl.BlockSpec((step, wide), lambda c, b: (row(c, b), c))
    return pl.pallas_call(
        functools.partial(experts_kernel, part),
        grid=(n, blocks),
        in_specs=[
            pl.BlockSpec((step, width), lambda c, b: (row(c, b), 0)),
            pl.BlockSpec((step, dy.shape[1]), lambda c, b: (row(c, b), 0)),
            pl.BlockSpec((owners // n, depth, width), lambda c, b: (c, 0, 0)),
            pl.BlockSpec((spread.shape[0], wide), lambda c, b: (0, c)),
        ],
        out_specs=[
            wide_spec,
            wide_spec,
            wide_spec,
            pl.BlockSpec((step, width), lambda c, b: (c * jnp.minimum(b, 1), 0)),
            pl.BlockSpec((step, width), lambda c, b: (c * jnp.maximum(b - 2, 0), 0)),
        ],
        out_shape=[wide_shape, wide_shape, wide_shape, half, half],
        scratch_shapes=[pltpu.VMEM((blocks, step, width), F32)],
        compiler_params=pltpu.CompilerParams(vmem_limit_bytes=VMEM),
        cost_estimate=TINY,
        name="experts_rows",
    )(h2, dy, weights, spread)


def expert_grads_kernel(
    part, dg_ref, du_ref, hid_ref, h2_ref, dy_ref, out_ref, token_ref
):
    width = h2_ref.shape[1]
    group = out_ref.shape[0]
    h2 = h2_ref[...]
    out_ref[:, :part] = outer(dg_ref[...], h2).astype(BF16).reshape(group, part, width)
    out_ref[:, part : 2 * part] = outer(du_ref[...], h2).astype(BF16).reshape(group, part, width)
    out_ref[:, 2 * part :] = (
        outer(hid_ref[...], dy_ref[:, :width]).astype(BF16).reshape(group, part, width)
    )
    token_ref[...] = jnp.zeros_like(token_ref)


def expert_grads_call(d_gate, d_up, hidden, h2, dy, owners, part):
    rows, width = h2.shape
    n = 4
    wide = d_gate.shape[1] // n
    wide_spec = pl.BlockSpec((rows, wide), lambda c: (0, c))
    return pl.pallas_call(
        functools.partial(expert_grads_kernel, part),
        grid=(n,),
        in_specs=[
            wide_spec,
            wide_spec,
            wide_spec,
            pl.BlockSpec((rows, width), lambda c: (0, 0)),
            pl.BlockSpec((rows, dy.shape[1]), lambda c: (0, 0)),
        ],
        out_specs=[
            pl.BlockSpec((owners // n, 3 * part, width), lambda c: (c, 0, 0)),
            pl.BlockSpec((8, 128), lambda c: (0, 0)),
        ],
        out_shape=[
            jax.ShapeDtypeStruct((owners, 3 * part, width), BF16),
            jax.ShapeDtypeStruct((8, 128), F32),
        ],
        compiler_params=pltpu.CompilerParams(vmem_limit_bytes=VMEM),
        cost_estimate=TINY,
        name="experts_weights",
    )(d_gate, d_up, hidden, h2, dy)


def add_placed_kernel(where_ref, theirs_ref, mine_ref, token_ref, out_ref):
    ring = mine_ref.shape[0]
    for k in range(ring):
        out_ref[lax.rem(where_ref[0] + k, ring)] = (
            theirs_ref[k].astype(F32) + mine_ref[k].astype(F32)
        ).astype(BF16)


def add_placed_call(where, theirs, mine, token):
    vmem = pl.BlockSpec(memory_space=pltpu.VMEM)
    return pl.pallas_call(
        add_placed_kernel,
        grid_spec=pltpu.PrefetchScalarGridSpec(
            num_scalar_prefetch=1,
            grid=(),
            in_specs=[vmem, vmem, pl.BlockSpec(memory_space=pl.ANY)],
            out_specs=vmem,
        ),
        out_shape=jax.ShapeDtypeStruct(mine.shape, BF16),
        compiler_params=pltpu.CompilerParams(vmem_limit_bytes=VMEM),
        cost_estimate=TINY,
        name="add_cores_placed",
    )(where, theirs, mine, token)


def exchange_sum(pieces, token=None):
    got = lax.all_to_all(pieces, "context", split_axis=0, concat_axis=0, tiled=True)
    if token is not None:
        got = after_call(got, token)
    return jnp.sum(got.astype(F32), axis=0)


def add_kernel(theirs_ref, mine_ref, token_ref, *out_refs):
    for k, out_ref in enumerate(out_refs):
        out_ref[...] = (theirs_ref[k].astype(F32) + mine_ref[k].astype(F32)).astype(BF16)


def add_call(theirs, mine, token):
    shape = theirs.shape
    one = jax.ShapeDtypeStruct(shape[1:], BF16)
    vmem = pl.BlockSpec(memory_space=pltpu.VMEM)
    return pl.pallas_call(
        add_kernel,
        in_specs=[vmem, vmem, pl.BlockSpec(memory_space=pl.ANY)],
        out_specs=[vmem] * shape[0],
        out_shape=[one] * shape[0],
        compiler_params=pltpu.CompilerParams(vmem_limit_bytes=VMEM),
        cost_estimate=TINY,
        name="add_cores",
    )(theirs, mine, token)


def gate_up_down_kernel(part, in_ref, gate_ref, up_ref, down_ref):
    last = in_ref.shape[2]
    count = in_ref.shape[0] * part
    gate_ref[...] = in_ref[:, :part].reshape(count, last).astype(F32).T
    up_ref[...] = in_ref[:, part : 2 * part].reshape(count, last).astype(F32).T
    down_ref[...] = in_ref[:, 2 * part :].reshape(count, last).astype(F32)


def gate_up_down_call(gathered, part):
    members, depth, width = gathered.shape
    ff = members * part
    n = 8
    step = width // n
    return pl.pallas_call(
        functools.partial(gate_up_down_kernel, part),
        grid=(n,),
        in_specs=[pl.BlockSpec((members, depth, step), lambda c: (0, 0, c))],
        out_specs=[
            pl.BlockSpec((step, ff), lambda c: (c, 0)),
            pl.BlockSpec((step, ff), lambda c: (c, 0)),
            pl.BlockSpec((ff, step), lambda c: (0, c)),
        ],
        out_shape=[
            jax.ShapeDtypeStruct((width, ff), F32),
            jax.ShapeDtypeStruct((width, ff), F32),
            jax.ShapeDtypeStruct((ff, width), F32),
        ],
        compiler_params=pltpu.CompilerParams(vmem_limit_bytes=VMEM),
        cost_estimate=TINY,
        name="experts_results",
    )(gathered)


def out_grads_kernel(heads_ref, mine_ref, theirs_ref, out_ref):
    total = outer(heads_ref[0], mine_ref[...]) + outer(heads_ref[1], theirs_ref[...])
    out_ref[...] = total.astype(BF16)


def out_grads_call(heads_out, mine, theirs):
    _, half, columns = heads_out.shape
    width = mine.shape[1]
    n = 4
    spec = pl.BlockSpec((half, width // n), lambda c: (0, c))
    return pl.pallas_call(
        out_grads_kernel,
        grid=(n,),
        in_specs=[pl.BlockSpec(heads_out.shape, lambda c: (0, 0, 0)), spec, spec],
        out_specs=pl.BlockSpec((columns, width // n), lambda c: (0, c)),
        out_shape=jax.ShapeDtypeStruct((columns, width), BF16),
        compiler_params=pltpu.CompilerParams(vmem_limit_bytes=VMEM),
        cost_estimate=TINY,
        name="out_weights",
    )(heads_out, mine, theirs)


def attend_grads_kernel(
    cut, place_ref, h1_ref, d_qkv_ref, out_ref, gains_ref, token_ref, *refs
):
    firsts, seconds, share = refs[:SIDE], refs[SIDE : 2 * SIDE], refs[-1]
    step = pl.program_id(0)
    last = d_qkv_ref.shape[1]
    depth = share.shape[1] - 16
    grad = outer(h1_ref[...], d_qkv_ref[...]).astype(BF16)
    share[:, :depth, :last] = grad.reshape(SIDE, depth, last)
    rows, columns = out_ref.shape[1], share.shape[2] - last
    for k in range(depth // rows):
        share[:, k * rows : (k + 1) * rows, last:] = out_ref[:, :, k * columns : (k + 1) * columns]
    share[:, depth:] = gains_ref[...]
    for k in range(SIDE):

        @pl.when(step == k)
        def _():
            firsts[k][...] = share[:, :cut]

        seconds[k][0] = share[lax.rem(place_ref[1] + k, SIDE), cut:]


def attend_grads_call(place, h1, d_qkv, grad_out, gains, token, cut):
    rows, width = h1.shape
    owners, extra, columns = gains.shape
    depth = width // owners
    last = d_qkv.shape[1]

    def at(i, place):
        return lax.rem(place[0] + i, SIDE)

    first = jax.ShapeDtypeStruct((SIDE, cut, columns), BF16)
    second = jax.ShapeDtypeStruct((SIDE, depth + extra - cut, columns), BF16)
    outs = pl.pallas_call(
        functools.partial(attend_grads_kernel, cut),
        grid_spec=pltpu.PrefetchScalarGridSpec(
            num_scalar_prefetch=1,
            grid=(SIDE,),
            in_specs=[
                pl.BlockSpec((rows, width // SIDE), lambda i, place: (0, at(i, place))),
                pl.BlockSpec((rows, last), lambda i, place: (0, 0)),
                pl.BlockSpec((SIDE,) + grad_out.shape[1:], lambda i, place: (at(i, place), 0, 0)),
                pl.BlockSpec((SIDE, extra, columns), lambda i, place: (at(i, place), 0, 0)),
                pl.BlockSpec(memory_space=pl.ANY),
            ],
            out_specs=[pl.BlockSpec(first.shape, lambda i, place: (0, 0, 0))] * SIDE
            + [pl.BlockSpec((1,) + second.shape[1:], lambda i, place: (i, 0, 0))] * SIDE,
            scratch_shapes=[pltpu.VMEM((SIDE, depth + extra, columns), BF16)],
        ),
        out_shape=[first] * SIDE + [second] * SIDE,
        compiler_params=pltpu.CompilerParams(vmem_limit_bytes=VMEM),
        cost_estimate=TINY,
        name="attention_weights",
    )(place, h1, d_qkv, grad_out, gains, token)
    return outs[:SIDE], outs[SIDE:]


def total_of(refs):
    total = refs[0][...].astype(F32)
    for ref in refs[1:]:
        total = total + ref[...].astype(F32)
    return total.astype(BF16)


def half_sum_kernel(place_ref, *refs):
    outs, total = refs[2 * SIDE + 1 : -1], refs[-1]
    firsts, seconds = outs[:SIDE], outs[SIDE:]
    total[...] = total_of(refs[:SIDE])
    other = total_of(refs[SIDE : 2 * SIDE])
    for k in range(SIDE):
        firsts[k][...] = total[lax.rem(place_ref[1] + k, SIDE)]
        seconds[k][...] = other[k]


def half_sum_call(place, firsts, seconds, token):
    vmem = pl.BlockSpec(memory_space=pltpu.VMEM)
    outs = pl.pallas_call(
        half_sum_kernel,
        grid_spec=pltpu.PrefetchScalarGridSpec(
            num_scalar_prefetch=1,
            grid=(),
            in_specs=[vmem] * (2 * SIDE) + [pl.BlockSpec(memory_space=pl.ANY)],
            out_specs=[vmem] * (2 * SIDE),
            scratch_shapes=[pltpu.VMEM(firsts[0].shape, BF16)],
        ),
        out_shape=[jax.ShapeDtypeStruct(v.shape[1:], BF16) for v in (*firsts, *seconds)],
        compiler_params=pltpu.CompilerParams(vmem_limit_bytes=VMEM),
        cost_estimate=TINY,
        name="half_sum",
    )(place, *firsts, *seconds, token)
    return outs[:SIDE], outs[SIDE:]


def last_sum_kernel(token_ref, *refs):
    out = refs[-1]
    cut = refs[0].shape[0]
    out[:cut] = total_of(refs[:SIDE])
    out[cut:] = total_of(refs[SIDE : 2 * SIDE])


def last_sum_call(firsts, seconds, token):
    rows, columns = firsts[0].shape[0] + seconds[0].shape[0], firsts[0].shape[1]
    vmem = pl.BlockSpec(memory_space=pltpu.VMEM)
    return pl.pallas_call(
        last_sum_kernel,
        in_specs=[pl.BlockSpec(memory_space=pl.ANY)] + [vmem] * (2 * SIDE),
        out_specs=vmem,
        out_shape=jax.ShapeDtypeStruct((rows, columns), BF16),
        compiler_params=pltpu.CompilerParams(vmem_limit_bytes=VMEM),
        cost_estimate=TINY,
        name="last_sum",
    )(token, *firsts, *seconds)


def plane_send(pieces, dx, dz):
    return [pieces[0]] + [plane(pieces[k], -k * dx, -k * dz) for k in range(1, SIDE)]


def columns_kernel(heads_width, size, where_ref, mine_ref, theirs_ref, q_ref, k_ref, v_ref, sum_ref):
    depth = q_ref.shape[0]
    mine, theirs = mine_ref[0].astype(F32), theirs_ref[0].astype(F32)
    first = where_ref[1] == 0
    q_ref[:, :heads_width] = jnp.where(first, mine[:depth, :heads_width], theirs[:depth, :heads_width])
    q_ref[:, heads_width:] = jnp.where(first, theirs[:depth, :heads_width], mine[:depth, :heads_width])
    both = mine + theirs
    k_ref[...] = both[:depth, heads_width : heads_width + size]
    v_ref[...] = both[:depth, heads_width + size :]

    @pl.when(pl.program_id(0) == 0)
    def _():
        sum_ref[...] = jnp.zeros_like(sum_ref)

    sum_ref[...] += both[depth:]


def columns_call(where, mine, theirs, depth, heads_width, size):
    ring, rows, last = mine.shape
    cores = 2

    def at(k, where):
        return (0, lax.rem(where[0] + k, ring))

    return pl.pallas_call(
        functools.partial(columns_kernel, heads_width, size),
        grid_spec=pltpu.PrefetchScalarGridSpec(
            num_scalar_prefetch=1,
            grid=(ring,),
            in_specs=[pl.BlockSpec((1, rows, last), lambda k, where: (k, 0, 0))] * 2,
            out_specs=[
                pl.BlockSpec((depth, cores * heads_width), at),
                pl.BlockSpec((depth, size), at),
                pl.BlockSpec((depth, size), at),
                pl.BlockSpec((rows - depth, last), lambda k, where: (0, 0)),
            ],
        ),
        out_shape=[
            jax.ShapeDtypeStruct((depth, ring * cores * heads_width), F32),
            jax.ShapeDtypeStruct((depth, ring * size), F32),
            jax.ShapeDtypeStruct((depth, ring * size), F32),
            jax.ShapeDtypeStruct((rows - depth, last), F32),
        ],
        compiler_params=pltpu.CompilerParams(vmem_limit_bytes=VMEM),
        cost_estimate=TINY,
        name="columns_results",
    )(where, mine, theirs)


def rows_kernel(where_ref, mine_ref, theirs_ref, out_ref):
    count = mine_ref.shape[1]
    mine, theirs = mine_ref[0].astype(F32), theirs_ref[0].astype(F32)
    first = where_ref[1] == 0
    out_ref[:count] = jnp.where(first, mine, theirs)
    out_ref[count:] = jnp.where(first, theirs, mine)


def rows_call(where, mine, theirs):
    ring, count, width = mine.shape
    cores = 2
    return pl.pallas_call(
        rows_kernel,
        grid_spec=pltpu.PrefetchScalarGridSpec(
            num_scalar_prefetch=1,
            grid=(ring,),
            in_specs=[pl.BlockSpec((1, count, width), lambda k, where: (k, 0, 0))] * 2,
            out_specs=pl.BlockSpec(
                (cores * count, width), lambda k, where: (lax.rem(where[0] + k, ring), 0)
            ),
        ),
        out_shape=jax.ShapeDtypeStruct((ring * cores * count, width), F32),
        compiler_params=pltpu.CompilerParams(vmem_limit_bytes=VMEM),
        cost_estimate=TINY,
        name="rows_results",
    )(where, mine, theirs)


def expert_out_kernel(part, hid_ref, w_ref, token_ref, theirs_ref, mine_ref):
    width = w_ref.shape[2]
    block = pl.program_id(0)
    total = matmul(hid_ref[...], w_ref[...].reshape(w_ref.shape[0] * part, width)).astype(BF16)

    @pl.when(block < 2)
    def _():
        theirs_ref[...] = total

    @pl.when(block >= 2)
    def _():
        mine_ref[...] = total


def expert_out_call(hidden, weights, token, part):
    rows, wide = hidden.shape
    owners, _, width = weights.shape
    blocks = 4
    step = rows // blocks
    half = jax.ShapeDtypeStruct((rows // 2, width), BF16)
    return pl.pallas_call(
        functools.partial(expert_out_kernel, part),
        grid=(blocks,),
        in_specs=[
            pl.BlockSpec((step, wide), lambda b: ((b + blocks // 2) % blocks, 0)),
            pl.BlockSpec((owners, part, width), lambda b: (0, 2, 0)),
            pl.BlockSpec(memory_space=pl.ANY),
        ],
        out_specs=[
            pl.BlockSpec((step, width), lambda b: (jnp.minimum(b, 1), 0)),
            pl.BlockSpec((step, width), lambda b: (jnp.maximum(b - 2, 0), 0)),
        ],
        out_shape=[half, half],
        compiler_params=pltpu.CompilerParams(vmem_limit_bytes=VMEM),
        cost_estimate=pl.CostEstimate(
            flops=2 * rows * wide * width, bytes_accessed=20_000_000, transcendentals=0
        ),
        name="experts_out",
    )(hidden, weights, token)


def local(
    tokens,
    lengths,
    routes,
    mix_weights,
    cotangent,
    w_query,
    key_weight,
    value_weight,
    w_out,
    norm_attn,
    norm_moe,
    norm_query,
    norm_key,
    w_gate,
    w_up,
    w_down,
):
    owners = lax.axis_size("experts")
    ring = lax.axis_size("context")
    cores = lax.axis_size("dp")
    members = ring * cores
    y = lax.axis_index("context")
    d = lax.axis_index("dp")
    j = y * cores + d
    micro, _, row_count, width = tokens.shape
    head = norm_query.shape[0] * owners
    q_width = w_query.shape[1] // members
    q_heads = q_width // head
    depth = w_query.shape[0]
    ff = w_gate.shape[2]
    ff_part = ff // members
    out_rows = w_out.shape[0]
    out_part = out_rows // members
    seqs = cores * micro
    span = ring * row_count
    rows = seqs * span
    scale = head ** (-0.5)

    forth = [
        (es * members + k, ((es % cores) * members + k) * members + es // cores)
        for es in range(owners)
        for k in range(members)
    ]
    back = [(b, a) for a, b in forth]
    out_chunk = lax.ppermute(
        lax.dynamic_slice_in_dim(w_out, j * out_part, out_part, axis=0), EVERY, forth
    )
    expert_pack = jnp.concatenate(
        [
            lax.dynamic_slice_in_dim(w_gate[0], j * ff_part, ff_part, axis=1).T,
            lax.dynamic_slice_in_dim(w_up[0], j * ff_part, ff_part, axis=1).T,
            lax.dynamic_slice_in_dim(w_down[0], j * ff_part, ff_part, axis=0),
        ],
        axis=0,
    )
    gains = jnp.concatenate([norm_attn, norm_moe, norm_query, norm_key])
    packed = jnp.concatenate(
        [
            lax.dynamic_slice_in_dim(w_query, j * q_width, q_width, axis=1),
            lax.dynamic_slice_in_dim(key_weight, y * head, head, axis=1),
            lax.dynamic_slice_in_dim(value_weight, y * head, head, axis=1),
            jnp.concatenate(jnp.split(out_chunk, depth // out_part, axis=1), axis=0),
        ],
        axis=1,
    )
    qkv_width = q_width + 2 * head
    gain_rows = jnp.pad(gains[None], ((0, 15), (0, packed.shape[1] - gains.shape[0])))
    shared = lax.all_gather(
        jnp.concatenate([packed, gain_rows]), "experts", axis=0, tiled=False
    )
    expert_all = lax.all_gather(expert_pack, "experts", axis=0, tiled=False)
    gain_row = shared[:, depth]
    gain_row = gain_row.astype(F32)
    gain_attn = gain_row[:, :depth].reshape(-1)
    gain_moe = gain_row[:, depth : 2 * depth].reshape(-1)
    eighth = norm_query.shape[0]
    gain_query = gain_row[:, 2 * depth : 2 * depth + eighth].reshape(-1)
    gain_key = gain_row[:, 2 * depth + eighth : 2 * depth + 2 * eighth].reshape(-1)
    hidden_width = owners * ff_part

    where = jnp.stack([y, d]).astype(jnp.int32)
    x_own = tokens[:, 0]
    x_rows = gather_rows(x_own, ring)
    len_all = jnp.stack([lengths[:, 0], swap(lengths[:, 0])]).reshape(seqs)
    own_pos = y * row_count + jnp.arange(row_count, dtype=jnp.int32)
    valid = (own_pos[None, :] < lengths[:, 0][:, None]).astype(F32)
    dy_own = (cotangent[:, 0].astype(F32) * valid[:, :, None]).astype(BF16)
    ids = jnp.arange(owners, dtype=jnp.int32)
    mix_own = jnp.sum(
        jnp.where(routes[:, 0][..., None] == ids, mix_weights[:, 0][..., None], 0.0), axis=2
    )
    mix_high = mix_own.astype(BF16)
    mix_low = (mix_own - mix_high.astype(F32)).astype(BF16)
    lanes = 128
    mix_pad = jnp.zeros((micro, row_count, lanes - 2 * owners), BF16)
    dy_mix = gather_rows(jnp.concatenate([dy_own, mix_high, mix_low, mix_pad], axis=-1), ring)
    dy_mix = dy_mix.reshape(rows, width + lanes)
    lane = jnp.arange(lanes, dtype=jnp.int32)
    spread = (
        (jnp.arange(hidden_width, dtype=jnp.int32)[None, :] // ff_part == (lane % owners)[:, None])
        & (lane < 2 * owners)[:, None]
    ).astype(BF16)

    k_index = jnp.arange(span, dtype=jnp.int32)
    pos = ((y + k_index // row_count) % ring) * row_count + k_index % row_count
    frequency = ROPE_BASE ** (-jnp.arange(head // 2, dtype=F32) * 2.0 / head)
    phase = pos.astype(F32)[:, None] * frequency[None, :]
    cosines, sines = jnp.cos(phase), jnp.sin(phase)
    cosines = jnp.concatenate([cosines, cosines], axis=1)
    sines = jnp.concatenate([-sines, sines], axis=1)
    allowed = (pos[None, None, :] <= pos[None, :, None]) & (
        pos[None, None, :] < len_all[:, None, None]
    )
    bias = jnp.where(allowed, 0.0, -1e30).astype(F32)

    shape = (ring, micro, row_count, width)
    head_gains = (gain_query[None], gain_key[None])
    h1, qkv, heads_out, theirs, mine = attend_call(
        functools.partial(attend_kernel, q_heads, scale),
        (x_rows, gain_attn[None], shared, cosines, sines, bias, *head_gains, dy_mix),
        ("rows", "", "", "", "", "bias", "", "", "token"),
        (
            ("rows", width, BF16),
            ("rows", qkv_width, F32),
            ("rows", q_width, BF16),
            ("parts", width, BF16),
        ),
        [pltpu.VMEM((span, q_width), BF16), pltpu.VMEM((span, width), BF16)],
        shape,
        "attention",
        TINY,
    )
    attn_own = scatter_rows(theirs[0], mine[0])
    x1 = x_own.astype(F32) + attn_own
    inverse_mid = inverse_rms(x1)
    h2 = gather_rows((x1 * inverse_mid * gain_moe).astype(BF16), ring).reshape(rows, width)

    d_gate, d_up, hidden, theirs, mine = experts_call(h2, dy_mix, expert_all, spread, ff_part)
    grad_experts, token = expert_grads_call(
        d_gate, d_up, hidden, h2, dy_mix, owners, ff_part
    )
    pieces = add_call(swap(theirs.reshape(shape)), mine.reshape(shape), token)
    d_h2 = ring_sum(pieces)
    moe_theirs, moe_mine = expert_out_call(hidden, expert_all, token, ff_part)

    grad_gain_moe = jnp.sum(d_h2 * x1 * inverse_mid, axis=(0, 1))
    d_x1 = dy_own.astype(F32) + norm_back(d_h2, x1, inverse_mid, gain_moe)
    grad_experts = lax.psum_scatter(
        after_call(grad_experts, pieces[1]), "experts", scatter_dimension=0, tiled=False
    )
    moe_pieces = add_placed_call(
        where, swap(moe_theirs.reshape(shape)), moe_mine.reshape(shape), hidden
    )
    d_mine = after_call(ring_stack(d_x1.astype(BF16), ring), moe_pieces)
    d_theirs = swap(d_mine)
    grad_out = out_grads_call(
        heads_out.reshape(2, rows // 2, q_width),
        d_mine.reshape(-1, width),
        d_theirs.reshape(-1, width),
    )
    grad_out = grad_out.reshape(owners, out_part, width)
    d_qkv, theirs, mine, sum_q, sum_k, sum_x = attend_call(
        functools.partial(attend_back_kernel, q_heads, scale),
        (
            d_theirs[None],
            d_mine[None],
            x_rows,
            gain_attn[None],
            shared,
            cosines,
            sines,
            bias,
            *head_gains,
            qkv,
            moe_pieces,
            grad_out,
        ),
        (
            "theirs",
            "mine",
            "rows",
            "",
            "",
            "",
            "",
            "bias",
            "",
            "",
            "rows",
            "token",
            "token",
        ),
        (
            ("rows", qkv_width, BF16),
            ("parts", width, BF16),
            ("sum", head, F32),
            ("sum", head, F32),
            ("sum", width, F32),
        ),
        [pltpu.VMEM((span, qkv_width), BF16)],
        shape,
        "attention_back",
        pl.CostEstimate(flops=9_000_000_000, bytes_accessed=90_000_000, transcendentals=0),
    )
    output = (x1 + exchange_sum(moe_pieces, d_qkv)).astype(BF16)[:, None]
    grad_gain_query, grad_gain_key, grad_gain_attn = sum_q[0], sum_k[0], sum_x[0]
    h1, d_qkv = h1.reshape(rows, width), d_qkv.reshape(rows, qkv_width)

    grad_gains = jnp.concatenate(
        [
            grad_gain_attn.reshape(owners, depth),
            grad_gain_moe.reshape(owners, depth),
            grad_gain_query.reshape(owners, eighth),
            grad_gain_key.reshape(owners, eighth),
        ],
        axis=1,
    ).astype(BF16)
    grad_gains = jnp.pad(
        grad_gains[:, None], ((0, 0), (0, 15), (0, shared.shape[2] - grad_gains.shape[1]))
    )
    index = lax.axis_index("experts")
    place = jnp.stack([index // SIDE, index % SIDE]).astype(jnp.int32)
    firsts, seconds = attend_grads_call(
        place, h1, d_qkv, grad_out, grad_gains, output, depth // 2 + 16
    )
    h1_pieces = add_placed_call(where, swap(theirs[0]), mine[0], firsts[1])
    d_h1 = exchange_sum(h1_pieces)
    x_f32 = x_own.astype(F32)
    input_grad = (d_x1 + norm_back(d_h1, x_f32, inverse_rms(x_f32), gain_attn))[:, None]
    grad_experts = after_call(grad_experts, h1_pieces)
    all_experts = lax.all_gather(grad_experts, GROUP, axis=0, tiled=False)
    firsts, seconds = plane_send(firsts, 1, 0), plane_send(seconds, 0, 1)
    firsts, seconds = half_sum_call(place, firsts, seconds, grad_out)
    result_gate, result_up, result_down = gate_up_down_call(all_experts, ff_part)
    grads = last_sum_call(plane_send(firsts, 0, 1), plane_send(seconds, 1, 0), d_h1)
    out_sum = jnp.concatenate(
        [grads[k * out_part : (k + 1) * out_part, qkv_width:] for k in range(depth // out_part)],
        axis=1,
    )
    result_q, result_k, result_v, gain_sum = columns_call(
        where, *gather_members(grads[:, :qkv_width]), depth, q_width, head
    )
    out_sum = after_call(lax.ppermute(out_sum, EVERY, back), input_grad, result_down)
    result_out = rows_call(where, *gather_members(out_sum))
    gain_sum = gain_sum[0]
    return (
        output,
        input_grad,
        result_q,
        result_k,
        result_v,
        result_out,
        gain_sum[:depth],
        gain_sum[depth : 2 * depth],
        gain_sum[2 * depth : 2 * depth + eighth],
        gain_sum[2 * depth + eighth : 2 * depth + 2 * eighth],
        result_gate[None],
        result_up[None],
        result_down[None],
    )


def solution(mesh):
    rows = P(None, ("experts", "dp"), "context", None)
    in_specs = (
        rows,
        P(None, ("experts", "dp")),
        rows,
        rows,
        rows,
        P("experts", None),
        P("experts", None),
        P("experts", None),
        P("experts", None),
        P("experts"),
        P("experts"),
        P("experts"),
        P("experts"),
        P("experts", None, None),
        P("experts", None, None),
        P("experts", None, None),
    )
    out_specs = (
        rows,
        rows,
        P("experts", None),
        P("experts", None),
        P("experts", None),
        P("experts", None),
        P("experts"),
        P("experts"),
        P("experts"),
        P("experts"),
        P("experts", None, None),
        P("experts", None, None),
        P("experts", None, None),
    )
    return jax.shard_map(local, mesh=mesh, in_specs=in_specs, out_specs=out_specs, check_vma=False)
```

```python
import functools

import jax
import jax.numpy as jnp
from jax import lax
from jax.experimental import pallas as pl
from jax.experimental.pallas import tpu as pltpu
from jax.sharding import PartitionSpec as P

EPS = 1e-06
ROPE_BASE = 1000000.0
F32 = jnp.float32
BF16 = jnp.bfloat16
GROUP = ("context", "dp")
EVERY = ("experts", "context", "dp")
VMEM = 60 * 1024 * 1024
SIDE = 4
TINY = pl.CostEstimate(flops=0, bytes_accessed=1000, transcendentals=0)


def inverse_rms(v):
    return lax.rsqrt(jnp.mean(v * v, axis=-1, keepdims=True) + EPS)


def norm_back(grad_in, v, inverse, gain):
    scaled = grad_in * gain
    return inverse * scaled - v * inverse**3 * jnp.mean(scaled * v, axis=-1, keepdims=True)


def matmul(left, right):
    return jnp.dot(left, right, preferred_element_type=F32)


def against(left, right):
    return lax.dot_general(left, right, (((1,), (1,)), ((), ())), preferred_element_type=F32)


def outer(left, right):
    return lax.dot_general(left, right, (((0,), (0,)), ((), ())), preferred_element_type=F32)


def swap(v):
    return lax.ppermute(v, "dp", [(0, 1), (1, 0)])


def ring_stack(own, ring):
    pieces = [own]
    for k in range(1, ring):
        pieces.append(lax.ppermute(own, "context", [((i + k) % ring, i) for i in range(ring)]))
    return jnp.stack(pieces)


def gather_rows(own, ring):
    mine = ring_stack(own, ring)
    return jnp.stack([mine, swap(mine)])


def ring_sum(pieces):
    ring = len(pieces)
    total = pieces[0].astype(F32)
    for k in range(1, ring):
        got = lax.ppermute(pieces[k], "context", [(i, (i + k) % ring) for i in range(ring)])
        total = total + got.astype(F32)
    return total


def add_cores(theirs, mine):
    other = swap(theirs)
    return [
        (mine[k].astype(F32) + other[k].astype(F32)).astype(BF16) for k in range(mine.shape[0])
    ]


def scatter_rows(theirs, mine):
    return ring_sum(add_cores(theirs, mine))


def gather_members(v, *tokens):
    ring = lax.axis_size("context")
    pieces = [after_call(v, *tokens) if tokens else v]
    for k in range(1, ring):
        pieces.append(lax.ppermute(v, "context", [((i + k) % ring, i) for i in range(ring)]))
    mine = jnp.stack(pieces)
    return mine, swap(mine)


def plane(v, dx, dz):
    moves = [
        (((i // SIDE + dx) % SIDE) * SIDE + (i % SIDE + dz) % SIDE, i) for i in range(SIDE * SIDE)
    ]
    return lax.ppermute(v, "experts", moves)


def after_kernel(v_ref, *refs):
    pass


def after_call(v, *tokens):
    anywhere = pl.BlockSpec(memory_space=pl.ANY)
    return pl.pallas_call(
        after_kernel,
        in_specs=[anywhere] * (1 + len(tokens)),
        out_specs=anywhere,
        out_shape=jax.ShapeDtypeStruct(v.shape, v.dtype),
        input_output_aliases={0: 0},
        cost_estimate=TINY,
        name="after",
    )(v, *tokens)


def rope(v, cosines, sines):
    return v * cosines + pltpu.roll(v, v.shape[-1] // 2, 1) * sines


def rope_back(v, cosines, sines):
    return v * cosines + pltpu.roll(v * sines, v.shape[-1] // 2, 1)


def flat(ref):
    v = ref[...]
    return v.reshape(v.shape[1] * v.shape[3], v.shape[4])


def chunks(ref, columns):
    v = ref[:, :-16, :columns]
    return v.reshape(v.shape[0] * v.shape[1], columns)


def out_blocks(ref, first):
    last = ref.shape[2] - first
    rows = last // ref.shape[0]
    for k in range((ref.shape[1] - 16) // rows):
        yield k * last, (k + 1) * last, ref[:, k * rows : (k + 1) * rows, first:].reshape(last, last)


def put(ref, v):
    ref[...] = v.reshape(ref.shape).astype(ref.dtype)


def attend_kernel(
    heads,
    scale,
    x_ref,
    gain_ref,
    w_ref,
    cos_ref,
    sin_ref,
    bias_ref,
    gain_q_ref,
    gain_k_ref,
    token_ref,
    h1_ref,
    qkv_ref,
    heads_ref,
    theirs_ref,
    mine_ref,
    heads_out,
    total,
):
    size = cos_ref.shape[1]
    x = flat(x_ref).astype(F32)
    h1 = (x * inverse_rms(x) * gain_ref[...]).astype(BF16)
    put(h1_ref, h1)
    width = (heads + 2) * size
    qkv = matmul(h1, chunks(w_ref, width))
    put(qkv_ref, qkv)
    cosines, sines, bias = cos_ref[...], sin_ref[...], bias_ref[0]
    k_pre = qkv[:, heads * size : (heads + 1) * size]
    key = rope(k_pre * inverse_rms(k_pre) * gain_k_ref[...], cosines, sines).astype(BF16)
    value = qkv[:, (heads + 1) * size :].astype(BF16)
    for g in range(heads):
        q_pre = qkv[:, g * size : (g + 1) * size]
        query = rope(q_pre * inverse_rms(q_pre) * gain_q_ref[...], cosines, sines).astype(BF16)
        logits = against(query, key) * scale + bias
        scaled = jnp.exp(logits - jnp.max(logits, axis=-1, keepdims=True))
        soft = (scaled * (1.0 / jnp.sum(scaled, axis=-1, keepdims=True))).astype(BF16)
        heads_out[:, g * size : (g + 1) * size] = matmul(soft, value).astype(BF16)
    out = heads_out[...]
    put(heads_ref, out)
    for first, last, block in out_blocks(w_ref, width):
        total[:, first:last] = matmul(out, block).astype(BF16)

    @pl.when(pl.program_id(0) < 2)
    def _():
        put(theirs_ref, total[...])

    @pl.when(pl.program_id(0) >= 2)
    def _():
        put(mine_ref, total[...])


def attend_back_kernel(
    heads,
    scale,
    theirs_da_ref,
    mine_da_ref,
    x_ref,
    gain_ref,
    w_ref,
    cos_ref,
    sin_ref,
    bias_ref,
    gain_q_ref,
    gain_k_ref,
    qkv_ref,
    token_ref,
    other_token_ref,
    d_qkv_ref,
    theirs_ref,
    mine_ref,
    sum_q_ref,
    sum_k_ref,
    sum_x_ref,
    d_qkv,
):
    size = cos_ref.shape[1]
    step = pl.program_id(0)

    @pl.when(step == 0)
    def _():
        sum_q_ref[...] = jnp.zeros_like(sum_q_ref)
        sum_k_ref[...] = jnp.zeros_like(sum_k_ref)
        sum_x_ref[...] = jnp.zeros_like(sum_x_ref)

    width = (heads + 2) * size
    da = jnp.where(step < 2, flat(theirs_da_ref), flat(mine_da_ref))
    d_heads = None
    for first, last, block in out_blocks(w_ref, width):
        piece = against(da[:, first:last], block)
        d_heads = piece if d_heads is None else d_heads + piece
    d_heads = d_heads.astype(BF16)
    qkv = flat(qkv_ref)
    cosines, sines, bias = cos_ref[...], sin_ref[...], bias_ref[0]
    gain_q, gain_k = gain_q_ref[...], gain_k_ref[...]
    k_pre = qkv[:, heads * size : (heads + 1) * size]
    inverse_k = inverse_rms(k_pre)
    key = rope(k_pre * inverse_k * gain_k, cosines, sines).astype(BF16)
    value = qkv[:, (heads + 1) * size :].astype(BF16)
    d_key = jnp.zeros(k_pre.shape, F32)
    d_value = jnp.zeros(k_pre.shape, F32)
    sum_q = jnp.zeros((1, size), F32)
    for g in range(heads):
        q_pre = qkv[:, g * size : (g + 1) * size]
        inverse_q = inverse_rms(q_pre)
        query = rope(q_pre * inverse_q * gain_q, cosines, sines).astype(BF16)
        logits = against(query, key) * scale + bias
        scaled = jnp.exp(logits - jnp.max(logits, axis=-1, keepdims=True))
        probs = scaled * (1.0 / jnp.sum(scaled, axis=-1, keepdims=True))
        d_head = d_heads[:, g * size : (g + 1) * size]
        d_probs = against(d_head, value)
        d_scores = probs * (d_probs - jnp.sum(probs * d_probs, axis=-1, keepdims=True))
        d_scores = d_scores.astype(BF16)
        d_query = rope_back(matmul(d_scores, key) * scale, cosines, sines)
        d_key = d_key + outer(d_scores, query)
        d_value = d_value + outer(probs.astype(BF16), d_head)
        sum_q = sum_q + jnp.sum(d_query * q_pre * inverse_q, axis=0, keepdims=True)
        d_qkv[:, g * size : (g + 1) * size] = norm_back(d_query, q_pre, inverse_q, gain_q).astype(
            BF16
        )
    d_key = rope_back(d_key * scale, cosines, sines)
    sum_k = jnp.sum(d_key * k_pre * inverse_k, axis=0, keepdims=True)
    d_qkv[:, heads * size : (heads + 1) * size] = norm_back(d_key, k_pre, inverse_k, gain_k).astype(
        BF16
    )
    d_qkv[:, (heads + 1) * size :] = d_value.astype(BF16)
    grads = d_qkv[...]
    put(d_qkv_ref, grads)
    part = against(grads, chunks(w_ref, width))
    x = flat(x_ref).astype(F32)
    sum_x_ref[0:1, :] += jnp.sum(part * (x * inverse_rms(x)), axis=0, keepdims=True)
    sum_q_ref[0:1, :] += sum_q
    sum_k_ref[0:1, :] += sum_k

    @pl.when(step < 2)
    def _():
        put(theirs_ref, part)

    @pl.when(step >= 2)
    def _():
        put(mine_ref, part)


def attend_call(kernel, operands, extra, outputs, scratch, shape, name, cost):
    ring, micro, row_count, width = shape

    def rows_spec(last):
        return pl.BlockSpec(
            (1, ring, 1, row_count, last), lambda b: (1 - b // 2, 0, b % 2, 0, 0)
        )

    def whole(v):
        return pl.BlockSpec(v.shape, lambda b: (0,) * v.ndim)

    def slot_spec(v, kind):
        block = (1, ring, 1, row_count, v.shape[-1])
        if kind == "theirs":
            return pl.BlockSpec(block, lambda b: (0, 0, jnp.minimum(b, 1), 0, 0))
        return pl.BlockSpec(block, lambda b: (0, 0, jnp.maximum(b - 2, 0), 0, 0))

    in_specs = [
        rows_spec(v.shape[-1])
        if kind == "rows"
        else slot_spec(v, kind)
        if kind in ("theirs", "mine")
        else pl.BlockSpec((1,) + v.shape[1:], lambda b: ((1 - b // 2) * micro + b % 2, 0, 0))
        if kind == "bias"
        else pl.BlockSpec(memory_space=pl.ANY)
        if kind == "token"
        else whole(v)
        for v, kind in zip(operands, extra)
    ]
    out_shape, out_specs = [], []
    for kind, last, dtype in outputs:
        if kind == "rows":
            out_shape.append(jax.ShapeDtypeStruct((2, ring, micro, row_count, last), dtype))
            out_specs.append(rows_spec(last))
        elif kind == "parts":
            one = jax.ShapeDtypeStruct((1, ring, micro, row_count, last), dtype)
            out_shape += [one, one]
            block = (1, ring, 1, row_count, last)
            out_specs.append(pl.BlockSpec(block, lambda b: (0, 0, jnp.minimum(b, 1), 0, 0)))
            out_specs.append(pl.BlockSpec(block, lambda b: (0, 0, jnp.maximum(b - 2, 0), 0, 0)))
        else:
            out_shape.append(jax.ShapeDtypeStruct((8, last), dtype))
            out_specs.append(pl.BlockSpec((8, last), lambda b: (0, 0)))
    return pl.pallas_call(
        kernel,
        grid=(2 * micro,),
        in_specs=in_specs,
        out_specs=out_specs,
        out_shape=out_shape,
        scratch_shapes=scratch,
        compiler_params=pltpu.CompilerParams(vmem_limit_bytes=VMEM),
        cost_estimate=cost,
        name=name,
    )(*operands)


def experts_kernel(
    part, h2_ref, dy_ref, w_ref, spread_ref, dg_ref, du_ref, hid_ref, theirs_ref, mine_ref, acc
):
    chunk, block = pl.program_id(0), pl.program_id(1)
    width = h2_ref.shape[1]
    count = w_ref.shape[0] * part
    gate_w = w_ref[:, :part].reshape(count, width)
    up_w = w_ref[:, part : 2 * part].reshape(count, width)
    down_w = w_ref[:, 2 * part :].reshape(count, width)
    h2 = h2_ref[...]
    mix = matmul(dy_ref[:, width:], spread_ref[...])
    gate = against(h2, gate_w)
    up = against(h2, up_w)
    d_hidden = against(dy_ref[:, :width], down_w) * mix
    sigma = jax.nn.sigmoid(gate)
    silu = gate * sigma
    hid_ref[...] = (silu * up * mix).astype(BF16)
    d_gate = (d_hidden * up * sigma * (1.0 + gate * (1.0 - sigma))).astype(BF16)
    d_up = (d_hidden * silu).astype(BF16)
    dg_ref[...] = d_gate
    du_ref[...] = d_up
    total = matmul(d_gate, gate_w) + matmul(d_up, up_w)

    @pl.when(chunk == 0)
    def _():
        acc[block] = total

    @pl.when((chunk == 1) & (block < 2))
    def _():
        theirs_ref[...] = (acc[block] + total).astype(BF16)

    @pl.when((chunk == 1) & (block >= 2))
    def _():
        mine_ref[...] = (acc[block] + total).astype(BF16)


def experts_call(h2, dy, weights, spread, part):
    rows, width = h2.shape
    owners, depth, _ = weights.shape
    hidden = owners * part
    n, blocks = 2, 4
    step, wide = rows // blocks, hidden // n
    half = jax.ShapeDtypeStruct((rows // 2, width), BF16)
    wide_shape = jax.ShapeDtypeStruct((rows, hidden), BF16)

    def row(c, b):
        return (b + blocks // 2) % blocks

    wide_spec = pl.BlockSpec((step, wide), lambda c, b: (row(c, b), c))
    return pl.pallas_call(
        functools.partial(experts_kernel, part),
        grid=(n, blocks),
        in_specs=[
            pl.BlockSpec((step, width), lambda c, b: (row(c, b), 0)),
            pl.BlockSpec((step, dy.shape[1]), lambda c, b: (row(c, b), 0)),
            pl.BlockSpec((owners // n, depth, width), lambda c, b: (c, 0, 0)),
            pl.BlockSpec((spread.shape[0], wide), lambda c, b: (0, c)),
        ],
        out_specs=[
            wide_spec,
            wide_spec,
            wide_spec,
            pl.BlockSpec((step, width), lambda c, b: (c * jnp.minimum(b, 1), 0)),
            pl.BlockSpec((step, width), lambda c, b: (c * jnp.maximum(b - 2, 0), 0)),
        ],
        out_shape=[wide_shape, wide_shape, wide_shape, half, half],
        scratch_shapes=[pltpu.VMEM((blocks, step, width), F32)],
        compiler_params=pltpu.CompilerParams(vmem_limit_bytes=VMEM),
        cost_estimate=TINY,
        name="experts_rows",
    )(h2, dy, weights, spread)


def expert_grads_kernel(
    part, dg_ref, du_ref, hid_ref, h2_ref, dy_ref, out_ref, token_ref
):
    width = h2_ref.shape[1]
    group = out_ref.shape[0]
    h2 = h2_ref[...]
    out_ref[:, :part] = outer(dg_ref[...], h2).astype(BF16).reshape(group, part, width)
    out_ref[:, part : 2 * part] = outer(du_ref[...], h2).astype(BF16).reshape(group, part, width)
    out_ref[:, 2 * part :] = (
        outer(hid_ref[...], dy_ref[:, :width]).astype(BF16).reshape(group, part, width)
    )
    token_ref[...] = jnp.zeros_like(token_ref)


def expert_grads_call(d_gate, d_up, hidden, h2, dy, owners, part):
    rows, width = h2.shape
    n = 4
    wide = d_gate.shape[1] // n
    wide_spec = pl.BlockSpec((rows, wide), lambda c: (0, c))
    return pl.pallas_call(
        functools.partial(expert_grads_kernel, part),
        grid=(n,),
        in_specs=[
            wide_spec,
            wide_spec,
            wide_spec,
            pl.BlockSpec((rows, width), lambda c: (0, 0)),
            pl.BlockSpec((rows, dy.shape[1]), lambda c: (0, 0)),
        ],
        out_specs=[
            pl.BlockSpec((owners // n, 3 * part, width), lambda c: (c, 0, 0)),
            pl.BlockSpec((8, 128), lambda c: (0, 0)),
        ],
        out_shape=[
            jax.ShapeDtypeStruct((owners, 3 * part, width), BF16),
            jax.ShapeDtypeStruct((8, 128), F32),
        ],
        compiler_params=pltpu.CompilerParams(vmem_limit_bytes=VMEM),
        cost_estimate=TINY,
        name="experts_weights",
    )(d_gate, d_up, hidden, h2, dy)


def add_placed_kernel(where_ref, theirs_ref, mine_ref, token_ref, out_ref):
    ring = mine_ref.shape[0]
    for k in range(ring):
        out_ref[lax.rem(where_ref[0] + k, ring)] = (
            theirs_ref[k].astype(F32) + mine_ref[k].astype(F32)
        ).astype(BF16)


def add_placed_call(where, theirs, mine, token):
    vmem = pl.BlockSpec(memory_space=pltpu.VMEM)
    return pl.pallas_call(
        add_placed_kernel,
        grid_spec=pltpu.PrefetchScalarGridSpec(
            num_scalar_prefetch=1,
            grid=(),
            in_specs=[vmem, vmem, pl.BlockSpec(memory_space=pl.ANY)],
            out_specs=vmem,
        ),
        out_shape=jax.ShapeDtypeStruct(mine.shape, BF16),
        compiler_params=pltpu.CompilerParams(vmem_limit_bytes=VMEM),
        cost_estimate=TINY,
        name="add_cores_placed",
    )(where, theirs, mine, token)


def exchange_sum(pieces, token=None):
    got = lax.all_to_all(pieces, "context", split_axis=0, concat_axis=0, tiled=True)
    if token is not None:
        got = after_call(got, token)
    return jnp.sum(got.astype(F32), axis=0)


def add_kernel(theirs_ref, mine_ref, token_ref, *out_refs):
    for k, out_ref in enumerate(out_refs):
        out_ref[...] = (theirs_ref[k].astype(F32) + mine_ref[k].astype(F32)).astype(BF16)


def add_call(theirs, mine, token):
    shape = theirs.shape
    one = jax.ShapeDtypeStruct(shape[1:], BF16)
    vmem = pl.BlockSpec(memory_space=pltpu.VMEM)
    return pl.pallas_call(
        add_kernel,
        in_specs=[vmem, vmem, pl.BlockSpec(memory_space=pl.ANY)],
        out_specs=[vmem] * shape[0],
        out_shape=[one] * shape[0],
        compiler_params=pltpu.CompilerParams(vmem_limit_bytes=VMEM),
        cost_estimate=TINY,
        name="add_cores",
    )(theirs, mine, token)


def gate_up_down_kernel(part, in_ref, gate_ref, up_ref, down_ref):
    last = in_ref.shape[2]
    count = in_ref.shape[0] * part
    gate_ref[...] = in_ref[:, :part].reshape(count, last).astype(F32).T
    up_ref[...] = in_ref[:, part : 2 * part].reshape(count, last).astype(F32).T
    down_ref[...] = in_ref[:, 2 * part :].reshape(count, last).astype(F32)


def gate_up_down_call(gathered, part):
    members, depth, width = gathered.shape
    ff = members * part
    n = 8
    step = width // n
    return pl.pallas_call(
        functools.partial(gate_up_down_kernel, part),
        grid=(n,),
        in_specs=[pl.BlockSpec((members, depth, step), lambda c: (0, 0, c))],
        out_specs=[
            pl.BlockSpec((step, ff), lambda c: (c, 0)),
            pl.BlockSpec((step, ff), lambda c: (c, 0)),
            pl.BlockSpec((ff, step), lambda c: (0, c)),
        ],
        out_shape=[
            jax.ShapeDtypeStruct((width, ff), F32),
            jax.ShapeDtypeStruct((width, ff), F32),
            jax.ShapeDtypeStruct((ff, width), F32),
        ],
        compiler_params=pltpu.CompilerParams(vmem_limit_bytes=VMEM),
        cost_estimate=TINY,
        name="experts_results",
    )(gathered)


def out_grads_kernel(heads_ref, mine_ref, theirs_ref, out_ref):
    total = outer(heads_ref[0], mine_ref[...]) + outer(heads_ref[1], theirs_ref[...])
    out_ref[...] = total.astype(BF16)


def out_grads_call(heads_out, mine, theirs):
    _, half, columns = heads_out.shape
    width = mine.shape[1]
    n = 4
    spec = pl.BlockSpec((half, width // n), lambda c: (0, c))
    return pl.pallas_call(
        out_grads_kernel,
        grid=(n,),
        in_specs=[pl.BlockSpec(heads_out.shape, lambda c: (0, 0, 0)), spec, spec],
        out_specs=pl.BlockSpec((columns, width // n), lambda c: (0, c)),
        out_shape=jax.ShapeDtypeStruct((columns, width), BF16),
        compiler_params=pltpu.CompilerParams(vmem_limit_bytes=VMEM),
        cost_estimate=TINY,
        name="out_weights",
    )(heads_out, mine, theirs)


def attend_grads_kernel(
    cut, place_ref, h1_ref, d_qkv_ref, out_ref, gains_ref, token_ref, *refs
):
    firsts, seconds, share = refs[:SIDE], refs[SIDE : 2 * SIDE], refs[-1]
    step = pl.program_id(0)
    last = d_qkv_ref.shape[1]
    depth = share.shape[1] - 16
    grad = outer(h1_ref[...], d_qkv_ref[...]).astype(BF16)
    share[:, :depth, :last] = grad.reshape(SIDE, depth, last)
    rows, columns = out_ref.shape[1], share.shape[2] - last
    for k in range(depth // rows):
        share[:, k * rows : (k + 1) * rows, last:] = out_ref[:, :, k * columns : (k + 1) * columns]
    share[:, depth:] = gains_ref[...]
    for k in range(SIDE):

        @pl.when(step == k)
        def _():
            firsts[k][...] = share[:, :cut]

        seconds[k][0] = share[lax.rem(place_ref[1] + k, SIDE), cut:]


def attend_grads_call(place, h1, d_qkv, grad_out, gains, token, cut):
    rows, width = h1.shape
    owners, extra, columns = gains.shape
    depth = width // owners
    last = d_qkv.shape[1]

    def at(i, place):
        return lax.rem(place[0] + i, SIDE)

    first = jax.ShapeDtypeStruct((SIDE, cut, columns), BF16)
    second = jax.ShapeDtypeStruct((SIDE, depth + extra - cut, columns), BF16)
    outs = pl.pallas_call(
        functools.partial(attend_grads_kernel, cut),
        grid_spec=pltpu.PrefetchScalarGridSpec(
            num_scalar_prefetch=1,
            grid=(SIDE,),
            in_specs=[
                pl.BlockSpec((rows, width // SIDE), lambda i, place: (0, at(i, place))),
                pl.BlockSpec((rows, last), lambda i, place: (0, 0)),
                pl.BlockSpec((SIDE,) + grad_out.shape[1:], lambda i, place: (at(i, place), 0, 0)),
                pl.BlockSpec((SIDE, extra, columns), lambda i, place: (at(i, place), 0, 0)),
                pl.BlockSpec(memory_space=pl.ANY),
            ],
            out_specs=[pl.BlockSpec(first.shape, lambda i, place: (0, 0, 0))] * SIDE
            + [pl.BlockSpec((1,) + second.shape[1:], lambda i, place: (i, 0, 0))] * SIDE,
            scratch_shapes=[pltpu.VMEM((SIDE, depth + extra, columns), BF16)],
        ),
        out_shape=[first] * SIDE + [second] * SIDE,
        compiler_params=pltpu.CompilerParams(vmem_limit_bytes=VMEM),
        cost_estimate=TINY,
        name="attention_weights",
    )(place, h1, d_qkv, grad_out, gains, token)
    return outs[:SIDE], outs[SIDE:]


def total_of(refs):
    total = refs[0][...].astype(F32)
    for ref in refs[1:]:
        total = total + ref[...].astype(F32)
    return total.astype(BF16)


def half_sum_kernel(place_ref, *refs):
    outs, total = refs[2 * SIDE + 1 : -1], refs[-1]
    firsts, seconds = outs[:SIDE], outs[SIDE:]
    total[...] = total_of(refs[:SIDE])
    other = total_of(refs[SIDE : 2 * SIDE])
    for k in range(SIDE):
        firsts[k][...] = total[lax.rem(place_ref[1] + k, SIDE)]
        seconds[k][...] = other[k]


def half_sum_call(place, firsts, seconds, token):
    vmem = pl.BlockSpec(memory_space=pltpu.VMEM)
    outs = pl.pallas_call(
        half_sum_kernel,
        grid_spec=pltpu.PrefetchScalarGridSpec(
            num_scalar_prefetch=1,
            grid=(),
            in_specs=[vmem] * (2 * SIDE) + [pl.BlockSpec(memory_space=pl.ANY)],
            out_specs=[vmem] * (2 * SIDE),
            scratch_shapes=[pltpu.VMEM(firsts[0].shape, BF16)],
        ),
        out_shape=[jax.ShapeDtypeStruct(v.shape[1:], BF16) for v in (*firsts, *seconds)],
        compiler_params=pltpu.CompilerParams(vmem_limit_bytes=VMEM),
        cost_estimate=TINY,
        name="half_sum",
    )(place, *firsts, *seconds, token)
    return outs[:SIDE], outs[SIDE:]


def last_sum_kernel(token_ref, *refs):
    out = refs[-1]
    cut = refs[0].shape[0]
    out[:cut] = total_of(refs[:SIDE])
    out[cut:] = total_of(refs[SIDE : 2 * SIDE])


def last_sum_call(firsts, seconds, token):
    rows, columns = firsts[0].shape[0] + seconds[0].shape[0], firsts[0].shape[1]
    vmem = pl.BlockSpec(memory_space=pltpu.VMEM)
    return pl.pallas_call(
        last_sum_kernel,
        in_specs=[pl.BlockSpec(memory_space=pl.ANY)] + [vmem] * (2 * SIDE),
        out_specs=vmem,
        out_shape=jax.ShapeDtypeStruct((rows, columns), BF16),
        compiler_params=pltpu.CompilerParams(vmem_limit_bytes=VMEM),
        cost_estimate=TINY,
        name="last_sum",
    )(token, *firsts, *seconds)


def plane_send(pieces, dx, dz):
    return [pieces[0]] + [plane(pieces[k], -k * dx, -k * dz) for k in range(1, SIDE)]


def columns_kernel(heads_width, size, where_ref, mine_ref, theirs_ref, q_ref, k_ref, v_ref, sum_ref):
    depth = q_ref.shape[0]
    mine, theirs = mine_ref[0].astype(F32), theirs_ref[0].astype(F32)
    first = where_ref[1] == 0
    q_ref[:, :heads_width] = jnp.where(first, mine[:depth, :heads_width], theirs[:depth, :heads_width])
    q_ref[:, heads_width:] = jnp.where(first, theirs[:depth, :heads_width], mine[:depth, :heads_width])
    both = mine + theirs
    k_ref[...] = both[:depth, heads_width : heads_width + size]
    v_ref[...] = both[:depth, heads_width + size :]

    @pl.when(pl.program_id(0) == 0)
    def _():
        sum_ref[...] = jnp.zeros_like(sum_ref)

    sum_ref[...] += both[depth:]


def columns_call(where, mine, theirs, depth, heads_width, size):
    ring, rows, last = mine.shape
    cores = 2

    def at(k, where):
        return (0, lax.rem(where[0] + k, ring))

    return pl.pallas_call(
        functools.partial(columns_kernel, heads_width, size),
        grid_spec=pltpu.PrefetchScalarGridSpec(
            num_scalar_prefetch=1,
            grid=(ring,),
            in_specs=[pl.BlockSpec((1, rows, last), lambda k, where: (k, 0, 0))] * 2,
            out_specs=[
                pl.BlockSpec((depth, cores * heads_width), at),
                pl.BlockSpec((depth, size), at),
                pl.BlockSpec((depth, size), at),
                pl.BlockSpec((rows - depth, last), lambda k, where: (0, 0)),
            ],
        ),
        out_shape=[
            jax.ShapeDtypeStruct((depth, ring * cores * heads_width), F32),
            jax.ShapeDtypeStruct((depth, ring * size), F32),
            jax.ShapeDtypeStruct((depth, ring * size), F32),
            jax.ShapeDtypeStruct((rows - depth, last), F32),
        ],
        compiler_params=pltpu.CompilerParams(vmem_limit_bytes=VMEM),
        cost_estimate=TINY,
        name="columns_results",
    )(where, mine, theirs)


def rows_kernel(where_ref, mine_ref, theirs_ref, out_ref):
    count = mine_ref.shape[1]
    mine, theirs = mine_ref[0].astype(F32), theirs_ref[0].astype(F32)
    first = where_ref[1] == 0
    out_ref[:count] = jnp.where(first, mine, theirs)
    out_ref[count:] = jnp.where(first, theirs, mine)


def rows_call(where, mine, theirs):
    ring, count, width = mine.shape
    cores = 2
    return pl.pallas_call(
        rows_kernel,
        grid_spec=pltpu.PrefetchScalarGridSpec(
            num_scalar_prefetch=1,
            grid=(ring,),
            in_specs=[pl.BlockSpec((1, count, width), lambda k, where: (k, 0, 0))] * 2,
            out_specs=pl.BlockSpec(
                (cores * count, width), lambda k, where: (lax.rem(where[0] + k, ring), 0)
            ),
        ),
        out_shape=jax.ShapeDtypeStruct((ring * cores * count, width), F32),
        compiler_params=pltpu.CompilerParams(vmem_limit_bytes=VMEM),
        cost_estimate=TINY,
        name="rows_results",
    )(where, mine, theirs)


def expert_out_kernel(part, hid_ref, w_ref, token_ref, theirs_ref, mine_ref):
    width = w_ref.shape[2]
    block = pl.program_id(0)
    total = matmul(hid_ref[...], w_ref[...].reshape(w_ref.shape[0] * part, width)).astype(BF16)

    @pl.when(block < 2)
    def _():
        theirs_ref[...] = total

    @pl.when(block >= 2)
    def _():
        mine_ref[...] = total


def expert_out_call(hidden, weights, token, part):
    rows, wide = hidden.shape
    owners, _, width = weights.shape
    blocks = 4
    step = rows // blocks
    half = jax.ShapeDtypeStruct((rows // 2, width), BF16)
    return pl.pallas_call(
        functools.partial(expert_out_kernel, part),
        grid=(blocks,),
        in_specs=[
            pl.BlockSpec((step, wide), lambda b: ((b + blocks // 2) % blocks, 0)),
            pl.BlockSpec((owners, part, width), lambda b: (0, 2, 0)),
            pl.BlockSpec(memory_space=pl.ANY),
        ],
        out_specs=[
            pl.BlockSpec((step, width), lambda b: (jnp.minimum(b, 1), 0)),
            pl.BlockSpec((step, width), lambda b: (jnp.maximum(b - 2, 0), 0)),
        ],
        out_shape=[half, half],
        compiler_params=pltpu.CompilerParams(vmem_limit_bytes=VMEM),
        cost_estimate=pl.CostEstimate(
            flops=2 * rows * wide * width, bytes_accessed=20_000_000, transcendentals=0
        ),
        name="experts_out",
    )(hidden, weights, token)


def local(
    tokens,
    lengths,
    routes,
    mix_weights,
    cotangent,
    w_query,
    key_weight,
    value_weight,
    w_out,
    norm_attn,
    norm_moe,
    norm_query,
    norm_key,
    w_gate,
    w_up,
    w_down,
):
    owners = lax.axis_size("experts")
    ring = lax.axis_size("context")
    cores = lax.axis_size("dp")
    members = ring * cores
    y = lax.axis_index("context")
    d = lax.axis_index("dp")
    j = y * cores + d
    micro, _, row_count, width = tokens.shape
    head = norm_query.shape[0] * owners
    q_width = w_query.shape[1] // members
    q_heads = q_width // head
    depth = w_query.shape[0]
    ff = w_gate.shape[2]
    ff_part = ff // members
    out_rows = w_out.shape[0]
    out_part = out_rows // members
    seqs = cores * micro
    span = ring * row_count
    rows = seqs * span
    scale = head ** (-0.5)

    forth = [
        (es * members + k, ((es % cores) * members + k) * members + es // cores)
        for es in range(owners)
        for k in range(members)
    ]
    back = [(b, a) for a, b in forth]
    out_chunk = lax.ppermute(
        lax.dynamic_slice_in_dim(w_out, j * out_part, out_part, axis=0), EVERY, forth
    )
    expert_pack = jnp.concatenate(
        [
            lax.dynamic_slice_in_dim(w_gate[0], j * ff_part, ff_part, axis=1).T,
            lax.dynamic_slice_in_dim(w_up[0], j * ff_part, ff_part, axis=1).T,
            lax.dynamic_slice_in_dim(w_down[0], j * ff_part, ff_part, axis=0),
        ],
        axis=0,
    )
    gains = jnp.concatenate([norm_attn, norm_moe, norm_query, norm_key])
    packed = jnp.concatenate(
        [
            lax.dynamic_slice_in_dim(w_query, j * q_width, q_width, axis=1),
            lax.dynamic_slice_in_dim(key_weight, y * head, head, axis=1),
            lax.dynamic_slice_in_dim(value_weight, y * head, head, axis=1),
            jnp.concatenate(jnp.split(out_chunk, depth // out_part, axis=1), axis=0),
        ],
        axis=1,
    )
    qkv_width = q_width + 2 * head
    gain_rows = jnp.pad(gains[None], ((0, 15), (0, packed.shape[1] - gains.shape[0])))
    shared = lax.all_gather(
        jnp.concatenate([packed, gain_rows]), "experts", axis=0, tiled=False
    )
    expert_all = lax.all_gather(expert_pack, "experts", axis=0, tiled=False)
    gain_row = shared[:, depth]
    gain_row = gain_row.astype(F32)
    gain_attn = gain_row[:, :depth].reshape(-1)
    gain_moe = gain_row[:, depth : 2 * depth].reshape(-1)
    eighth = norm_query.shape[0]
    gain_query = gain_row[:, 2 * depth : 2 * depth + eighth].reshape(-1)
    gain_key = gain_row[:, 2 * depth + eighth : 2 * depth + 2 * eighth].reshape(-1)
    hidden_width = owners * ff_part

    where = jnp.stack([y, d]).astype(jnp.int32)
    x_own = tokens[:, 0]
    x_rows = gather_rows(x_own, ring)
    len_all = jnp.stack([lengths[:, 0], swap(lengths[:, 0])]).reshape(seqs)
    own_pos = y * row_count + jnp.arange(row_count, dtype=jnp.int32)
    valid = (own_pos[None, :] < lengths[:, 0][:, None]).astype(F32)
    dy_own = (cotangent[:, 0].astype(F32) * valid[:, :, None]).astype(BF16)
    ids = jnp.arange(owners, dtype=jnp.int32)
    mix_own = jnp.sum(
        jnp.where(routes[:, 0][..., None] == ids, mix_weights[:, 0][..., None], 0.0), axis=2
    )
    mix_high = mix_own.astype(BF16)
    mix_low = (mix_own - mix_high.astype(F32)).astype(BF16)
    lanes = 128
    mix_pad = jnp.zeros((micro, row_count, lanes - 2 * owners), BF16)
    dy_mix = gather_rows(jnp.concatenate([dy_own, mix_high, mix_low, mix_pad], axis=-1), ring)
    dy_mix = dy_mix.reshape(rows, width + lanes)
    lane = jnp.arange(lanes, dtype=jnp.int32)
    spread = (
        (jnp.arange(hidden_width, dtype=jnp.int32)[None, :] // ff_part == (lane % owners)[:, None])
        & (lane < 2 * owners)[:, None]
    ).astype(BF16)

    k_index = jnp.arange(span, dtype=jnp.int32)
    pos = ((y + k_index // row_count) % ring) * row_count + k_index % row_count
    frequency = ROPE_BASE ** (-jnp.arange(head // 2, dtype=F32) * 2.0 / head)
    phase = pos.astype(F32)[:, None] * frequency[None, :]
    cosines, sines = jnp.cos(phase), jnp.sin(phase)
    cosines = jnp.concatenate([cosines, cosines], axis=1)
    sines = jnp.concatenate([-sines, sines], axis=1)
    allowed = (pos[None, None, :] <= pos[None, :, None]) & (
        pos[None, None, :] < len_all[:, None, None]
    )
    bias = jnp.where(allowed, 0.0, -1e30).astype(F32)

    shape = (ring, micro, row_count, width)
    head_gains = (gain_query[None], gain_key[None])
    h1, qkv, heads_out, theirs, mine = attend_call(
        functools.partial(attend_kernel, q_heads, scale),
        (x_rows, gain_attn[None], shared, cosines, sines, bias, *head_gains, dy_mix),
        ("rows", "", "", "", "", "bias", "", "", "token"),
        (
            ("rows", width, BF16),
            ("rows", qkv_width, F32),
            ("rows", q_width, BF16),
            ("parts", width, BF16),
        ),
        [pltpu.VMEM((span, q_width), BF16), pltpu.VMEM((span, width), BF16)],
        shape,
        "attention",
        TINY,
    )
    attn_own = scatter_rows(theirs[0], mine[0])
    x1 = x_own.astype(F32) + attn_own
    inverse_mid = inverse_rms(x1)
    h2 = gather_rows((x1 * inverse_mid * gain_moe).astype(BF16), ring).reshape(rows, width)

    d_gate, d_up, hidden, theirs, mine = experts_call(h2, dy_mix, expert_all, spread, ff_part)
    grad_experts, token = expert_grads_call(
        d_gate, d_up, hidden, h2, dy_mix, owners, ff_part
    )
    pieces = add_call(swap(theirs.reshape(shape)), mine.reshape(shape), token)
    d_h2 = ring_sum(pieces)
    moe_theirs, moe_mine = expert_out_call(hidden, expert_all, token, ff_part)

    grad_gain_moe = jnp.sum(d_h2 * x1 * inverse_mid, axis=(0, 1))
    d_x1 = dy_own.astype(F32) + norm_back(d_h2, x1, inverse_mid, gain_moe)
    grad_experts = lax.psum_scatter(
        after_call(grad_experts, pieces[1]), "experts", scatter_dimension=0, tiled=False
    )
    moe_pieces = add_placed_call(
        where, swap(moe_theirs.reshape(shape)), moe_mine.reshape(shape), hidden
    )
    d_mine = after_call(ring_stack(d_x1.astype(BF16), ring), moe_pieces)
    d_theirs = swap(d_mine)
    grad_out = out_grads_call(
        heads_out.reshape(2, rows // 2, q_width),
        d_mine.reshape(-1, width),
        d_theirs.reshape(-1, width),
    )
    grad_out = grad_out.reshape(owners, out_part, width)
    d_qkv, theirs, mine, sum_q, sum_k, sum_x = attend_call(
        functools.partial(attend_back_kernel, q_heads, scale),
        (
            d_theirs[None],
            d_mine[None],
            x_rows,
            gain_attn[None],
            shared,
            cosines,
            sines,
            bias,
            *head_gains,
            qkv,
            moe_pieces,
            grad_out,
        ),
        (
            "theirs",
            "mine",
            "rows",
            "",
            "",
            "",
            "",
            "bias",
            "",
            "",
            "rows",
            "token",
            "token",
        ),
        (
            ("rows", qkv_width, BF16),
            ("parts", width, BF16),
            ("sum", head, F32),
            ("sum", head, F32),
            ("sum", width, F32),
        ),
        [pltpu.VMEM((span, qkv_width), BF16)],
        shape,
        "attention_back",
        pl.CostEstimate(flops=9_000_000_000, bytes_accessed=90_000_000, transcendentals=0),
    )
    output = (x1 + exchange_sum(moe_pieces, d_qkv)).astype(BF16)[:, None]
    grad_gain_query, grad_gain_key, grad_gain_attn = sum_q[0], sum_k[0], sum_x[0]
    h1, d_qkv = h1.reshape(rows, width), d_qkv.reshape(rows, qkv_width)

    grad_gains = jnp.concatenate(
        [
            grad_gain_attn.reshape(owners, depth),
            grad_gain_moe.reshape(owners, depth),
            grad_gain_query.reshape(owners, eighth),
            grad_gain_key.reshape(owners, eighth),
        ],
        axis=1,
    ).astype(BF16)
    grad_gains = jnp.pad(
        grad_gains[:, None], ((0, 0), (0, 15), (0, shared.shape[2] - grad_gains.shape[1]))
    )
    index = lax.axis_index("experts")
    place = jnp.stack([index // SIDE, index % SIDE]).astype(jnp.int32)
    firsts, seconds = attend_grads_call(
        place, h1, d_qkv, grad_out, grad_gains, output, depth // 2 + 16
    )
    h1_theirs = swap(theirs[0])
    h1_pieces = add_placed_call(where, h1_theirs, mine[0], firsts[1])
    d_h1 = exchange_sum(h1_pieces)
    x_f32 = x_own.astype(F32)
    input_grad = (d_x1 + norm_back(d_h1, x_f32, inverse_rms(x_f32), gain_attn))[:, None]
    grad_experts = after_call(grad_experts, firsts[1], h1_theirs)
    all_experts = lax.all_gather(grad_experts, GROUP, axis=0, tiled=False)
    firsts, seconds = plane_send(firsts, 1, 0), plane_send(seconds, 0, 1)
    firsts, seconds = half_sum_call(place, firsts, seconds, h1_pieces)
    result_gate, result_up, result_down = gate_up_down_call(all_experts, ff_part)
    grads = last_sum_call(plane_send(firsts, 0, 1), plane_send(seconds, 1, 0), h1_pieces)
    out_sum = jnp.concatenate(
        [grads[k * out_part : (k + 1) * out_part, qkv_width:] for k in range(depth // out_part)],
        axis=1,
    )
    result_q, result_k, result_v, gain_sum = columns_call(
        where, *gather_members(grads[:, :qkv_width]), depth, q_width, head
    )
    out_sum = after_call(lax.ppermute(out_sum, EVERY, back), input_grad, result_down)
    result_out = rows_call(where, *gather_members(out_sum, result_q))
    gain_sum = gain_sum[0]
    return (
        output,
        input_grad,
        result_q,
        result_k,
        result_v,
        result_out,
        gain_sum[:depth],
        gain_sum[depth : 2 * depth],
        gain_sum[2 * depth : 2 * depth + eighth],
        gain_sum[2 * depth + eighth : 2 * depth + 2 * eighth],
        result_gate[None],
        result_up[None],
        result_down[None],
    )


def solution(mesh):
    rows = P(None, ("experts", "dp"), "context", None)
    in_specs = (
        rows,
        P(None, ("experts", "dp")),
        rows,
        rows,
        rows,
        P("experts", None),
        P("experts", None),
        P("experts", None),
        P("experts", None),
        P("experts"),
        P("experts"),
        P("experts"),
        P("experts"),
        P("experts", None, None),
        P("experts", None, None),
        P("experts", None, None),
    )
    out_specs = (
        rows,
        rows,
        P("experts", None),
        P("experts", None),
        P("experts", None),
        P("experts", None),
        P("experts"),
        P("experts"),
        P("experts"),
        P("experts"),
        P("experts", None, None),
        P("experts", None, None),
        P("experts", None, None),
    )
    return jax.shard_map(local, mesh=mesh, in_specs=in_specs, out_specs=out_specs, check_vma=False)
```

```python
import functools

import jax
import jax.numpy as jnp
from jax import lax
from jax.experimental import pallas as pl
from jax.experimental.pallas import tpu as pltpu
from jax.sharding import PartitionSpec as P

EPS = 1e-06
ROPE_BASE = 1000000.0
F32 = jnp.float32
BF16 = jnp.bfloat16
GROUP = ("context", "dp")
EVERY = ("experts", "context", "dp")
VMEM = 60 * 1024 * 1024
SIDE = 4
TINY = pl.CostEstimate(flops=0, bytes_accessed=1000, transcendentals=0)


def inverse_rms(v):
    return lax.rsqrt(jnp.mean(v * v, axis=-1, keepdims=True) + EPS)


def norm_back(grad_in, v, inverse, gain):
    scaled = grad_in * gain
    return inverse * scaled - v * inverse**3 * jnp.mean(scaled * v, axis=-1, keepdims=True)


def matmul(left, right):
    return jnp.dot(left, right, preferred_element_type=F32)


def against(left, right):
    return lax.dot_general(left, right, (((1,), (1,)), ((), ())), preferred_element_type=F32)


def outer(left, right):
    return lax.dot_general(left, right, (((0,), (0,)), ((), ())), preferred_element_type=F32)


def swap(v):
    return lax.ppermute(v, "dp", [(0, 1), (1, 0)])


def ring_stack(own, ring):
    pieces = [own]
    for k in range(1, ring):
        pieces.append(lax.ppermute(own, "context", [((i + k) % ring, i) for i in range(ring)]))
    return jnp.stack(pieces)


def gather_rows(own, ring):
    mine = ring_stack(own, ring)
    return jnp.stack([mine, swap(mine)])


def ring_sum(pieces):
    ring = len(pieces)
    total = pieces[0].astype(F32)
    for k in range(1, ring):
        got = lax.ppermute(pieces[k], "context", [(i, (i + k) % ring) for i in range(ring)])
        total = total + got.astype(F32)
    return total


def add_cores(theirs, mine):
    other = swap(theirs)
    return [
        (mine[k].astype(F32) + other[k].astype(F32)).astype(BF16) for k in range(mine.shape[0])
    ]


def scatter_rows(theirs, mine):
    return ring_sum(add_cores(theirs, mine))


def gather_members(v, *tokens):
    ring = lax.axis_size("context")
    pieces = [after_call(v, *tokens) if tokens else v]
    for k in range(1, ring):
        pieces.append(lax.ppermute(v, "context", [((i + k) % ring, i) for i in range(ring)]))
    mine = jnp.stack(pieces)
    return mine, swap(mine)


def plane(v, dx, dz):
    moves = [
        (((i // SIDE + dx) % SIDE) * SIDE + (i % SIDE + dz) % SIDE, i) for i in range(SIDE * SIDE)
    ]
    return lax.ppermute(v, "experts", moves)


def after_kernel(v_ref, *refs):
    pass


def after_call(v, *tokens):
    anywhere = pl.BlockSpec(memory_space=pl.ANY)
    return pl.pallas_call(
        after_kernel,
        in_specs=[anywhere] * (1 + len(tokens)),
        out_specs=anywhere,
        out_shape=jax.ShapeDtypeStruct(v.shape, v.dtype),
        input_output_aliases={0: 0},
        cost_estimate=TINY,
        name="after",
    )(v, *tokens)


def rope(v, cosines, sines):
    return v * cosines + pltpu.roll(v, v.shape[-1] // 2, 1) * sines


def rope_back(v, cosines, sines):
    return v * cosines + pltpu.roll(v * sines, v.shape[-1] // 2, 1)


def flat(ref):
    v = ref[...]
    return v.reshape(v.shape[1] * v.shape[3], v.shape[4])


def chunks(ref, columns):
    v = ref[:, :-16, :columns]
    return v.reshape(v.shape[0] * v.shape[1], columns)


def out_blocks(ref, first):
    last = ref.shape[2] - first
    rows = last // ref.shape[0]
    for k in range((ref.shape[1] - 16) // rows):
        yield k * last, (k + 1) * last, ref[:, k * rows : (k + 1) * rows, first:].reshape(last, last)


def put(ref, v):
    ref[...] = v.reshape(ref.shape).astype(ref.dtype)


def attend_kernel(
    heads,
    scale,
    x_ref,
    gain_ref,
    w_ref,
    cos_ref,
    sin_ref,
    bias_ref,
    gain_q_ref,
    gain_k_ref,
    token_ref,
    h1_ref,
    qkv_ref,
    heads_ref,
    theirs_ref,
    mine_ref,
    heads_out,
    total,
):
    size = cos_ref.shape[1]
    x = flat(x_ref).astype(F32)
    h1 = (x * inverse_rms(x) * gain_ref[...]).astype(BF16)
    put(h1_ref, h1)
    width = (heads + 2) * size
    qkv = matmul(h1, chunks(w_ref, width))
    put(qkv_ref, qkv)
    cosines, sines, bias = cos_ref[...], sin_ref[...], bias_ref[0]
    k_pre = qkv[:, heads * size : (heads + 1) * size]
    key = rope(k_pre * inverse_rms(k_pre) * gain_k_ref[...], cosines, sines).astype(BF16)
    value = qkv[:, (heads + 1) * size :].astype(BF16)
    for g in range(heads):
        q_pre = qkv[:, g * size : (g + 1) * size]
        query = rope(q_pre * inverse_rms(q_pre) * gain_q_ref[...], cosines, sines).astype(BF16)
        logits = against(query, key) * scale + bias
        scaled = jnp.exp(logits - jnp.max(logits, axis=-1, keepdims=True))
        soft = (scaled * (1.0 / jnp.sum(scaled, axis=-1, keepdims=True))).astype(BF16)
        heads_out[:, g * size : (g + 1) * size] = matmul(soft, value).astype(BF16)
    out = heads_out[...]
    put(heads_ref, out)
    for first, last, block in out_blocks(w_ref, width):
        total[:, first:last] = matmul(out, block).astype(BF16)

    @pl.when(pl.program_id(0) < 2)
    def _():
        put(theirs_ref, total[...])

    @pl.when(pl.program_id(0) >= 2)
    def _():
        put(mine_ref, total[...])


def attend_back_kernel(
    heads,
    scale,
    theirs_da_ref,
    mine_da_ref,
    x_ref,
    gain_ref,
    w_ref,
    cos_ref,
    sin_ref,
    bias_ref,
    gain_q_ref,
    gain_k_ref,
    qkv_ref,
    token_ref,
    other_token_ref,
    d_qkv_ref,
    theirs_ref,
    mine_ref,
    sum_q_ref,
    sum_k_ref,
    sum_x_ref,
    d_qkv,
):
    size = cos_ref.shape[1]
    step = pl.program_id(0)

    @pl.when(step == 0)
    def _():
        sum_q_ref[...] = jnp.zeros_like(sum_q_ref)
        sum_k_ref[...] = jnp.zeros_like(sum_k_ref)
        sum_x_ref[...] = jnp.zeros_like(sum_x_ref)

    width = (heads + 2) * size
    da = jnp.where(step < 2, flat(theirs_da_ref), flat(mine_da_ref))
    d_heads = None
    for first, last, block in out_blocks(w_ref, width):
        piece = against(da[:, first:last], block)
        d_heads = piece if d_heads is None else d_heads + piece
    d_heads = d_heads.astype(BF16)
    qkv = flat(qkv_ref)
    cosines, sines, bias = cos_ref[...], sin_ref[...], bias_ref[0]
    gain_q, gain_k = gain_q_ref[...], gain_k_ref[...]
    k_pre = qkv[:, heads * size : (heads + 1) * size]
    inverse_k = inverse_rms(k_pre)
    key = rope(k_pre * inverse_k * gain_k, cosines, sines).astype(BF16)
    value = qkv[:, (heads + 1) * size :].astype(BF16)
    d_key = jnp.zeros(k_pre.shape, F32)
    d_value = jnp.zeros(k_pre.shape, F32)
    sum_q = jnp.zeros((1, size), F32)
    for g in range(heads):
        q_pre = qkv[:, g * size : (g + 1) * size]
        inverse_q = inverse_rms(q_pre)
        query = rope(q_pre * inverse_q * gain_q, cosines, sines).astype(BF16)
        logits = against(query, key) * scale + bias
        scaled = jnp.exp(logits - jnp.max(logits, axis=-1, keepdims=True))
        probs = scaled * (1.0 / jnp.sum(scaled, axis=-1, keepdims=True))
        d_head = d_heads[:, g * size : (g + 1) * size]
        d_probs = against(d_head, value)
        d_scores = probs * (d_probs - jnp.sum(probs * d_probs, axis=-1, keepdims=True))
        d_scores = d_scores.astype(BF16)
        d_query = rope_back(matmul(d_scores, key) * scale, cosines, sines)
        d_key = d_key + outer(d_scores, query)
        d_value = d_value + outer(probs.astype(BF16), d_head)
        sum_q = sum_q + jnp.sum(d_query * q_pre * inverse_q, axis=0, keepdims=True)
        d_qkv[:, g * size : (g + 1) * size] = norm_back(d_query, q_pre, inverse_q, gain_q).astype(
            BF16
        )
    d_key = rope_back(d_key * scale, cosines, sines)
    sum_k = jnp.sum(d_key * k_pre * inverse_k, axis=0, keepdims=True)
    d_qkv[:, heads * size : (heads + 1) * size] = norm_back(d_key, k_pre, inverse_k, gain_k).astype(
        BF16
    )
    d_qkv[:, (heads + 1) * size :] = d_value.astype(BF16)
    grads = d_qkv[...]
    put(d_qkv_ref, grads)
    part = against(grads, chunks(w_ref, width))
    x = flat(x_ref).astype(F32)
    sum_x_ref[0:1, :] += jnp.sum(part * (x * inverse_rms(x)), axis=0, keepdims=True)
    sum_q_ref[0:1, :] += sum_q
    sum_k_ref[0:1, :] += sum_k

    @pl.when(step < 2)
    def _():
        put(theirs_ref, part)

    @pl.when(step >= 2)
    def _():
        put(mine_ref, part)


def attend_call(kernel, operands, extra, outputs, scratch, shape, name, cost):
    ring, micro, row_count, width = shape

    def rows_spec(last):
        return pl.BlockSpec(
            (1, ring, 1, row_count, last), lambda b: (1 - b // 2, 0, b % 2, 0, 0)
        )

    def whole(v):
        return pl.BlockSpec(v.shape, lambda b: (0,) * v.ndim)

    def slot_spec(v, kind):
        block = (1, ring, 1, row_count, v.shape[-1])
        if kind == "theirs":
            return pl.BlockSpec(block, lambda b: (0, 0, jnp.minimum(b, 1), 0, 0))
        return pl.BlockSpec(block, lambda b: (0, 0, jnp.maximum(b - 2, 0), 0, 0))

    in_specs = [
        rows_spec(v.shape[-1])
        if kind == "rows"
        else slot_spec(v, kind)
        if kind in ("theirs", "mine")
        else pl.BlockSpec((1,) + v.shape[1:], lambda b: ((1 - b // 2) * micro + b % 2, 0, 0))
        if kind == "bias"
        else pl.BlockSpec(memory_space=pl.ANY)
        if kind == "token"
        else whole(v)
        for v, kind in zip(operands, extra)
    ]
    out_shape, out_specs = [], []
    for kind, last, dtype in outputs:
        if kind == "rows":
            out_shape.append(jax.ShapeDtypeStruct((2, ring, micro, row_count, last), dtype))
            out_specs.append(rows_spec(last))
        elif kind == "parts":
            one = jax.ShapeDtypeStruct((1, ring, micro, row_count, last), dtype)
            out_shape += [one, one]
            block = (1, ring, 1, row_count, last)
            out_specs.append(pl.BlockSpec(block, lambda b: (0, 0, jnp.minimum(b, 1), 0, 0)))
            out_specs.append(pl.BlockSpec(block, lambda b: (0, 0, jnp.maximum(b - 2, 0), 0, 0)))
        else:
            out_shape.append(jax.ShapeDtypeStruct((8, last), dtype))
            out_specs.append(pl.BlockSpec((8, last), lambda b: (0, 0)))
    return pl.pallas_call(
        kernel,
        grid=(2 * micro,),
        in_specs=in_specs,
        out_specs=out_specs,
        out_shape=out_shape,
        scratch_shapes=scratch,
        compiler_params=pltpu.CompilerParams(vmem_limit_bytes=VMEM),
        cost_estimate=cost,
        name=name,
    )(*operands)


def experts_kernel(
    part, h2_ref, dy_ref, w_ref, spread_ref, dg_ref, du_ref, hid_ref, theirs_ref, mine_ref, acc
):
    chunk, block = pl.program_id(0), pl.program_id(1)
    width = h2_ref.shape[1]
    count = w_ref.shape[0] * part
    gate_w = w_ref[:, :part].reshape(count, width)
    up_w = w_ref[:, part : 2 * part].reshape(count, width)
    down_w = w_ref[:, 2 * part :].reshape(count, width)
    h2 = h2_ref[...]
    mix = matmul(dy_ref[:, width:], spread_ref[...])
    gate = against(h2, gate_w)
    up = against(h2, up_w)
    d_hidden = against(dy_ref[:, :width], down_w) * mix
    sigma = jax.nn.sigmoid(gate)
    silu = gate * sigma
    hid_ref[...] = (silu * up * mix).astype(BF16)
    d_gate = (d_hidden * up * sigma * (1.0 + gate * (1.0 - sigma))).astype(BF16)
    d_up = (d_hidden * silu).astype(BF16)
    dg_ref[...] = d_gate
    du_ref[...] = d_up
    total = matmul(d_gate, gate_w) + matmul(d_up, up_w)

    @pl.when(chunk == 0)
    def _():
        acc[block] = total

    @pl.when((chunk == 1) & (block < 2))
    def _():
        theirs_ref[...] = (acc[block] + total).astype(BF16)

    @pl.when((chunk == 1) & (block >= 2))
    def _():
        mine_ref[...] = (acc[block] + total).astype(BF16)


def experts_call(h2, dy, weights, spread, part):
    rows, width = h2.shape
    owners, depth, _ = weights.shape
    hidden = owners * part
    n, blocks = 2, 4
    step, wide = rows // blocks, hidden // n
    half = jax.ShapeDtypeStruct((rows // 2, width), BF16)
    wide_shape = jax.ShapeDtypeStruct((rows, hidden), BF16)

    def row(c, b):
        return (b + blocks // 2) % blocks

    wide_spec = pl.BlockSpec((step, wide), lambda c, b: (row(c, b), c))
    return pl.pallas_call(
        functools.partial(experts_kernel, part),
        grid=(n, blocks),
        in_specs=[
            pl.BlockSpec((step, width), lambda c, b: (row(c, b), 0)),
            pl.BlockSpec((step, dy.shape[1]), lambda c, b: (row(c, b), 0)),
            pl.BlockSpec((owners // n, depth, width), lambda c, b: (c, 0, 0)),
            pl.BlockSpec((spread.shape[0], wide), lambda c, b: (0, c)),
        ],
        out_specs=[
            wide_spec,
            wide_spec,
            wide_spec,
            pl.BlockSpec((step, width), lambda c, b: (c * jnp.minimum(b, 1), 0)),
            pl.BlockSpec((step, width), lambda c, b: (c * jnp.maximum(b - 2, 0), 0)),
        ],
        out_shape=[wide_shape, wide_shape, wide_shape, half, half],
        scratch_shapes=[pltpu.VMEM((blocks, step, width), F32)],
        compiler_params=pltpu.CompilerParams(vmem_limit_bytes=VMEM),
        cost_estimate=TINY,
        name="experts_rows",
    )(h2, dy, weights, spread)


def expert_grads_kernel(
    part, dg_ref, du_ref, hid_ref, h2_ref, dy_ref, out_ref, token_ref
):
    width = h2_ref.shape[1]
    group = out_ref.shape[0]
    h2 = h2_ref[...]
    out_ref[:, :part] = outer(dg_ref[...], h2).astype(BF16).reshape(group, part, width)
    out_ref[:, part : 2 * part] = outer(du_ref[...], h2).astype(BF16).reshape(group, part, width)
    out_ref[:, 2 * part :] = (
        outer(hid_ref[...], dy_ref[:, :width]).astype(BF16).reshape(group, part, width)
    )
    token_ref[...] = jnp.zeros_like(token_ref)


def expert_grads_call(d_gate, d_up, hidden, h2, dy, owners, part):
    rows, width = h2.shape
    n = 4
    wide = d_gate.shape[1] // n
    wide_spec = pl.BlockSpec((rows, wide), lambda c: (0, c))
    return pl.pallas_call(
        functools.partial(expert_grads_kernel, part),
        grid=(n,),
        in_specs=[
            wide_spec,
            wide_spec,
            wide_spec,
            pl.BlockSpec((rows, width), lambda c: (0, 0)),
            pl.BlockSpec((rows, dy.shape[1]), lambda c: (0, 0)),
        ],
        out_specs=[
            pl.BlockSpec((owners // n, 3 * part, width), lambda c: (c, 0, 0)),
            pl.BlockSpec((8, 128), lambda c: (0, 0)),
        ],
        out_shape=[
            jax.ShapeDtypeStruct((owners, 3 * part, width), BF16),
            jax.ShapeDtypeStruct((8, 128), F32),
        ],
        compiler_params=pltpu.CompilerParams(vmem_limit_bytes=VMEM),
        cost_estimate=TINY,
        name="experts_weights",
    )(d_gate, d_up, hidden, h2, dy)


def add_placed_kernel(where_ref, theirs_ref, mine_ref, token_ref, out_ref):
    ring = mine_ref.shape[0]
    for k in range(ring):
        out_ref[lax.rem(where_ref[0] + k, ring)] = (
            theirs_ref[k].astype(F32) + mine_ref[k].astype(F32)
        ).astype(BF16)


def add_placed_call(where, theirs, mine, token):
    vmem = pl.BlockSpec(memory_space=pltpu.VMEM)
    return pl.pallas_call(
        add_placed_kernel,
        grid_spec=pltpu.PrefetchScalarGridSpec(
            num_scalar_prefetch=1,
            grid=(),
            in_specs=[vmem, vmem, pl.BlockSpec(memory_space=pl.ANY)],
            out_specs=vmem,
        ),
        out_shape=jax.ShapeDtypeStruct(mine.shape, BF16),
        compiler_params=pltpu.CompilerParams(vmem_limit_bytes=VMEM),
        cost_estimate=TINY,
        name="add_cores_placed",
    )(where, theirs, mine, token)


def exchange_sum(pieces, token=None):
    got = lax.all_to_all(pieces, "context", split_axis=0, concat_axis=0, tiled=True)
    if token is not None:
        got = after_call(got, token)
    return jnp.sum(got.astype(F32), axis=0)


def add_kernel(theirs_ref, mine_ref, token_ref, *out_refs):
    for k, out_ref in enumerate(out_refs):
        out_ref[...] = (theirs_ref[k].astype(F32) + mine_ref[k].astype(F32)).astype(BF16)


def add_call(theirs, mine, token):
    shape = theirs.shape
    one = jax.ShapeDtypeStruct(shape[1:], BF16)
    vmem = pl.BlockSpec(memory_space=pltpu.VMEM)
    return pl.pallas_call(
        add_kernel,
        in_specs=[vmem, vmem, pl.BlockSpec(memory_space=pl.ANY)],
        out_specs=[vmem] * shape[0],
        out_shape=[one] * shape[0],
        compiler_params=pltpu.CompilerParams(vmem_limit_bytes=VMEM),
        cost_estimate=TINY,
        name="add_cores",
    )(theirs, mine, token)


def gate_up_down_kernel(part, in_ref, gate_ref, up_ref, down_ref):
    last = in_ref.shape[2]
    count = in_ref.shape[0] * part
    gate_ref[...] = in_ref[:, :part].reshape(count, last).astype(F32).T
    up_ref[...] = in_ref[:, part : 2 * part].reshape(count, last).astype(F32).T
    down_ref[...] = in_ref[:, 2 * part :].reshape(count, last).astype(F32)


def gate_up_down_call(gathered, part):
    members, depth, width = gathered.shape
    ff = members * part
    n = 8
    step = width // n
    return pl.pallas_call(
        functools.partial(gate_up_down_kernel, part),
        grid=(n,),
        in_specs=[pl.BlockSpec((members, depth, step), lambda c: (0, 0, c))],
        out_specs=[
            pl.BlockSpec((step, ff), lambda c: (c, 0)),
            pl.BlockSpec((step, ff), lambda c: (c, 0)),
            pl.BlockSpec((ff, step), lambda c: (0, c)),
        ],
        out_shape=[
            jax.ShapeDtypeStruct((width, ff), F32),
            jax.ShapeDtypeStruct((width, ff), F32),
            jax.ShapeDtypeStruct((ff, width), F32),
        ],
        compiler_params=pltpu.CompilerParams(vmem_limit_bytes=VMEM),
        cost_estimate=TINY,
        name="experts_results",
    )(gathered)


def out_grads_kernel(heads_ref, mine_ref, theirs_ref, out_ref):
    total = outer(heads_ref[0], mine_ref[...]) + outer(heads_ref[1], theirs_ref[...])
    out_ref[...] = total.astype(BF16)


def out_grads_call(heads_out, mine, theirs):
    _, half, columns = heads_out.shape
    width = mine.shape[1]
    n = 4
    spec = pl.BlockSpec((half, width // n), lambda c: (0, c))
    return pl.pallas_call(
        out_grads_kernel,
        grid=(n,),
        in_specs=[pl.BlockSpec(heads_out.shape, lambda c: (0, 0, 0)), spec, spec],
        out_specs=pl.BlockSpec((columns, width // n), lambda c: (0, c)),
        out_shape=jax.ShapeDtypeStruct((columns, width), BF16),
        compiler_params=pltpu.CompilerParams(vmem_limit_bytes=VMEM),
        cost_estimate=TINY,
        name="out_weights",
    )(heads_out, mine, theirs)


def attend_grads_kernel(
    cut, place_ref, h1_ref, d_qkv_ref, out_ref, gains_ref, token_ref, *refs
):
    firsts, seconds, share = refs[:SIDE], refs[SIDE : 2 * SIDE], refs[-1]
    step = pl.program_id(0)
    last = d_qkv_ref.shape[1]
    depth = share.shape[1] - 16
    grad = outer(h1_ref[...], d_qkv_ref[...]).astype(BF16)
    share[:, :depth, :last] = grad.reshape(SIDE, depth, last)
    rows, columns = out_ref.shape[1], share.shape[2] - last
    for k in range(depth // rows):
        share[:, k * rows : (k + 1) * rows, last:] = out_ref[:, :, k * columns : (k + 1) * columns]
    share[:, depth:] = gains_ref[...]
    for k in range(SIDE):

        @pl.when(step == k)
        def _():
            firsts[k][...] = share[:, :cut]

        seconds[k][0] = share[lax.rem(place_ref[1] + k, SIDE), cut:]


def attend_grads_call(place, h1, d_qkv, grad_out, gains, token, cut):
    rows, width = h1.shape
    owners, extra, columns = gains.shape
    depth = width // owners
    last = d_qkv.shape[1]

    def at(i, place):
        return lax.rem(place[0] + i, SIDE)

    first = jax.ShapeDtypeStruct((SIDE, cut, columns), BF16)
    second = jax.ShapeDtypeStruct((SIDE, depth + extra - cut, columns), BF16)
    outs = pl.pallas_call(
        functools.partial(attend_grads_kernel, cut),
        grid_spec=pltpu.PrefetchScalarGridSpec(
            num_scalar_prefetch=1,
            grid=(SIDE,),
            in_specs=[
                pl.BlockSpec((rows, width // SIDE), lambda i, place: (0, at(i, place))),
                pl.BlockSpec((rows, last), lambda i, place: (0, 0)),
                pl.BlockSpec((SIDE,) + grad_out.shape[1:], lambda i, place: (at(i, place), 0, 0)),
                pl.BlockSpec((SIDE, extra, columns), lambda i, place: (at(i, place), 0, 0)),
                pl.BlockSpec(memory_space=pl.ANY),
            ],
            out_specs=[pl.BlockSpec(first.shape, lambda i, place: (0, 0, 0))] * SIDE
            + [pl.BlockSpec((1,) + second.shape[1:], lambda i, place: (i, 0, 0))] * SIDE,
            scratch_shapes=[pltpu.VMEM((SIDE, depth + extra, columns), BF16)],
        ),
        out_shape=[first] * SIDE + [second] * SIDE,
        compiler_params=pltpu.CompilerParams(vmem_limit_bytes=VMEM),
        cost_estimate=TINY,
        name="attention_weights",
    )(place, h1, d_qkv, grad_out, gains, token)
    return outs[:SIDE], outs[SIDE:]


def total_of(refs):
    total = refs[0][...].astype(F32)
    for ref in refs[1:]:
        total = total + ref[...].astype(F32)
    return total.astype(BF16)


def half_sum_kernel(place_ref, *refs):
    outs, total = refs[2 * SIDE + 1 : -1], refs[-1]
    firsts, seconds = outs[:SIDE], outs[SIDE:]
    total[...] = total_of(refs[:SIDE])
    other = total_of(refs[SIDE : 2 * SIDE])
    for k in range(SIDE):
        firsts[k][...] = total[lax.rem(place_ref[1] + k, SIDE)]
        seconds[k][...] = other[k]


def half_sum_call(place, firsts, seconds, token):
    vmem = pl.BlockSpec(memory_space=pltpu.VMEM)
    outs = pl.pallas_call(
        half_sum_kernel,
        grid_spec=pltpu.PrefetchScalarGridSpec(
            num_scalar_prefetch=1,
            grid=(),
            in_specs=[vmem] * (2 * SIDE) + [pl.BlockSpec(memory_space=pl.ANY)],
            out_specs=[vmem] * (2 * SIDE),
            scratch_shapes=[pltpu.VMEM(firsts[0].shape, BF16)],
        ),
        out_shape=[jax.ShapeDtypeStruct(v.shape[1:], BF16) for v in (*firsts, *seconds)],
        compiler_params=pltpu.CompilerParams(vmem_limit_bytes=VMEM),
        cost_estimate=TINY,
        name="half_sum",
    )(place, *firsts, *seconds, token)
    return outs[:SIDE], outs[SIDE:]


def last_sum_kernel(token_ref, *refs):
    out = refs[-1]
    cut = refs[0].shape[0]
    out[:cut] = total_of(refs[:SIDE])
    out[cut:] = total_of(refs[SIDE : 2 * SIDE])


def last_sum_call(firsts, seconds, token):
    rows, columns = firsts[0].shape[0] + seconds[0].shape[0], firsts[0].shape[1]
    vmem = pl.BlockSpec(memory_space=pltpu.VMEM)
    return pl.pallas_call(
        last_sum_kernel,
        in_specs=[pl.BlockSpec(memory_space=pl.ANY)] + [vmem] * (2 * SIDE),
        out_specs=vmem,
        out_shape=jax.ShapeDtypeStruct((rows, columns), BF16),
        compiler_params=pltpu.CompilerParams(vmem_limit_bytes=VMEM),
        cost_estimate=TINY,
        name="last_sum",
    )(token, *firsts, *seconds)


def plane_send(pieces, dx, dz):
    return [pieces[0]] + [plane(pieces[k], -k * dx, -k * dz) for k in range(1, SIDE)]


def columns_kernel(heads_width, size, where_ref, mine_ref, theirs_ref, q_ref, k_ref, v_ref, sum_ref):
    depth = q_ref.shape[0]
    mine, theirs = mine_ref[0].astype(F32), theirs_ref[0].astype(F32)
    first = where_ref[1] == 0
    q_ref[:, :heads_width] = jnp.where(first, mine[:depth, :heads_width], theirs[:depth, :heads_width])
    q_ref[:, heads_width:] = jnp.where(first, theirs[:depth, :heads_width], mine[:depth, :heads_width])
    both = mine + theirs
    k_ref[...] = both[:depth, heads_width : heads_width + size]
    v_ref[...] = both[:depth, heads_width + size :]

    @pl.when(pl.program_id(0) == 0)
    def _():
        sum_ref[...] = jnp.zeros_like(sum_ref)

    sum_ref[...] += both[depth:]


def columns_call(where, mine, theirs, depth, heads_width, size):
    ring, rows, last = mine.shape
    cores = 2

    def at(k, where):
        return (0, lax.rem(where[0] + k, ring))

    return pl.pallas_call(
        functools.partial(columns_kernel, heads_width, size),
        grid_spec=pltpu.PrefetchScalarGridSpec(
            num_scalar_prefetch=1,
            grid=(ring,),
            in_specs=[pl.BlockSpec((1, rows, last), lambda k, where: (k, 0, 0))] * 2,
            out_specs=[
                pl.BlockSpec((depth, cores * heads_width), at),
                pl.BlockSpec((depth, size), at),
                pl.BlockSpec((depth, size), at),
                pl.BlockSpec((rows - depth, last), lambda k, where: (0, 0)),
            ],
        ),
        out_shape=[
            jax.ShapeDtypeStruct((depth, ring * cores * heads_width), F32),
            jax.ShapeDtypeStruct((depth, ring * size), F32),
            jax.ShapeDtypeStruct((depth, ring * size), F32),
            jax.ShapeDtypeStruct((rows - depth, last), F32),
        ],
        compiler_params=pltpu.CompilerParams(vmem_limit_bytes=VMEM),
        cost_estimate=TINY,
        name="columns_results",
    )(where, mine, theirs)


def rows_kernel(where_ref, mine_ref, theirs_ref, out_ref):
    count = mine_ref.shape[1]
    mine, theirs = mine_ref[0].astype(F32), theirs_ref[0].astype(F32)
    first = where_ref[1] == 0
    out_ref[:count] = jnp.where(first, mine, theirs)
    out_ref[count:] = jnp.where(first, theirs, mine)


def rows_call(where, mine, theirs):
    ring, count, width = mine.shape
    cores = 2
    return pl.pallas_call(
        rows_kernel,
        grid_spec=pltpu.PrefetchScalarGridSpec(
            num_scalar_prefetch=1,
            grid=(ring,),
            in_specs=[pl.BlockSpec((1, count, width), lambda k, where: (k, 0, 0))] * 2,
            out_specs=pl.BlockSpec(
                (cores * count, width), lambda k, where: (lax.rem(where[0] + k, ring), 0)
            ),
        ),
        out_shape=jax.ShapeDtypeStruct((ring * cores * count, width), F32),
        compiler_params=pltpu.CompilerParams(vmem_limit_bytes=VMEM),
        cost_estimate=TINY,
        name="rows_results",
    )(where, mine, theirs)


def expert_out_kernel(part, hid_ref, w_ref, token_ref, theirs_ref, mine_ref):
    width = w_ref.shape[2]
    block = pl.program_id(0)
    total = matmul(hid_ref[...], w_ref[...].reshape(w_ref.shape[0] * part, width)).astype(BF16)

    @pl.when(block < 2)
    def _():
        theirs_ref[...] = total

    @pl.when(block >= 2)
    def _():
        mine_ref[...] = total


def expert_out_call(hidden, weights, token, part):
    rows, wide = hidden.shape
    owners, _, width = weights.shape
    blocks = 4
    step = rows // blocks
    half = jax.ShapeDtypeStruct((rows // 2, width), BF16)
    return pl.pallas_call(
        functools.partial(expert_out_kernel, part),
        grid=(blocks,),
        in_specs=[
            pl.BlockSpec((step, wide), lambda b: ((b + blocks // 2) % blocks, 0)),
            pl.BlockSpec((owners, part, width), lambda b: (0, 2, 0)),
            pl.BlockSpec(memory_space=pl.ANY),
        ],
        out_specs=[
            pl.BlockSpec((step, width), lambda b: (jnp.minimum(b, 1), 0)),
            pl.BlockSpec((step, width), lambda b: (jnp.maximum(b - 2, 0), 0)),
        ],
        out_shape=[half, half],
        compiler_params=pltpu.CompilerParams(vmem_limit_bytes=VMEM),
        cost_estimate=pl.CostEstimate(
            flops=2 * rows * wide * width, bytes_accessed=20_000_000, transcendentals=0
        ),
        name="experts_out",
    )(hidden, weights, token)


def local(
    tokens,
    lengths,
    routes,
    mix_weights,
    cotangent,
    w_query,
    key_weight,
    value_weight,
    w_out,
    norm_attn,
    norm_moe,
    norm_query,
    norm_key,
    w_gate,
    w_up,
    w_down,
):
    owners = lax.axis_size("experts")
    ring = lax.axis_size("context")
    cores = lax.axis_size("dp")
    members = ring * cores
    y = lax.axis_index("context")
    d = lax.axis_index("dp")
    j = y * cores + d
    micro, _, row_count, width = tokens.shape
    head = norm_query.shape[0] * owners
    q_width = w_query.shape[1] // members
    q_heads = q_width // head
    depth = w_query.shape[0]
    ff = w_gate.shape[2]
    ff_part = ff // members
    out_rows = w_out.shape[0]
    out_part = out_rows // members
    seqs = cores * micro
    span = ring * row_count
    rows = seqs * span
    scale = head ** (-0.5)

    forth = [
        (es * members + k, ((es % cores) * members + k) * members + es // cores)
        for es in range(owners)
        for k in range(members)
    ]
    back = [(b, a) for a, b in forth]
    out_chunk = lax.ppermute(
        lax.dynamic_slice_in_dim(w_out, j * out_part, out_part, axis=0), EVERY, forth
    )
    expert_pack = jnp.concatenate(
        [
            lax.dynamic_slice_in_dim(w_gate[0], j * ff_part, ff_part, axis=1).T,
            lax.dynamic_slice_in_dim(w_up[0], j * ff_part, ff_part, axis=1).T,
            lax.dynamic_slice_in_dim(w_down[0], j * ff_part, ff_part, axis=0),
        ],
        axis=0,
    )
    gains = jnp.concatenate([norm_attn, norm_moe, norm_query, norm_key])
    packed = jnp.concatenate(
        [
            lax.dynamic_slice_in_dim(w_query, j * q_width, q_width, axis=1),
            lax.dynamic_slice_in_dim(key_weight, y * head, head, axis=1),
            lax.dynamic_slice_in_dim(value_weight, y * head, head, axis=1),
            jnp.concatenate(jnp.split(out_chunk, depth // out_part, axis=1), axis=0),
        ],
        axis=1,
    )
    qkv_width = q_width + 2 * head
    gain_rows = jnp.pad(gains[None], ((0, 15), (0, packed.shape[1] - gains.shape[0])))
    shared = lax.all_gather(
        jnp.concatenate([packed, gain_rows]), "experts", axis=0, tiled=False
    )
    expert_all = lax.all_gather(expert_pack, "experts", axis=0, tiled=False)
    gain_row = shared[:, depth]
    gain_row = gain_row.astype(F32)
    gain_attn = gain_row[:, :depth].reshape(-1)
    gain_moe = gain_row[:, depth : 2 * depth].reshape(-1)
    eighth = norm_query.shape[0]
    gain_query = gain_row[:, 2 * depth : 2 * depth + eighth].reshape(-1)
    gain_key = gain_row[:, 2 * depth + eighth : 2 * depth + 2 * eighth].reshape(-1)
    hidden_width = owners * ff_part

    where = jnp.stack([y, d]).astype(jnp.int32)
    x_own = tokens[:, 0]
    x_rows = gather_rows(x_own, ring)
    len_all = jnp.stack([lengths[:, 0], swap(lengths[:, 0])]).reshape(seqs)
    own_pos = y * row_count + jnp.arange(row_count, dtype=jnp.int32)
    valid = (own_pos[None, :] < lengths[:, 0][:, None]).astype(F32)
    dy_own = (cotangent[:, 0].astype(F32) * valid[:, :, None]).astype(BF16)
    ids = jnp.arange(owners, dtype=jnp.int32)
    mix_own = jnp.sum(
        jnp.where(routes[:, 0][..., None] == ids, mix_weights[:, 0][..., None], 0.0), axis=2
    )
    mix_high = mix_own.astype(BF16)
    mix_low = (mix_own - mix_high.astype(F32)).astype(BF16)
    lanes = 128
    mix_pad = jnp.zeros((micro, row_count, lanes - 2 * owners), BF16)
    dy_mix = gather_rows(jnp.concatenate([dy_own, mix_high, mix_low, mix_pad], axis=-1), ring)
    dy_mix = dy_mix.reshape(rows, width + lanes)
    lane = jnp.arange(lanes, dtype=jnp.int32)
    spread = (
        (jnp.arange(hidden_width, dtype=jnp.int32)[None, :] // ff_part == (lane % owners)[:, None])
        & (lane < 2 * owners)[:, None]
    ).astype(BF16)

    k_index = jnp.arange(span, dtype=jnp.int32)
    pos = ((y + k_index // row_count) % ring) * row_count + k_index % row_count
    frequency = ROPE_BASE ** (-jnp.arange(head // 2, dtype=F32) * 2.0 / head)
    phase = pos.astype(F32)[:, None] * frequency[None, :]
    cosines, sines = jnp.cos(phase), jnp.sin(phase)
    cosines = jnp.concatenate([cosines, cosines], axis=1)
    sines = jnp.concatenate([-sines, sines], axis=1)
    allowed = (pos[None, None, :] <= pos[None, :, None]) & (
        pos[None, None, :] < len_all[:, None, None]
    )
    bias = jnp.where(allowed, 0.0, -1e30).astype(F32)

    shape = (ring, micro, row_count, width)
    head_gains = (gain_query[None], gain_key[None])
    h1, qkv, heads_out, theirs, mine = attend_call(
        functools.partial(attend_kernel, q_heads, scale),
        (x_rows, gain_attn[None], shared, cosines, sines, bias, *head_gains, dy_mix),
        ("rows", "", "", "", "", "bias", "", "", "token"),
        (
            ("rows", width, BF16),
            ("rows", qkv_width, F32),
            ("rows", q_width, BF16),
            ("parts", width, BF16),
        ),
        [pltpu.VMEM((span, q_width), BF16), pltpu.VMEM((span, width), BF16)],
        shape,
        "attention",
        TINY,
    )
    attn_own = scatter_rows(theirs[0], mine[0])
    x1 = x_own.astype(F32) + attn_own
    inverse_mid = inverse_rms(x1)
    h2 = gather_rows((x1 * inverse_mid * gain_moe).astype(BF16), ring).reshape(rows, width)

    d_gate, d_up, hidden, theirs, mine = experts_call(h2, dy_mix, expert_all, spread, ff_part)
    grad_experts, token = expert_grads_call(
        d_gate, d_up, hidden, h2, dy_mix, owners, ff_part
    )
    pieces = add_call(swap(theirs.reshape(shape)), mine.reshape(shape), token)
    d_h2 = ring_sum(pieces)
    moe_theirs, moe_mine = expert_out_call(hidden, expert_all, token, ff_part)

    grad_gain_moe = jnp.sum(d_h2 * x1 * inverse_mid, axis=(0, 1))
    d_x1 = dy_own.astype(F32) + norm_back(d_h2, x1, inverse_mid, gain_moe)
    grad_experts = lax.psum_scatter(
        after_call(grad_experts, pieces[1]), "experts", scatter_dimension=0, tiled=False
    )
    moe_pieces = add_placed_call(
        where, swap(moe_theirs.reshape(shape)), moe_mine.reshape(shape), hidden
    )
    d_mine = after_call(ring_stack(d_x1.astype(BF16), ring), moe_pieces)
    d_theirs = swap(d_mine)
    grad_out = out_grads_call(
        heads_out.reshape(2, rows // 2, q_width),
        d_mine.reshape(-1, width),
        d_theirs.reshape(-1, width),
    )
    grad_out = grad_out.reshape(owners, out_part, width)
    d_qkv, theirs, mine, sum_q, sum_k, sum_x = attend_call(
        functools.partial(attend_back_kernel, q_heads, scale),
        (
            d_theirs[None],
            d_mine[None],
            x_rows,
            gain_attn[None],
            shared,
            cosines,
            sines,
            bias,
            *head_gains,
            qkv,
            moe_pieces,
            grad_out,
        ),
        (
            "theirs",
            "mine",
            "rows",
            "",
            "",
            "",
            "",
            "bias",
            "",
            "",
            "rows",
            "token",
            "token",
        ),
        (
            ("rows", qkv_width, BF16),
            ("parts", width, BF16),
            ("sum", head, F32),
            ("sum", head, F32),
            ("sum", width, F32),
        ),
        [pltpu.VMEM((span, qkv_width), BF16)],
        shape,
        "attention_back",
        pl.CostEstimate(flops=9_000_000_000, bytes_accessed=90_000_000, transcendentals=0),
    )
    output = (x1 + exchange_sum(moe_pieces, d_qkv)).astype(BF16)[:, None]
    grad_gain_query, grad_gain_key, grad_gain_attn = sum_q[0], sum_k[0], sum_x[0]
    h1, d_qkv = h1.reshape(rows, width), d_qkv.reshape(rows, qkv_width)

    grad_gains = jnp.concatenate(
        [
            grad_gain_attn.reshape(owners, depth),
            grad_gain_moe.reshape(owners, depth),
            grad_gain_query.reshape(owners, eighth),
            grad_gain_key.reshape(owners, eighth),
        ],
        axis=1,
    ).astype(BF16)
    grad_gains = jnp.pad(
        grad_gains[:, None], ((0, 0), (0, 15), (0, shared.shape[2] - grad_gains.shape[1]))
    )
    index = lax.axis_index("experts")
    place = jnp.stack([index // SIDE, index % SIDE]).astype(jnp.int32)
    firsts, seconds = attend_grads_call(
        place, h1, d_qkv, grad_out, grad_gains, output, depth // 2 + 16
    )
    h1_theirs = swap(theirs[0])
    h1_pieces = add_placed_call(where, h1_theirs, mine[0], firsts[1])
    d_h1 = exchange_sum(h1_pieces)
    x_f32 = x_own.astype(F32)
    input_grad = (d_x1 + norm_back(d_h1, x_f32, inverse_rms(x_f32), gain_attn))[:, None]
    grad_experts = after_call(grad_experts, firsts[1], h1_theirs)
    all_experts = lax.all_gather(grad_experts, GROUP, axis=0, tiled=False)
    firsts, seconds = plane_send(firsts, 1, 0), plane_send(seconds, 0, 1)
    firsts, seconds = half_sum_call(place, firsts, seconds, h1_pieces)
    result_gate, result_up, result_down = gate_up_down_call(all_experts, ff_part)
    grads = last_sum_call(plane_send(firsts, 0, 1), plane_send(seconds, 1, 0), input_grad)
    out_sum = jnp.concatenate(
        [grads[k * out_part : (k + 1) * out_part, qkv_width:] for k in range(depth // out_part)],
        axis=1,
    )
    result_q, result_k, result_v, gain_sum = columns_call(
        where, *gather_members(grads[:, :qkv_width]), depth, q_width, head
    )
    out_sum = after_call(lax.ppermute(out_sum, EVERY, back), result_down)
    result_out = rows_call(where, *gather_members(out_sum, result_q))
    gain_sum = gain_sum[0]
    return (
        output,
        input_grad,
        result_q,
        result_k,
        result_v,
        result_out,
        gain_sum[:depth],
        gain_sum[depth : 2 * depth],
        gain_sum[2 * depth : 2 * depth + eighth],
        gain_sum[2 * depth + eighth : 2 * depth + 2 * eighth],
        result_gate[None],
        result_up[None],
        result_down[None],
    )


def solution(mesh):
    rows = P(None, ("experts", "dp"), "context", None)
    in_specs = (
        rows,
        P(None, ("experts", "dp")),
        rows,
        rows,
        rows,
        P("experts", None),
        P("experts", None),
        P("experts", None),
        P("experts", None),
        P("experts"),
        P("experts"),
        P("experts"),
        P("experts"),
        P("experts", None, None),
        P("experts", None, None),
        P("experts", None, None),
    )
    out_specs = (
        rows,
        rows,
        P("experts", None),
        P("experts", None),
        P("experts", None),
        P("experts", None),
        P("experts"),
        P("experts"),
        P("experts"),
        P("experts"),
        P("experts", None, None),
        P("experts", None, None),
        P("experts", None, None),
    )
    return jax.shard_map(local, mesh=mesh, in_specs=in_specs, out_specs=out_specs, check_vma=False)
```

```python
import functools

import jax
import jax.numpy as jnp
from jax import lax
from jax.experimental import pallas as pl
from jax.experimental.pallas import tpu as pltpu
from jax.sharding import PartitionSpec as P

EPS = 1e-06
ROPE_BASE = 1000000.0
F32 = jnp.float32
BF16 = jnp.bfloat16
GROUP = ("context", "dp")
EVERY = ("experts", "context", "dp")
VMEM = 60 * 1024 * 1024
SIDE = 4
TINY = pl.CostEstimate(flops=0, bytes_accessed=1000, transcendentals=0)


def inverse_rms(v):
    return lax.rsqrt(jnp.mean(v * v, axis=-1, keepdims=True) + EPS)


def norm_back(grad_in, v, inverse, gain):
    scaled = grad_in * gain
    return inverse * scaled - v * inverse**3 * jnp.mean(scaled * v, axis=-1, keepdims=True)


def matmul(left, right):
    return jnp.dot(left, right, preferred_element_type=F32)


def against(left, right):
    return lax.dot_general(left, right, (((1,), (1,)), ((), ())), preferred_element_type=F32)


def outer(left, right):
    return lax.dot_general(left, right, (((0,), (0,)), ((), ())), preferred_element_type=F32)


def swap(v):
    return lax.ppermute(v, "dp", [(0, 1), (1, 0)])


def ring_stack(own, ring):
    pieces = [own]
    for k in range(1, ring):
        pieces.append(lax.ppermute(own, "context", [((i + k) % ring, i) for i in range(ring)]))
    return jnp.stack(pieces)


def gather_rows(own, ring):
    mine = ring_stack(own, ring)
    return jnp.stack([mine, swap(mine)])


def ring_sum(pieces):
    ring = len(pieces)
    total = pieces[0].astype(F32)
    for k in range(1, ring):
        got = lax.ppermute(pieces[k], "context", [(i, (i + k) % ring) for i in range(ring)])
        total = total + got.astype(F32)
    return total


def add_cores(theirs, mine):
    other = swap(theirs)
    return [
        (mine[k].astype(F32) + other[k].astype(F32)).astype(BF16) for k in range(mine.shape[0])
    ]


def scatter_rows(theirs, mine):
    return ring_sum(add_cores(theirs, mine))


def gather_members(v, *tokens):
    ring = lax.axis_size("context")
    pieces = [after_call(v, *tokens) if tokens else v]
    for k in range(1, ring):
        pieces.append(lax.ppermute(v, "context", [((i + k) % ring, i) for i in range(ring)]))
    mine = jnp.stack(pieces)
    return mine, swap(mine)


def plane(v, dx, dz):
    moves = [
        (((i // SIDE + dx) % SIDE) * SIDE + (i % SIDE + dz) % SIDE, i) for i in range(SIDE * SIDE)
    ]
    return lax.ppermute(v, "experts", moves)


def after_kernel(v_ref, *refs):
    pass


def after_call(v, *tokens):
    anywhere = pl.BlockSpec(memory_space=pl.ANY)
    return pl.pallas_call(
        after_kernel,
        in_specs=[anywhere] * (1 + len(tokens)),
        out_specs=anywhere,
        out_shape=jax.ShapeDtypeStruct(v.shape, v.dtype),
        input_output_aliases={0: 0},
        cost_estimate=TINY,
        name="after",
    )(v, *tokens)


def rope(v, cosines, sines):
    return v * cosines + pltpu.roll(v, v.shape[-1] // 2, 1) * sines


def rope_back(v, cosines, sines):
    return v * cosines + pltpu.roll(v * sines, v.shape[-1] // 2, 1)


def flat(ref):
    v = ref[...]
    return v.reshape(v.shape[1] * v.shape[3], v.shape[4])


def chunks(ref, columns):
    v = ref[:, :-16, :columns]
    return v.reshape(v.shape[0] * v.shape[1], columns)


def out_blocks(ref, first):
    last = ref.shape[2] - first
    rows = last // ref.shape[0]
    for k in range((ref.shape[1] - 16) // rows):
        yield k * last, (k + 1) * last, ref[:, k * rows : (k + 1) * rows, first:].reshape(last, last)


def put(ref, v):
    ref[...] = v.reshape(ref.shape).astype(ref.dtype)


def attend_kernel(
    heads,
    scale,
    x_ref,
    gain_ref,
    w_ref,
    cos_ref,
    sin_ref,
    bias_ref,
    gain_q_ref,
    gain_k_ref,
    token_ref,
    h1_ref,
    qkv_ref,
    heads_ref,
    theirs_ref,
    mine_ref,
    heads_out,
    total,
):
    size = cos_ref.shape[1]
    x = flat(x_ref).astype(F32)
    h1 = (x * inverse_rms(x) * gain_ref[...]).astype(BF16)
    put(h1_ref, h1)
    width = (heads + 2) * size
    qkv = matmul(h1, chunks(w_ref, width))
    put(qkv_ref, qkv)
    cosines, sines, bias = cos_ref[...], sin_ref[...], bias_ref[0]
    k_pre = qkv[:, heads * size : (heads + 1) * size]
    key = rope(k_pre * inverse_rms(k_pre) * gain_k_ref[...], cosines, sines).astype(BF16)
    value = qkv[:, (heads + 1) * size :].astype(BF16)
    for g in range(heads):
        q_pre = qkv[:, g * size : (g + 1) * size]
        query = rope(q_pre * inverse_rms(q_pre) * gain_q_ref[...], cosines, sines).astype(BF16)
        logits = against(query, key) * scale + bias
        scaled = jnp.exp(logits - jnp.max(logits, axis=-1, keepdims=True))
        soft = (scaled * (1.0 / jnp.sum(scaled, axis=-1, keepdims=True))).astype(BF16)
        heads_out[:, g * size : (g + 1) * size] = matmul(soft, value).astype(BF16)
    out = heads_out[...]
    put(heads_ref, out)
    for first, last, block in out_blocks(w_ref, width):
        total[:, first:last] = matmul(out, block).astype(BF16)

    @pl.when(pl.program_id(0) < 2)
    def _():
        put(theirs_ref, total[...])

    @pl.when(pl.program_id(0) >= 2)
    def _():
        put(mine_ref, total[...])


def attend_back_kernel(
    heads,
    scale,
    theirs_da_ref,
    mine_da_ref,
    x_ref,
    gain_ref,
    w_ref,
    cos_ref,
    sin_ref,
    bias_ref,
    gain_q_ref,
    gain_k_ref,
    qkv_ref,
    token_ref,
    other_token_ref,
    d_qkv_ref,
    theirs_ref,
    mine_ref,
    sum_q_ref,
    sum_k_ref,
    sum_x_ref,
    d_qkv,
):
    size = cos_ref.shape[1]
    step = pl.program_id(0)

    @pl.when(step == 0)
    def _():
        sum_q_ref[...] = jnp.zeros_like(sum_q_ref)
        sum_k_ref[...] = jnp.zeros_like(sum_k_ref)
        sum_x_ref[...] = jnp.zeros_like(sum_x_ref)

    width = (heads + 2) * size
    da = jnp.where(step < 2, flat(theirs_da_ref), flat(mine_da_ref))
    d_heads = None
    for first, last, block in out_blocks(w_ref, width):
        piece = against(da[:, first:last], block)
        d_heads = piece if d_heads is None else d_heads + piece
    d_heads = d_heads.astype(BF16)
    qkv = flat(qkv_ref)
    cosines, sines, bias = cos_ref[...], sin_ref[...], bias_ref[0]
    gain_q, gain_k = gain_q_ref[...], gain_k_ref[...]
    k_pre = qkv[:, heads * size : (heads + 1) * size]
    inverse_k = inverse_rms(k_pre)
    key = rope(k_pre * inverse_k * gain_k, cosines, sines).astype(BF16)
    value = qkv[:, (heads + 1) * size :].astype(BF16)
    d_key = jnp.zeros(k_pre.shape, F32)
    d_value = jnp.zeros(k_pre.shape, F32)
    sum_q = jnp.zeros((1, size), F32)
    for g in range(heads):
        q_pre = qkv[:, g * size : (g + 1) * size]
        inverse_q = inverse_rms(q_pre)
        query = rope(q_pre * inverse_q * gain_q, cosines, sines).astype(BF16)
        logits = against(query, key) * scale + bias
        scaled = jnp.exp(logits - jnp.max(logits, axis=-1, keepdims=True))
        probs = scaled * (1.0 / jnp.sum(scaled, axis=-1, keepdims=True))
        d_head = d_heads[:, g * size : (g + 1) * size]
        d_probs = against(d_head, value)
        d_scores = probs * (d_probs - jnp.sum(probs * d_probs, axis=-1, keepdims=True))
        d_scores = d_scores.astype(BF16)
        d_query = rope_back(matmul(d_scores, key) * scale, cosines, sines)
        d_key = d_key + outer(d_scores, query)
        d_value = d_value + outer(probs.astype(BF16), d_head)
        sum_q = sum_q + jnp.sum(d_query * q_pre * inverse_q, axis=0, keepdims=True)
        d_qkv[:, g * size : (g + 1) * size] = norm_back(d_query, q_pre, inverse_q, gain_q).astype(
            BF16
        )
    d_key = rope_back(d_key * scale, cosines, sines)
    sum_k = jnp.sum(d_key * k_pre * inverse_k, axis=0, keepdims=True)
    d_qkv[:, heads * size : (heads + 1) * size] = norm_back(d_key, k_pre, inverse_k, gain_k).astype(
        BF16
    )
    d_qkv[:, (heads + 1) * size :] = d_value.astype(BF16)
    grads = d_qkv[...]
    put(d_qkv_ref, grads)
    part = against(grads, chunks(w_ref, width))
    x = flat(x_ref).astype(F32)
    sum_x_ref[0:1, :] += jnp.sum(part * (x * inverse_rms(x)), axis=0, keepdims=True)
    sum_q_ref[0:1, :] += sum_q
    sum_k_ref[0:1, :] += sum_k

    @pl.when(step < 2)
    def _():
        put(theirs_ref, part)

    @pl.when(step >= 2)
    def _():
        put(mine_ref, part)


def attend_call(kernel, operands, extra, outputs, scratch, shape, name, cost):
    ring, micro, row_count, width = shape

    def rows_spec(last):
        return pl.BlockSpec(
            (1, ring, 1, row_count, last), lambda b: (1 - b // 2, 0, b % 2, 0, 0)
        )

    def whole(v):
        return pl.BlockSpec(v.shape, lambda b: (0,) * v.ndim)

    def slot_spec(v, kind):
        block = (1, ring, 1, row_count, v.shape[-1])
        if kind == "theirs":
            return pl.BlockSpec(block, lambda b: (0, 0, jnp.minimum(b, 1), 0, 0))
        return pl.BlockSpec(block, lambda b: (0, 0, jnp.maximum(b - 2, 0), 0, 0))

    in_specs = [
        rows_spec(v.shape[-1])
        if kind == "rows"
        else slot_spec(v, kind)
        if kind in ("theirs", "mine")
        else pl.BlockSpec((1,) + v.shape[1:], lambda b: ((1 - b // 2) * micro + b % 2, 0, 0))
        if kind == "bias"
        else pl.BlockSpec(memory_space=pl.ANY)
        if kind == "token"
        else whole(v)
        for v, kind in zip(operands, extra)
    ]
    out_shape, out_specs = [], []
    for kind, last, dtype in outputs:
        if kind == "rows":
            out_shape.append(jax.ShapeDtypeStruct((2, ring, micro, row_count, last), dtype))
            out_specs.append(rows_spec(last))
        elif kind == "parts":
            one = jax.ShapeDtypeStruct((1, ring, micro, row_count, last), dtype)
            out_shape += [one, one]
            block = (1, ring, 1, row_count, last)
            out_specs.append(pl.BlockSpec(block, lambda b: (0, 0, jnp.minimum(b, 1), 0, 0)))
            out_specs.append(pl.BlockSpec(block, lambda b: (0, 0, jnp.maximum(b - 2, 0), 0, 0)))
        else:
            out_shape.append(jax.ShapeDtypeStruct((8, last), dtype))
            out_specs.append(pl.BlockSpec((8, last), lambda b: (0, 0)))
    return pl.pallas_call(
        kernel,
        grid=(2 * micro,),
        in_specs=in_specs,
        out_specs=out_specs,
        out_shape=out_shape,
        scratch_shapes=scratch,
        compiler_params=pltpu.CompilerParams(vmem_limit_bytes=VMEM),
        cost_estimate=cost,
        name=name,
    )(*operands)


def experts_kernel(
    part, h2_ref, dy_ref, w_ref, spread_ref, dg_ref, du_ref, hid_ref, theirs_ref, mine_ref, acc
):
    chunk, block = pl.program_id(0), pl.program_id(1)
    width = h2_ref.shape[1]
    count = w_ref.shape[0] * part
    gate_w = w_ref[:, :part].reshape(count, width)
    up_w = w_ref[:, part : 2 * part].reshape(count, width)
    down_w = w_ref[:, 2 * part :].reshape(count, width)
    h2 = h2_ref[...]
    mix = matmul(dy_ref[:, width:], spread_ref[...])
    gate = against(h2, gate_w)
    up = against(h2, up_w)
    d_hidden = against(dy_ref[:, :width], down_w) * mix
    sigma = jax.nn.sigmoid(gate)
    silu = gate * sigma
    hid_ref[...] = (silu * up * mix).astype(BF16)
    d_gate = (d_hidden * up * sigma * (1.0 + gate * (1.0 - sigma))).astype(BF16)
    d_up = (d_hidden * silu).astype(BF16)
    dg_ref[...] = d_gate
    du_ref[...] = d_up
    total = matmul(d_gate, gate_w) + matmul(d_up, up_w)

    @pl.when(chunk == 0)
    def _():
        acc[block] = total

    @pl.when((chunk == 1) & (block < 2))
    def _():
        theirs_ref[...] = (acc[block] + total).astype(BF16)

    @pl.when((chunk == 1) & (block >= 2))
    def _():
        mine_ref[...] = (acc[block] + total).astype(BF16)


def experts_call(h2, dy, weights, spread, part):
    rows, width = h2.shape
    owners, depth, _ = weights.shape
    hidden = owners * part
    n, blocks = 2, 4
    step, wide = rows // blocks, hidden // n
    half = jax.ShapeDtypeStruct((rows // 2, width), BF16)
    wide_shape = jax.ShapeDtypeStruct((rows, hidden), BF16)

    def row(c, b):
        return (b + blocks // 2) % blocks

    wide_spec = pl.BlockSpec((step, wide), lambda c, b: (row(c, b), c))
    return pl.pallas_call(
        functools.partial(experts_kernel, part),
        grid=(n, blocks),
        in_specs=[
            pl.BlockSpec((step, width), lambda c, b: (row(c, b), 0)),
            pl.BlockSpec((step, dy.shape[1]), lambda c, b: (row(c, b), 0)),
            pl.BlockSpec((owners // n, depth, width), lambda c, b: (c, 0, 0)),
            pl.BlockSpec((spread.shape[0], wide), lambda c, b: (0, c)),
        ],
        out_specs=[
            wide_spec,
            wide_spec,
            wide_spec,
            pl.BlockSpec((step, width), lambda c, b: (c * jnp.minimum(b, 1), 0)),
            pl.BlockSpec((step, width), lambda c, b: (c * jnp.maximum(b - 2, 0), 0)),
        ],
        out_shape=[wide_shape, wide_shape, wide_shape, half, half],
        scratch_shapes=[pltpu.VMEM((blocks, step, width), F32)],
        compiler_params=pltpu.CompilerParams(vmem_limit_bytes=VMEM),
        cost_estimate=TINY,
        name="experts_rows",
    )(h2, dy, weights, spread)


def expert_grads_kernel(
    part, dg_ref, du_ref, hid_ref, h2_ref, dy_ref, out_ref, token_ref
):
    width = h2_ref.shape[1]
    group = out_ref.shape[0]
    h2 = h2_ref[...]
    out_ref[:, :part] = outer(dg_ref[...], h2).astype(BF16).reshape(group, part, width)
    out_ref[:, part : 2 * part] = outer(du_ref[...], h2).astype(BF16).reshape(group, part, width)
    out_ref[:, 2 * part :] = (
        outer(hid_ref[...], dy_ref[:, :width]).astype(BF16).reshape(group, part, width)
    )
    token_ref[...] = jnp.zeros_like(token_ref)


def expert_grads_call(d_gate, d_up, hidden, h2, dy, owners, part):
    rows, width = h2.shape
    n = 4
    wide = d_gate.shape[1] // n
    wide_spec = pl.BlockSpec((rows, wide), lambda c: (0, c))
    return pl.pallas_call(
        functools.partial(expert_grads_kernel, part),
        grid=(n,),
        in_specs=[
            wide_spec,
            wide_spec,
            wide_spec,
            pl.BlockSpec((rows, width), lambda c: (0, 0)),
            pl.BlockSpec((rows, dy.shape[1]), lambda c: (0, 0)),
        ],
        out_specs=[
            pl.BlockSpec((owners // n, 3 * part, width), lambda c: (c, 0, 0)),
            pl.BlockSpec((8, 128), lambda c: (0, 0)),
        ],
        out_shape=[
            jax.ShapeDtypeStruct((owners, 3 * part, width), BF16),
            jax.ShapeDtypeStruct((8, 128), F32),
        ],
        compiler_params=pltpu.CompilerParams(vmem_limit_bytes=VMEM),
        cost_estimate=TINY,
        name="experts_weights",
    )(d_gate, d_up, hidden, h2, dy)


def add_placed_kernel(where_ref, theirs_ref, mine_ref, token_ref, out_ref):
    ring = mine_ref.shape[0]
    for k in range(ring):
        out_ref[lax.rem(where_ref[0] + k, ring)] = (
            theirs_ref[k].astype(F32) + mine_ref[k].astype(F32)
        ).astype(BF16)


def add_placed_call(where, theirs, mine, token):
    vmem = pl.BlockSpec(memory_space=pltpu.VMEM)
    return pl.pallas_call(
        add_placed_kernel,
        grid_spec=pltpu.PrefetchScalarGridSpec(
            num_scalar_prefetch=1,
            grid=(),
            in_specs=[vmem, vmem, pl.BlockSpec(memory_space=pl.ANY)],
            out_specs=vmem,
        ),
        out_shape=jax.ShapeDtypeStruct(mine.shape, BF16),
        compiler_params=pltpu.CompilerParams(vmem_limit_bytes=VMEM),
        cost_estimate=TINY,
        name="add_cores_placed",
    )(where, theirs, mine, token)


def exchange_sum(pieces, token=None):
    got = lax.all_to_all(pieces, "context", split_axis=0, concat_axis=0, tiled=True)
    if token is not None:
        got = after_call(got, token)
    return jnp.sum(got.astype(F32), axis=0)


def add_kernel(theirs_ref, mine_ref, token_ref, *out_refs):
    for k, out_ref in enumerate(out_refs):
        out_ref[...] = (theirs_ref[k].astype(F32) + mine_ref[k].astype(F32)).astype(BF16)


def add_call(theirs, mine, token):
    shape = theirs.shape
    one = jax.ShapeDtypeStruct(shape[1:], BF16)
    vmem = pl.BlockSpec(memory_space=pltpu.VMEM)
    return pl.pallas_call(
        add_kernel,
        in_specs=[vmem, vmem, pl.BlockSpec(memory_space=pl.ANY)],
        out_specs=[vmem] * shape[0],
        out_shape=[one] * shape[0],
        compiler_params=pltpu.CompilerParams(vmem_limit_bytes=VMEM),
        cost_estimate=TINY,
        name="add_cores",
    )(theirs, mine, token)


def gate_up_down_kernel(part, in_ref, gate_ref, up_ref, down_ref):
    last = in_ref.shape[2]
    count = in_ref.shape[0] * part
    gate_ref[...] = in_ref[:, :part].reshape(count, last).astype(F32).T
    up_ref[...] = in_ref[:, part : 2 * part].reshape(count, last).astype(F32).T
    down_ref[...] = in_ref[:, 2 * part :].reshape(count, last).astype(F32)


def gate_up_down_call(gathered, part):
    members, depth, width = gathered.shape
    ff = members * part
    n = 8
    step = width // n
    return pl.pallas_call(
        functools.partial(gate_up_down_kernel, part),
        grid=(n,),
        in_specs=[pl.BlockSpec((members, depth, step), lambda c: (0, 0, c))],
        out_specs=[
            pl.BlockSpec((step, ff), lambda c: (c, 0)),
            pl.BlockSpec((step, ff), lambda c: (c, 0)),
            pl.BlockSpec((ff, step), lambda c: (0, c)),
        ],
        out_shape=[
            jax.ShapeDtypeStruct((width, ff), F32),
            jax.ShapeDtypeStruct((width, ff), F32),
            jax.ShapeDtypeStruct((ff, width), F32),
        ],
        compiler_params=pltpu.CompilerParams(vmem_limit_bytes=VMEM),
        cost_estimate=TINY,
        name="experts_results",
    )(gathered)


def out_grads_kernel(heads_ref, mine_ref, theirs_ref, out_ref):
    total = outer(heads_ref[0], mine_ref[...]) + outer(heads_ref[1], theirs_ref[...])
    out_ref[...] = total.astype(BF16)


def out_grads_call(heads_out, mine, theirs):
    _, half, columns = heads_out.shape
    width = mine.shape[1]
    n = 4
    spec = pl.BlockSpec((half, width // n), lambda c: (0, c))
    return pl.pallas_call(
        out_grads_kernel,
        grid=(n,),
        in_specs=[pl.BlockSpec(heads_out.shape, lambda c: (0, 0, 0)), spec, spec],
        out_specs=pl.BlockSpec((columns, width // n), lambda c: (0, c)),
        out_shape=jax.ShapeDtypeStruct((columns, width), BF16),
        compiler_params=pltpu.CompilerParams(vmem_limit_bytes=VMEM),
        cost_estimate=TINY,
        name="out_weights",
    )(heads_out, mine, theirs)


def attend_grads_kernel(
    cut, place_ref, h1_ref, d_qkv_ref, out_ref, gains_ref, token_ref, *refs
):
    firsts, seconds, share = refs[:SIDE], refs[SIDE : 2 * SIDE], refs[-1]
    step = pl.program_id(0)
    last = d_qkv_ref.shape[1]
    depth = share.shape[1] - 16
    grad = outer(h1_ref[...], d_qkv_ref[...]).astype(BF16)
    share[:, :depth, :last] = grad.reshape(SIDE, depth, last)
    rows, columns = out_ref.shape[1], share.shape[2] - last
    for k in range(depth // rows):
        share[:, k * rows : (k + 1) * rows, last:] = out_ref[:, :, k * columns : (k + 1) * columns]
    share[:, depth:] = gains_ref[...]
    for k in range(SIDE):

        @pl.when(step == k)
        def _():
            firsts[k][...] = share[:, :cut]

        seconds[k][0] = share[lax.rem(place_ref[1] + k, SIDE), cut:]


def attend_grads_call(place, h1, d_qkv, grad_out, gains, token, cut):
    rows, width = h1.shape
    owners, extra, columns = gains.shape
    depth = width // owners
    last = d_qkv.shape[1]

    def at(i, place):
        return lax.rem(place[0] + i, SIDE)

    first = jax.ShapeDtypeStruct((SIDE, cut, columns), BF16)
    second = jax.ShapeDtypeStruct((SIDE, depth + extra - cut, columns), BF16)
    outs = pl.pallas_call(
        functools.partial(attend_grads_kernel, cut),
        grid_spec=pltpu.PrefetchScalarGridSpec(
            num_scalar_prefetch=1,
            grid=(SIDE,),
            in_specs=[
                pl.BlockSpec((rows, width // SIDE), lambda i, place: (0, at(i, place))),
                pl.BlockSpec((rows, last), lambda i, place: (0, 0)),
                pl.BlockSpec((SIDE,) + grad_out.shape[1:], lambda i, place: (at(i, place), 0, 0)),
                pl.BlockSpec((SIDE, extra, columns), lambda i, place: (at(i, place), 0, 0)),
                pl.BlockSpec(memory_space=pl.ANY),
            ],
            out_specs=[pl.BlockSpec(first.shape, lambda i, place: (0, 0, 0))] * SIDE
            + [pl.BlockSpec((1,) + second.shape[1:], lambda i, place: (i, 0, 0))] * SIDE,
            scratch_shapes=[pltpu.VMEM((SIDE, depth + extra, columns), BF16)],
        ),
        out_shape=[first] * SIDE + [second] * SIDE,
        compiler_params=pltpu.CompilerParams(vmem_limit_bytes=VMEM),
        cost_estimate=TINY,
        name="attention_weights",
    )(place, h1, d_qkv, grad_out, gains, token)
    return outs[:SIDE], outs[SIDE:]


def total_of(refs):
    total = refs[0][...].astype(F32)
    for ref in refs[1:]:
        total = total + ref[...].astype(F32)
    return total.astype(BF16)


def half_sum_kernel(place_ref, *refs):
    outs, total = refs[2 * SIDE + 1 : -1], refs[-1]
    firsts, seconds = outs[:SIDE], outs[SIDE:]
    total[...] = total_of(refs[:SIDE])
    other = total_of(refs[SIDE : 2 * SIDE])
    for k in range(SIDE):
        firsts[k][...] = total[lax.rem(place_ref[1] + k, SIDE)]
        seconds[k][...] = other[k]


def half_sum_call(place, firsts, seconds, token):
    vmem = pl.BlockSpec(memory_space=pltpu.VMEM)
    outs = pl.pallas_call(
        half_sum_kernel,
        grid_spec=pltpu.PrefetchScalarGridSpec(
            num_scalar_prefetch=1,
            grid=(),
            in_specs=[vmem] * (2 * SIDE) + [pl.BlockSpec(memory_space=pl.ANY)],
            out_specs=[vmem] * (2 * SIDE),
            scratch_shapes=[pltpu.VMEM(firsts[0].shape, BF16)],
        ),
        out_shape=[jax.ShapeDtypeStruct(v.shape[1:], BF16) for v in (*firsts, *seconds)],
        compiler_params=pltpu.CompilerParams(vmem_limit_bytes=VMEM),
        cost_estimate=TINY,
        name="half_sum",
    )(place, *firsts, *seconds, token)
    return outs[:SIDE], outs[SIDE:]


def last_sum_kernel(token_ref, *refs):
    out = refs[-1]
    cut = refs[0].shape[0]
    out[:cut] = total_of(refs[:SIDE])
    out[cut:] = total_of(refs[SIDE : 2 * SIDE])


def last_sum_call(firsts, seconds, token):
    rows, columns = firsts[0].shape[0] + seconds[0].shape[0], firsts[0].shape[1]
    vmem = pl.BlockSpec(memory_space=pltpu.VMEM)
    return pl.pallas_call(
        last_sum_kernel,
        in_specs=[pl.BlockSpec(memory_space=pl.ANY)] + [vmem] * (2 * SIDE),
        out_specs=vmem,
        out_shape=jax.ShapeDtypeStruct((rows, columns), BF16),
        compiler_params=pltpu.CompilerParams(vmem_limit_bytes=VMEM),
        cost_estimate=TINY,
        name="last_sum",
    )(token, *firsts, *seconds)


def plane_send(pieces, dx, dz):
    return [pieces[0]] + [plane(pieces[k], -k * dx, -k * dz) for k in range(1, SIDE)]


def columns_kernel(heads_width, size, where_ref, mine_ref, theirs_ref, q_ref, k_ref, v_ref, sum_ref):
    depth = q_ref.shape[0]
    mine, theirs = mine_ref[0].astype(F32), theirs_ref[0].astype(F32)
    first = where_ref[1] == 0
    q_ref[:, :heads_width] = jnp.where(first, mine[:depth, :heads_width], theirs[:depth, :heads_width])
    q_ref[:, heads_width:] = jnp.where(first, theirs[:depth, :heads_width], mine[:depth, :heads_width])
    both = mine + theirs
    k_ref[...] = both[:depth, heads_width : heads_width + size]
    v_ref[...] = both[:depth, heads_width + size :]

    @pl.when(pl.program_id(0) == 0)
    def _():
        sum_ref[...] = jnp.zeros_like(sum_ref)

    sum_ref[...] += both[depth:]


def columns_call(where, mine, theirs, depth, heads_width, size):
    ring, rows, last = mine.shape
    cores = 2

    def at(k, where):
        return (0, lax.rem(where[0] + k, ring))

    return pl.pallas_call(
        functools.partial(columns_kernel, heads_width, size),
        grid_spec=pltpu.PrefetchScalarGridSpec(
            num_scalar_prefetch=1,
            grid=(ring,),
            in_specs=[pl.BlockSpec((1, rows, last), lambda k, where: (k, 0, 0))] * 2,
            out_specs=[
                pl.BlockSpec((depth, cores * heads_width), at),
                pl.BlockSpec((depth, size), at),
                pl.BlockSpec((depth, size), at),
                pl.BlockSpec((rows - depth, last), lambda k, where: (0, 0)),
            ],
        ),
        out_shape=[
            jax.ShapeDtypeStruct((depth, ring * cores * heads_width), F32),
            jax.ShapeDtypeStruct((depth, ring * size), F32),
            jax.ShapeDtypeStruct((depth, ring * size), F32),
            jax.ShapeDtypeStruct((rows - depth, last), F32),
        ],
        compiler_params=pltpu.CompilerParams(vmem_limit_bytes=VMEM),
        cost_estimate=TINY,
        name="columns_results",
    )(where, mine, theirs)


def rows_kernel(where_ref, mine_ref, theirs_ref, out_ref):
    count = mine_ref.shape[1]
    mine, theirs = mine_ref[0].astype(F32), theirs_ref[0].astype(F32)
    first = where_ref[1] == 0
    out_ref[:count] = jnp.where(first, mine, theirs)
    out_ref[count:] = jnp.where(first, theirs, mine)


def rows_call(where, mine, theirs):
    ring, count, width = mine.shape
    cores = 2
    return pl.pallas_call(
        rows_kernel,
        grid_spec=pltpu.PrefetchScalarGridSpec(
            num_scalar_prefetch=1,
            grid=(ring,),
            in_specs=[pl.BlockSpec((1, count, width), lambda k, where: (k, 0, 0))] * 2,
            out_specs=pl.BlockSpec(
                (cores * count, width), lambda k, where: (lax.rem(where[0] + k, ring), 0)
            ),
        ),
        out_shape=jax.ShapeDtypeStruct((ring * cores * count, width), F32),
        compiler_params=pltpu.CompilerParams(vmem_limit_bytes=VMEM),
        cost_estimate=TINY,
        name="rows_results",
    )(where, mine, theirs)


def expert_out_kernel(part, hid_ref, w_ref, token_ref, theirs_ref, mine_ref):
    width = w_ref.shape[2]
    block = pl.program_id(0)
    total = matmul(hid_ref[...], w_ref[...].reshape(w_ref.shape[0] * part, width)).astype(BF16)

    @pl.when(block < 2)
    def _():
        theirs_ref[...] = total

    @pl.when(block >= 2)
    def _():
        mine_ref[...] = total


def expert_out_call(hidden, weights, token, part):
    rows, wide = hidden.shape
    owners, _, width = weights.shape
    blocks = 4
    step = rows // blocks
    half = jax.ShapeDtypeStruct((rows // 2, width), BF16)
    return pl.pallas_call(
        functools.partial(expert_out_kernel, part),
        grid=(blocks,),
        in_specs=[
            pl.BlockSpec((step, wide), lambda b: ((b + blocks // 2) % blocks, 0)),
            pl.BlockSpec((owners, part, width), lambda b: (0, 2, 0)),
            pl.BlockSpec(memory_space=pl.ANY),
        ],
        out_specs=[
            pl.BlockSpec((step, width), lambda b: (jnp.minimum(b, 1), 0)),
            pl.BlockSpec((step, width), lambda b: (jnp.maximum(b - 2, 0), 0)),
        ],
        out_shape=[half, half],
        compiler_params=pltpu.CompilerParams(vmem_limit_bytes=VMEM),
        cost_estimate=pl.CostEstimate(
            flops=2 * rows * wide * width, bytes_accessed=20_000_000, transcendentals=0
        ),
        name="experts_out",
    )(hidden, weights, token)


def local(
    tokens,
    lengths,
    routes,
    mix_weights,
    cotangent,
    w_query,
    key_weight,
    value_weight,
    w_out,
    norm_attn,
    norm_moe,
    norm_query,
    norm_key,
    w_gate,
    w_up,
    w_down,
):
    owners = lax.axis_size("experts")
    ring = lax.axis_size("context")
    cores = lax.axis_size("dp")
    members = ring * cores
    y = lax.axis_index("context")
    d = lax.axis_index("dp")
    j = y * cores + d
    micro, _, row_count, width = tokens.shape
    head = norm_query.shape[0] * owners
    q_width = w_query.shape[1] // members
    q_heads = q_width // head
    depth = w_query.shape[0]
    ff = w_gate.shape[2]
    ff_part = ff // members
    out_rows = w_out.shape[0]
    out_part = out_rows // members
    seqs = cores * micro
    span = ring * row_count
    rows = seqs * span
    scale = head ** (-0.5)

    forth = [
        (es * members + k, ((es % cores) * members + k) * members + es // cores)
        for es in range(owners)
        for k in range(members)
    ]
    back = [(b, a) for a, b in forth]
    out_chunk = lax.ppermute(
        lax.dynamic_slice_in_dim(w_out, j * out_part, out_part, axis=0), EVERY, forth
    )
    expert_pack = jnp.concatenate(
        [
            lax.dynamic_slice_in_dim(w_gate[0], j * ff_part, ff_part, axis=1).T,
            lax.dynamic_slice_in_dim(w_up[0], j * ff_part, ff_part, axis=1).T,
            lax.dynamic_slice_in_dim(w_down[0], j * ff_part, ff_part, axis=0),
        ],
        axis=0,
    )
    gains = jnp.concatenate([norm_attn, norm_moe, norm_query, norm_key])
    packed = jnp.concatenate(
        [
            lax.dynamic_slice_in_dim(w_query, j * q_width, q_width, axis=1),
            lax.dynamic_slice_in_dim(key_weight, y * head, head, axis=1),
            lax.dynamic_slice_in_dim(value_weight, y * head, head, axis=1),
            jnp.concatenate(jnp.split(out_chunk, depth // out_part, axis=1), axis=0),
        ],
        axis=1,
    )
    qkv_width = q_width + 2 * head
    gain_rows = jnp.pad(gains[None], ((0, 15), (0, packed.shape[1] - gains.shape[0])))
    shared = lax.all_gather(
        jnp.concatenate([packed, gain_rows]), "experts", axis=0, tiled=False
    )
    expert_all = lax.all_gather(expert_pack, "experts", axis=0, tiled=False)
    gain_row = shared[:, depth]
    gain_row = gain_row.astype(F32)
    gain_attn = gain_row[:, :depth].reshape(-1)
    gain_moe = gain_row[:, depth : 2 * depth].reshape(-1)
    eighth = norm_query.shape[0]
    gain_query = gain_row[:, 2 * depth : 2 * depth + eighth].reshape(-1)
    gain_key = gain_row[:, 2 * depth + eighth : 2 * depth + 2 * eighth].reshape(-1)
    hidden_width = owners * ff_part

    where = jnp.stack([y, d]).astype(jnp.int32)
    x_own = tokens[:, 0]
    x_rows = gather_rows(x_own, ring)
    len_all = jnp.stack([lengths[:, 0], swap(lengths[:, 0])]).reshape(seqs)
    own_pos = y * row_count + jnp.arange(row_count, dtype=jnp.int32)
    valid = (own_pos[None, :] < lengths[:, 0][:, None]).astype(F32)
    dy_own = (cotangent[:, 0].astype(F32) * valid[:, :, None]).astype(BF16)
    ids = jnp.arange(owners, dtype=jnp.int32)
    mix_own = jnp.sum(
        jnp.where(routes[:, 0][..., None] == ids, mix_weights[:, 0][..., None], 0.0), axis=2
    )
    mix_high = mix_own.astype(BF16)
    mix_low = (mix_own - mix_high.astype(F32)).astype(BF16)
    lanes = 128
    mix_pad = jnp.zeros((micro, row_count, lanes - 2 * owners), BF16)
    dy_mix = gather_rows(jnp.concatenate([dy_own, mix_high, mix_low, mix_pad], axis=-1), ring)
    dy_mix = dy_mix.reshape(rows, width + lanes)
    lane = jnp.arange(lanes, dtype=jnp.int32)
    spread = (
        (jnp.arange(hidden_width, dtype=jnp.int32)[None, :] // ff_part == (lane % owners)[:, None])
        & (lane < 2 * owners)[:, None]
    ).astype(BF16)

    k_index = jnp.arange(span, dtype=jnp.int32)
    pos = ((y + k_index // row_count) % ring) * row_count + k_index % row_count
    frequency = ROPE_BASE ** (-jnp.arange(head // 2, dtype=F32) * 2.0 / head)
    phase = pos.astype(F32)[:, None] * frequency[None, :]
    cosines, sines = jnp.cos(phase), jnp.sin(phase)
    cosines = jnp.concatenate([cosines, cosines], axis=1)
    sines = jnp.concatenate([-sines, sines], axis=1)
    allowed = (pos[None, None, :] <= pos[None, :, None]) & (
        pos[None, None, :] < len_all[:, None, None]
    )
    bias = jnp.where(allowed, 0.0, -1e30).astype(F32)

    shape = (ring, micro, row_count, width)
    head_gains = (gain_query[None], gain_key[None])
    h1, qkv, heads_out, theirs, mine = attend_call(
        functools.partial(attend_kernel, q_heads, scale),
        (x_rows, gain_attn[None], shared, cosines, sines, bias, *head_gains, dy_mix),
        ("rows", "", "", "", "", "bias", "", "", "token"),
        (
            ("rows", width, BF16),
            ("rows", qkv_width, F32),
            ("rows", q_width, BF16),
            ("parts", width, BF16),
        ),
        [pltpu.VMEM((span, q_width), BF16), pltpu.VMEM((span, width), BF16)],
        shape,
        "attention",
        TINY,
    )
    attn_own = scatter_rows(theirs[0], mine[0])
    x1 = x_own.astype(F32) + attn_own
    inverse_mid = inverse_rms(x1)
    h2 = gather_rows((x1 * inverse_mid * gain_moe).astype(BF16), ring).reshape(rows, width)

    d_gate, d_up, hidden, theirs, mine = experts_call(h2, dy_mix, expert_all, spread, ff_part)
    grad_experts, token = expert_grads_call(
        d_gate, d_up, hidden, h2, dy_mix, owners, ff_part
    )
    pieces = add_call(swap(theirs.reshape(shape)), mine.reshape(shape), token)
    d_h2 = ring_sum(pieces)
    moe_theirs, moe_mine = expert_out_call(hidden, expert_all, token, ff_part)

    grad_gain_moe = jnp.sum(d_h2 * x1 * inverse_mid, axis=(0, 1))
    d_x1 = dy_own.astype(F32) + norm_back(d_h2, x1, inverse_mid, gain_moe)
    grad_experts = lax.psum_scatter(
        after_call(grad_experts, pieces[1]), "experts", scatter_dimension=0, tiled=False
    )
    moe_pieces = add_placed_call(
        where, swap(moe_theirs.reshape(shape)), moe_mine.reshape(shape), hidden
    )
    d_mine = after_call(ring_stack(d_x1.astype(BF16), ring), moe_pieces)
    d_theirs = swap(d_mine)
    grad_out = out_grads_call(
        heads_out.reshape(2, rows // 2, q_width),
        d_mine.reshape(-1, width),
        d_theirs.reshape(-1, width),
    )
    grad_out = grad_out.reshape(owners, out_part, width)
    d_qkv, theirs, mine, sum_q, sum_k, sum_x = attend_call(
        functools.partial(attend_back_kernel, q_heads, scale),
        (
            d_theirs[None],
            d_mine[None],
            x_rows,
            gain_attn[None],
            shared,
            cosines,
            sines,
            bias,
            *head_gains,
            qkv,
            moe_pieces,
            grad_out,
        ),
        (
            "theirs",
            "mine",
            "rows",
            "",
            "",
            "",
            "",
            "bias",
            "",
            "",
            "rows",
            "token",
            "token",
        ),
        (
            ("rows", qkv_width, BF16),
            ("parts", width, BF16),
            ("sum", head, F32),
            ("sum", head, F32),
            ("sum", width, F32),
        ),
        [pltpu.VMEM((span, qkv_width), BF16)],
        shape,
        "attention_back",
        pl.CostEstimate(flops=9_000_000_000, bytes_accessed=90_000_000, transcendentals=0),
    )
    output = (x1 + exchange_sum(moe_pieces, d_qkv)).astype(BF16)[:, None]
    grad_gain_query, grad_gain_key, grad_gain_attn = sum_q[0], sum_k[0], sum_x[0]
    h1, d_qkv = h1.reshape(rows, width), d_qkv.reshape(rows, qkv_width)

    grad_gains = jnp.concatenate(
        [
            grad_gain_attn.reshape(owners, depth),
            grad_gain_moe.reshape(owners, depth),
            grad_gain_query.reshape(owners, eighth),
            grad_gain_key.reshape(owners, eighth),
        ],
        axis=1,
    ).astype(BF16)
    grad_gains = jnp.pad(
        grad_gains[:, None], ((0, 0), (0, 15), (0, shared.shape[2] - grad_gains.shape[1]))
    )
    index = lax.axis_index("experts")
    place = jnp.stack([index // SIDE, index % SIDE]).astype(jnp.int32)
    firsts, seconds = attend_grads_call(
        place, h1, d_qkv, grad_out, grad_gains, output, depth // 2 + 16
    )
    h1_pieces = add_placed_call(where, swap(theirs[0]), mine[0], firsts[1])
    d_h1 = exchange_sum(h1_pieces)
    x_f32 = x_own.astype(F32)
    input_grad = (d_x1 + norm_back(d_h1, x_f32, inverse_rms(x_f32), gain_attn))[:, None]
    grad_experts = after_call(grad_experts, h1_pieces)
    all_experts = lax.all_gather(grad_experts, GROUP, axis=0, tiled=False)
    firsts, seconds = plane_send(firsts, 1, 0), plane_send(seconds, 0, 1)
    firsts, seconds = half_sum_call(place, firsts, seconds, grad_out)
    result_gate, result_up, result_down = gate_up_down_call(all_experts, ff_part)
    grads = last_sum_call(plane_send(firsts, 0, 1), plane_send(seconds, 1, 0), d_h1)
    out_sum = jnp.concatenate(
        [grads[k * out_part : (k + 1) * out_part, qkv_width:] for k in range(depth // out_part)],
        axis=1,
    )
    result_q, result_k, result_v, gain_sum = columns_call(
        where, *gather_members(grads[:, :qkv_width]), depth, q_width, head
    )
    out_sum = after_call(lax.ppermute(out_sum, EVERY, back), input_grad, result_down)
    result_out = rows_call(where, *gather_members(out_sum, result_q))
    gain_sum = gain_sum[0]
    return (
        output,
        input_grad,
        result_q,
        result_k,
        result_v,
        result_out,
        gain_sum[:depth],
        gain_sum[depth : 2 * depth],
        gain_sum[2 * depth : 2 * depth + eighth],
        gain_sum[2 * depth + eighth : 2 * depth + 2 * eighth],
        result_gate[None],
        result_up[None],
        result_down[None],
    )


def solution(mesh):
    rows = P(None, ("experts", "dp"), "context", None)
    in_specs = (
        rows,
        P(None, ("experts", "dp")),
        rows,
        rows,
        rows,
        P("experts", None),
        P("experts", None),
        P("experts", None),
        P("experts", None),
        P("experts"),
        P("experts"),
        P("experts"),
        P("experts"),
        P("experts", None, None),
        P("experts", None, None),
        P("experts", None, None),
    )
    out_specs = (
        rows,
        rows,
        P("experts", None),
        P("experts", None),
        P("experts", None),
        P("experts", None),
        P("experts"),
        P("experts"),
        P("experts"),
        P("experts"),
        P("experts", None, None),
        P("experts", None, None),
        P("experts", None, None),
    )
    return jax.shard_map(local, mesh=mesh, in_specs=in_specs, out_specs=out_specs, check_vma=False)
```
